32 devices in a mesh: page: 16 (over z, x, core), seq: 2 (over y).
Axes of the slice: x: 2, y: 2, z: 4, core: 2. Of those that a mesh axis runs over, the one named last changes fastest.
Arguments:
- tokens: bfloat16 [16, 1024, 1024], P('page', 'seq'), may hold values from -6 to 6
- patches: bfloat16 [16, 1088, 1024], P('page', 'seq'), may hold values from -6 to 6
- lengths: int32 [16], P('page'), may hold values from 513 to 1024, as said below
- blank_mask: int32 [16, 1088], P('page'), may hold values from 0 to 1, as said below
- cotangent: bfloat16 [16, 1024, 1024], P('page', 'seq'), may hold values from -6 to 6
- first_gain: bfloat16 [1024], P('seq'), may hold values from 0.25 to 1.75
- first_shift: bfloat16 [1024], P('seq'), may hold values from -1.25 to 1.25
- self_query: bfloat16 [1024, 1024], P('seq'), may hold values from -0.1875 to 0.1875
- self_query_bias: bfloat16 [1024], P('seq'), may hold values from -1.25 to 1.25
- self_key: bfloat16 [1024, 1024], P('seq'), may hold values from -0.1875 to 0.1875
- self_value: bfloat16 [1024, 1024], P('seq'), may hold values from -0.1875 to 0.1875
- self_value_bias: bfloat16 [1024], P('seq'), may hold values from -1.25 to 1.25
- self_output: bfloat16 [1024, 1024], P('seq'), may hold values from -3 to 3
- self_output_bias: bfloat16 [1024], P('seq'), may hold values from -1.25 to 1.25
- second_gain: bfloat16 [1024], P('seq'), may hold values from 0.25 to 1.75
- second_shift: bfloat16 [1024], P('seq'), may hold values from -1.25 to 1.25
- cross_query: bfloat16 [1024, 1024], P('seq'), may hold values from -0.1875 to 0.1875
- cross_query_bias: bfloat16 [1024], P('seq'), may hold values from -1.25 to 1.25
- cross_key: bfloat16 [1024, 1024], P('seq'), may hold values from -0.1875 to 0.1875
- cross_value: bfloat16 [1024, 1024], P('seq'), may hold values from -0.1875 to 0.1875
- cross_value_bias: bfloat16 [1024], P('seq'), may hold values from -1.25 to 1.25
- cross_output: bfloat16 [1024, 1024], P('seq'), may hold values from -3.5 to 3.5
- cross_output_bias: bfloat16 [1024], P('seq'), may hold values from -1.25 to 1.25
- third_gain: bfloat16 [1024], P('seq'), may hold values from 0.25 to 1.75
- third_shift: bfloat16 [1024], P('seq'), may hold values from -1.25 to 1.25
- ffn_inner: bfloat16 [1024, 4096], P('seq'), may hold values from -0.1875 to 0.1875
- ffn_inner_bias: bfloat16 [4096], P('seq'), may hold values from -1.25 to 1.25
- ffn_outer: bfloat16 [4096, 1024], P('seq'), may hold values from -0.09375 to 0.09375
- ffn_outer_bias: bfloat16 [1024], P('seq'), may hold values from -1.25 to 1.25
Outputs:
- outputs: bfloat16 [16, 1024, 1024], P('page', 'seq')
- grad_tokens: float32 [16, 1024, 1024], P('page', 'seq')
- grad_patches: float32 [16, 1088, 1024], P('page', 'seq')
- grad_first_gain: float32 [1024], P('seq')
- grad_first_shift: float32 [1024], P('seq')
- grad_self_query: float32 [1024, 1024], P('seq')
- grad_self_query_bias: float32 [1024], P('seq')
- grad_self_key: float32 [1024, 1024], P('seq')
- grad_self_value: float32 [1024, 1024], P('seq')
- grad_self_value_bias: float32 [1024], P('seq')
- grad_self_output: float32 [1024, 1024], P('seq')
- grad_self_output_bias: float32 [1024], P('seq')
- grad_second_gain: float32 [1024], P('seq')
- grad_second_shift: float32 [1024], P('seq')
- grad_cross_query: float32 [1024, 1024], P('seq')
- grad_cross_query_bias: float32 [1024], P('seq')
- grad_cross_key: float32 [1024, 1024], P('seq')
- grad_cross_value: float32 [1024, 1024], P('seq')
- grad_cross_value_bias: float32 [1024], P('seq')
- grad_cross_output: float32 [1024, 1024], P('seq')
- grad_cross_output_bias: float32 [1024], P('seq')
- grad_third_gain: float32 [1024], P('seq')
- grad_third_shift: float32 [1024], P('seq')
- grad_ffn_inner: float32 [1024, 4096], P('seq')
- grad_ffn_inner_bias: float32 [4096], P('seq')
- grad_ffn_outer: float32 [4096, 1024], P('seq')
- grad_ffn_outer_bias: float32 [1024], P('seq')
The draws below stay inside these ranges and needn't reach their ends.
Inputs may be any that keep to these rules, and one draw needn't show every extreme that they name: `lengths`: in each group of 1 consecutive pages one page (which one is drawn) has more than 512 valid tokens. `blank_mask`: the first patch of every page is never blank.
All inputs are finite; a program needn't handle non-finite values.
Results may differ from the reference program's by a relative error of at most 0.024.
Values may be sent and summed in bfloat16 or wider, within the bound.
No kernel may reach another device: no remote copies, remote signals or barrier semaphores. Data moves between devices by JAX's collectives and lax.ppermute only.
A program may use at most 448 MiB of HBM per device.

```python
import math
import jax
import jax.numpy as jnp
from jax import lax

D = 1024
HEADS = 16
HEAD = 64
FF = 4096
PAGE_LEN = 1024
PATCH_LEN = 1088
PAGES_DEV = 1
TOK_DEV = 512
PAGES = 16


def draw_lengths(key, part):
    key = jax.random.fold_in(key, 7)
    split_keys = jax.random.split(key, 6)
    group_total = PAGES // PAGES_DEV
    page_ids = jnp.arange(PAGES, dtype=jnp.int32)
    group_ids = page_ids // PAGES_DEV
    slot_ids = page_ids % PAGES_DEV
    base_len = jax.random.randint(split_keys[0], (PAGES,), PAGE_LEN // 4, PAGE_LEN + 1)
    long_len = jax.random.randint(split_keys[1], (PAGES,), PAGE_LEN - TOK_DEV + 1, PAGE_LEN + 1)
    chosen = jax.random.randint(split_keys[2], (group_total,), 0, PAGES_DEV)[group_ids]
    other_slot = (chosen + 1 + jax.random.randint(split_keys[3], (group_total,), 0, max(PAGES_DEV - 1, 1))[group_ids]) % PAGES_DEV
    group_long = jax.random.randint(split_keys[4], (), 0, group_total)
    group_short = jax.random.randint(split_keys[5], (), 0, group_total)
    is_chosen = slot_ids == chosen
    result = jnp.where(is_chosen, long_len, base_len)
    result = jnp.where(is_chosen & (group_ids == group_long), PAGE_LEN, result)
    result = jnp.where((slot_ids == other_slot) & ~is_chosen & (group_ids == group_short), PAGE_LEN // 4, result)
    return result.astype(jnp.int32)


def draw_blank_mask(key, part):
    key = jax.random.fold_in(key, 13)
    rolled = jax.random.randint(key, (PAGES, PATCH_LEN), 0, 10)
    columns = jnp.arange(PATCH_LEN, dtype=jnp.int32)[None, :]
    return jnp.where((rolled < 3) & (columns > 0), 1, 0).astype(jnp.int32)


def block_scale(rng, shape, pieces, least, high):
    loudness = 1.0
    for dim, blocks in pieces:
        steps = jax.random.uniform(jax.random.fold_in(jax.random.fold_in(rng, 6), dim), (blocks,), jnp.float32, least / len(pieces), high / len(pieces))
        loudness = loudness * jnp.repeat(jnp.exp(steps), shape[dim] // blocks).reshape((-1,) + (1,) * (len(shape) - 1 - dim))
    return loudness


def noise(key, extent, width, limit, cuts=(), kind=jnp.bfloat16):
    drawn = width * jax.random.normal(key, extent, jnp.float32)
    if cuts:
        drawn = drawn * block_scale(key, extent, cuts, -0.22, 0.18)
    return jnp.clip(drawn, -limit, limit).astype(kind)


def setup_inputs(seed: int = 0) -> dict:
    key_list = jax.random.split(jax.random.key(seed), 30)
    return {
        "tokens": noise(key_list[0], (PAGES, PAGE_LEN, D), 1.0, 6.0, ((0, 16), (1, 2))),
        "patches": noise(key_list[1], (PAGES, PATCH_LEN, D), 1.0, 6.0, ((0, 16), (1, 2))),
        "lengths": draw_lengths(jax.random.fold_in(key_list[29], 71), 0),
        "blank_mask": draw_blank_mask(jax.random.fold_in(key_list[29], 71), 0),
        "cotangent": noise(key_list[4], (PAGES, PAGE_LEN, D), 1.0, 6.0, ((0, 16), (1, 2))),
        "first_gain": jnp.clip(1.0 + 0.15 * jax.random.normal(key_list[5], (D,), jnp.float32), 0.25, 1.75).astype(jnp.bfloat16),
        "first_shift": noise(key_list[6], (D,), 0.2, 1.25, ((0, 2),)),
        "self_query": noise(key_list[7], (D, D), D ** -0.5, 0.1875, ((0, 2),)),
        "self_query_bias": noise(key_list[8], (D,), 0.2, 1.25, ((0, 2),)),
        "self_key": noise(key_list[9], (D, D), D ** -0.5, 0.1875, ((0, 2),)),
        "self_value": noise(key_list[10], (D, D), D ** -0.5, 0.1875, ((0, 2),)),
        "self_value_bias": noise(key_list[11], (D,), 0.2, 1.25, ((0, 2),)),
        "self_output": noise(key_list[12], (D, D), (max(D * 4 // PAGE_LEN, 1)) ** -0.5, 3.0, ((0, 2),)),
        "self_output_bias": noise(key_list[13], (D,), 0.2, 1.25, ((0, 2),)),
        "second_gain": jnp.clip(1.0 + 0.15 * jax.random.normal(key_list[14], (D,), jnp.float32), 0.25, 1.75).astype(jnp.bfloat16),
        "second_shift": noise(key_list[15], (D,), 0.2, 1.25, ((0, 2),)),
        "cross_query": noise(key_list[16], (D, D), D ** -0.5, 0.1875, ((0, 2),)),
        "cross_query_bias": noise(key_list[17], (D,), 0.2, 1.25, ((0, 2),)),
        "cross_key": noise(key_list[18], (D, D), D ** -0.5, 0.1875, ((0, 2),)),
        "cross_value": noise(key_list[19], (D, D), D ** -0.5, 0.1875, ((0, 2),)),
        "cross_value_bias": noise(key_list[20], (D,), 0.2, 1.25, ((0, 2),)),
        "cross_output": noise(key_list[21], (D, D), (max(D * 4 // PATCH_LEN, 1)) ** -0.5, 3.5, ((0, 2),)),
        "cross_output_bias": noise(key_list[22], (D,), 0.2, 1.25, ((0, 2),)),
        "third_gain": jnp.clip(1.0 + 0.15 * jax.random.normal(key_list[23], (D,), jnp.float32), 0.25, 1.75).astype(jnp.bfloat16),
        "third_shift": noise(key_list[24], (D,), 0.2, 1.25, ((0, 2),)),
        "ffn_inner": noise(key_list[25], (D, FF), D ** -0.5, 0.1875, ((0, 2),)),
        "ffn_inner_bias": noise(key_list[26], (FF,), 0.2, 1.25, ((0, 2),)),
        "ffn_outer": noise(key_list[27], (FF, D), FF ** -0.5, 0.09375, ((0, 2),)),
        "ffn_outer_bias": noise(key_list[28], (D,), 0.2, 1.25, ((0, 2),)),
    }


@jax.custom_vjp
def low(v):
    return lax.optimization_barrier(v.astype(jnp.bfloat16)).astype(jnp.float32)

@jax.custom_vjp
def low_back(v):
    return v

def low_keep(v):
    return (low(v), None)

def low_pass(kept, grad):
    return (grad,)

def back_keep(v):
    return (v, None)

def back_low(kept, grad):
    return (low(grad),)
low.defvjp(low_keep, low_pass)
low_back.defvjp(back_keep, back_low)
norm_epsilon = 1e-05
masked_score = -1000000000.0
top_precision = lax.Precision.HIGHEST

def layer_norm(values, norm_gain, norm_shift):
    center = values - lax.optimization_barrier(jnp.mean(values, axis=-1, keepdims=True))
    spread = lax.optimization_barrier(jnp.mean(center * center, axis=-1, keepdims=True))
    return center * lax.rsqrt(spread + norm_epsilon) * norm_gain + norm_shift

def matmul(left_side, right_side):
    return jnp.dot(left_side, right_side, precision=top_precision)

def attention(queries, key_rows, value_rows, allowed, valid_rows):
    query_count = queries.shape[0]
    heads_query = queries.reshape(query_count, HEADS, HEAD)
    heads_key = key_rows.reshape(key_rows.shape[0], HEADS, HEAD)
    heads_value = value_rows.reshape(value_rows.shape[0], HEADS, HEAD)
    scores = jnp.einsum('qhd,khd->hqk', heads_query, heads_key, precision=top_precision)
    scores = low_back(jnp.where(allowed[None], scores, masked_score))
    row_peak = lax.optimization_barrier(jnp.max(scores, axis=-1, keepdims=True))
    weights = jnp.exp(scores - row_peak)
    shares = weights / lax.optimization_barrier(jnp.sum(weights, axis=-1, keepdims=True))
    blended = jnp.einsum('hqk,khd->qhd', low(shares), heads_value, precision=top_precision)
    blended = blended.reshape(query_count, D) * valid_rows[:, None]
    return low_back(low(blended))

def layer(params, page_tokens, page_patches, length, blank_row):
    first_gain, first_shift, self_query, self_query_bias, self_key, self_value, self_value_bias, self_output, self_output_bias, second_gain, second_shift, cross_query, cross_query_bias, cross_key, cross_value, cross_value_bias, cross_output, cross_output_bias, third_gain, third_shift, ffn_inner, ffn_inner_bias, ffn_outer, ffn_outer_bias = params
    query_scale = 1.0 / math.sqrt(HEAD)
    positions = jnp.arange(PAGE_LEN, dtype=jnp.int32)
    valid_rows = (positions < length).astype(page_tokens.dtype)
    self_allowed = (positions[None, :] <= positions[:, None]) & (positions[None, :] < length)
    cross_allowed = jnp.broadcast_to((blank_row == 0)[None, :], (PAGE_LEN, PATCH_LEN))
    normed = low(layer_norm(page_tokens, first_gain, first_shift))
    queries = low_back(low((matmul(normed, self_query) + self_query_bias) * query_scale))
    key_rows = low_back(low(matmul(normed, self_key)))
    value_rows = low_back(low(matmul(normed, self_value) + self_value_bias))
    blended = attention(queries, key_rows, value_rows, self_allowed, valid_rows)
    hidden = page_tokens + low_back(matmul(blended, self_output) + self_output_bias)
    normed = low(layer_norm(hidden, second_gain, second_shift))
    queries = low_back(low((matmul(normed, cross_query) + cross_query_bias) * query_scale))
    key_rows = low_back(low(matmul(page_patches, cross_key)))
    value_rows = low_back(low(matmul(page_patches, cross_value) + cross_value_bias))
    blended = attention(queries, key_rows, value_rows, cross_allowed, valid_rows)
    hidden = hidden + low_back(matmul(blended, cross_output) + cross_output_bias)
    normed = low(layer_norm(hidden, third_gain, third_shift))
    inner_sum = low_back(matmul(normed, ffn_inner) + ffn_inner_bias)
    active = low(jax.nn.gelu(inner_sum, approximate=False))
    return hidden + low_back(matmul(active, ffn_outer) + ffn_outer_bias)

def reference(tokens, patches, lengths, blank_mask, cotangent, first_gain, first_shift, self_query, self_query_bias, self_key, self_value, self_value_bias, self_output, self_output_bias, second_gain, second_shift, cross_query, cross_query_bias, cross_key, cross_value, cross_value_bias, cross_output, cross_output_bias, third_gain, third_shift, ffn_inner, ffn_inner_bias, ffn_outer, ffn_outer_bias):
    params = tuple((weight_arg.astype(jnp.float32) for weight_arg in (first_gain, first_shift, self_query, self_query_bias, self_key, self_value, self_value_bias, self_output, self_output_bias, second_gain, second_shift, cross_query, cross_query_bias, cross_key, cross_value, cross_value_bias, cross_output, cross_output_bias, third_gain, third_shift, ffn_inner, ffn_inner_bias, ffn_outer, ffn_outer_bias)))

    def page_step(totals, page_item):
        page_tokens, page_patches, length, blank_row, page_cot = page_item

        def forward(weight_set, token_rows, patch_rows):
            return layer(weight_set, token_rows, patch_rows, length, blank_row)
        result, pull_back = jax.vjp(forward, params, page_tokens.astype(jnp.float32), page_patches.astype(jnp.float32))
        grad_params, grad_page_tokens, grad_page_patches = pull_back(page_cot.astype(jnp.float32))
        totals = jax.tree.map(lambda left_side, right_side: left_side + right_side, totals, grad_params)
        return (totals, (result.astype(jnp.bfloat16), grad_page_tokens, grad_page_patches))
    zero_set = tuple((jnp.zeros_like(weight_arg) for weight_arg in params))
    totals, stacked = lax.scan(page_step, zero_set, (tokens, patches, lengths, blank_mask, cotangent))
    return (stacked[0], stacked[1], stacked[2], totals[0], totals[1], totals[2], totals[3], totals[4], totals[5], totals[6], totals[7], totals[8], totals[9], totals[10], totals[11], totals[12], totals[13], totals[14], totals[15], totals[16], totals[17], totals[18], totals[19], totals[20], totals[21], totals[22], totals[23])
```

```python
import functools
import math

import jax
import jax.numpy as jnp
from jax import lax
from jax.experimental import pallas as pl
from jax.experimental.pallas import tpu as pltpu
from jax.sharding import Mesh
from jax.sharding import PartitionSpec as P

HEADS = 16
HEAD = 64


norm_epsilon = 1e-05
masked_score = -1000000000.0


def layer_norm(values, norm_gain, norm_shift):
    center = values - jnp.mean(values, axis=-1, keepdims=True)
    spread = jnp.mean(center * center, axis=-1, keepdims=True)
    return center * lax.rsqrt(spread + norm_epsilon) * norm_gain + norm_shift


pair_width = 2 * HEAD
vmem_bytes = 48 * 1024 * 1024


def dot_nt(left_side, right_side):
    return lax.dot_general(
        left_side, right_side, (((1,), (1,)), ((), ())), preferred_element_type=jnp.float32
    )


def dot_nn(left_side, right_side):
    return jnp.dot(left_side, right_side, preferred_element_type=jnp.float32)


def dot_tn(left_side, right_side):
    return lax.dot_general(
        left_side, right_side, (((0,), (0,)), ((), ())), preferred_element_type=jnp.float32
    )


def one_head(values, head):
    lane = lax.broadcasted_iota(jnp.int32, values.shape, 1)
    return jnp.where((lane >= head * HEAD) & (lane < (head + 1) * HEAD), values, 0)


class Plan:
    def __init__(self, kinds, key_rows, query_rows, chunk, causal):
        self.kinds = kinds
        self.key_rows = key_rows
        self.all_rows = key_rows * len(kinds)
        self.query_rows = query_rows
        self.chunk = min(chunk, query_rows)
        self.causal = causal

    def blocks(self, start, segments):
        found = []
        for segment in segments:
            rows = self.key_rows
            if self.causal and self.kinds[segment] == "limit":
                rows = min(rows, start + self.chunk)
            found.append((self.kinds[segment], pl.ds(segment * self.key_rows, rows)))
        return found


def query_limit(info_ref, start, chunk):
    lane = lax.broadcasted_iota(jnp.int32, (1, chunk), 1) + start
    place = info_ref[0] + lane
    return jnp.minimum(place, info_ref[1] - 1) - info_ref[2]


def masked_block(kind, scores, limit, bias_ref):
    if kind == "limit":
        key = lax.broadcasted_iota(jnp.int32, scores.shape, 0)
        return jnp.where(key <= limit, scores, masked_score)
    if kind == "bias":
        return scores + bias_ref[...]
    return scores


def run_segments(plan, info_ref, body):
    every = list(range(len(plan.kinds)))
    needed = [segment for segment in every if plan.kinds[segment] != "earlier"]
    if len(needed) == len(every):
        body(every)
        return
    pl.when(info_ref[3] == 1)(lambda: body(every))
    pl.when(info_ref[3] != 1)(lambda: body(needed))


def attend_kernel(plan, info_ref, query_ref, key_ref, value_ref, bias_ref, mixed_ref, log_ref):
    def body(segments):
        for start in range(0, plan.query_rows, plan.chunk):
            limit = query_limit(info_ref, start, plan.chunk)
            lane = lax.broadcasted_iota(jnp.int32, (1, plan.chunk), 1) + start
            valid = (info_ref[0] + lane < info_ref[1]).astype(jnp.float32)
            query = query_ref[pl.ds(start, plan.chunk), :]
            parts = []
            for head in range(2):
                head_query = one_head(query, head)
                blocks = plan.blocks(start, segments)
                scores = [
                    masked_block(kind, dot_nt(key_ref[rows, :], head_query), limit, bias_ref)
                    for kind, rows in blocks
                ]
                peak = jnp.max(scores[0], axis=0, keepdims=True)
                for block in scores[1:]:
                    peak = jnp.maximum(peak, jnp.max(block, axis=0, keepdims=True))
                total = jnp.zeros_like(peak)
                mixed = jnp.zeros((pair_width, plan.chunk), jnp.float32)
                for (kind, rows), block in zip(blocks, scores):
                    weights = jnp.exp(block - peak)
                    total = total + jnp.sum(weights, axis=0, keepdims=True)
                    mixed = mixed + dot_tn(value_ref[rows, :], weights.astype(jnp.bfloat16))
                parts.append(mixed[head * HEAD : (head + 1) * HEAD] * (valid / total))
                log_ref[0, pl.ds(head, 1), pl.ds(start, plan.chunk)] = peak + jnp.log(total)
            joined = jnp.concatenate(parts, axis=0)
            mixed_ref[pl.ds(start, plan.chunk), :] = joined.T.astype(jnp.bfloat16)

    run_segments(plan, info_ref, body)


def attend_back_kernel(
    plan,
    info_ref,
    query_ref,
    mixed_ref,
    grad_ref,
    log_ref,
    key_ref,
    value_ref,
    bias_ref,
    grad_query_ref,
    grad_key_ref,
    grad_value_ref,
    key_sum,
    value_sum,
):
    def body(segments):
        key_sum[...] = jnp.zeros_like(key_sum)
        value_sum[...] = jnp.zeros_like(value_sum)
        for start in range(0, plan.query_rows, plan.chunk):
            limit = query_limit(info_ref, start, plan.chunk)
            rows_here = pl.ds(start, plan.chunk)
            row = lax.broadcasted_iota(jnp.int32, (plan.chunk, 1), 0) + start
            valid = info_ref[0] + row < info_ref[1]
            query = query_ref[rows_here, :]
            grad = jnp.where(valid, grad_ref[rows_here, :], 0).astype(jnp.bfloat16)
            product = grad.astype(jnp.float32) * mixed_ref[rows_here, :].astype(jnp.float32)
            product = product.T
            parts = []
            for head in range(2):
                own = slice(head * HEAD, (head + 1) * HEAD)
                head_query, head_grad = one_head(query, head), one_head(grad, head)
                weighted = jnp.sum(product[own], axis=0, keepdims=True)
                log_total = log_ref[0, pl.ds(head, 1), rows_here]
                grad_query = jnp.zeros((pair_width, plan.chunk), jnp.float32)
                for kind, rows in plan.blocks(start, segments):
                    keys = key_ref[rows, :]
                    scores = masked_block(kind, dot_nt(keys, head_query), limit, bias_ref)
                    shares = jnp.exp(scores - log_total)
                    grad_shares = dot_nt(value_ref[rows, :], head_grad)
                    grad_scores = (shares * (grad_shares - weighted)).astype(jnp.bfloat16)
                    value_sum[rows, :] += dot_nn(shares.astype(jnp.bfloat16), head_grad)
                    key_sum[rows, :] += dot_nn(grad_scores, head_query)
                    grad_query = grad_query + dot_tn(keys, grad_scores)
                parts.append(grad_query[own])
            joined = jnp.concatenate(parts, axis=0) * (1.0 / math.sqrt(HEAD))
            grad_query_ref[rows_here, :] = joined.T.astype(jnp.bfloat16)
        grad_key_ref[...] = key_sum[...].astype(jnp.bfloat16)
        grad_value_ref[...] = value_sum[...].astype(jnp.bfloat16)

    run_segments(plan, info_ref, body)


def column_block(rows, first):
    return pl.BlockSpec((rows, pair_width), lambda step, info: (0, first + step))


def log_block(rows, first):
    return pl.BlockSpec((1, 2, rows), lambda step, info: (first + step, 0, 0))


def key_specs(plan, first):
    return [
        column_block(plan.all_rows, first),
        column_block(plan.all_rows, HEADS // 2 + first),
        pl.BlockSpec((plan.all_rows, 1), lambda step, info: (0, 0)),
    ]


any_block = pl.BlockSpec(memory_space=pl.ANY)


def skip_refs(kernel, place, count):
    def run(*refs):
        kernel(*refs[:place], *refs[place + count :])

    return run


def attend(plan, info, queries, key_values, bias, part, parts, into=()):
    pairs = HEADS // 2
    count, first = pairs // parts, part * (pairs // parts)
    rows, keys = plan.query_rows, plan.all_rows
    return pl.pallas_call(
        skip_refs(functools.partial(attend_kernel, plan), 5, len(into)),
        grid_spec=pltpu.PrefetchScalarGridSpec(
            num_scalar_prefetch=1,
            grid=(count,),
            in_specs=[column_block(rows, first)] + key_specs(plan, first) + [any_block] * len(into),
            out_specs=[column_block(rows, first), log_block(rows, first)],
        ),
        out_shape=[
            jax.ShapeDtypeStruct((rows, HEADS * HEAD), jnp.bfloat16),
            jax.ShapeDtypeStruct((pairs, 2, rows), jnp.float32),
        ],
        input_output_aliases={5 + index: index for index in range(len(into))},
        compiler_params=pltpu.CompilerParams(vmem_limit_bytes=vmem_bytes),
        cost_estimate=pl.CostEstimate(
            flops=4 * 4 * rows * keys * HEADS * HEAD // parts,
            bytes_accessed=4 * (rows + keys) * HEADS * HEAD // parts,
            transcendentals=rows * keys * HEADS // parts,
        ),
    )(info, queries, key_values, key_values, bias, *into)


def attend_back(
    plan, info, queries, mixed, grad_mixed, log_total, key_values, bias, part, parts, into=()
):
    pairs = HEADS // 2
    count, first = pairs // parts, part * (pairs // parts)
    rows, keys = plan.query_rows, plan.all_rows
    return pl.pallas_call(
        skip_refs(functools.partial(attend_back_kernel, plan), 8, len(into)),
        grid_spec=pltpu.PrefetchScalarGridSpec(
            num_scalar_prefetch=1,
            grid=(count,),
            in_specs=[column_block(rows, first)] * 3
            + [log_block(rows, first)]
            + key_specs(plan, first)
            + [any_block] * len(into),
            out_specs=[
                column_block(rows, first),
                column_block(keys, first),
                column_block(keys, first),
            ],
            scratch_shapes=[pltpu.VMEM((keys, pair_width), jnp.float32)] * 2,
        ),
        out_shape=[
            jax.ShapeDtypeStruct((rows, HEADS * HEAD), jnp.bfloat16),
            jax.ShapeDtypeStruct((keys, HEADS * HEAD), jnp.bfloat16),
            jax.ShapeDtypeStruct((keys, HEADS * HEAD), jnp.bfloat16),
        ],
        input_output_aliases={8 + index: index for index in range(len(into))},
        compiler_params=pltpu.CompilerParams(vmem_limit_bytes=vmem_bytes),
        cost_estimate=pl.CostEstimate(
            flops=4 * 10 * rows * keys * HEADS * HEAD // parts,
            bytes_accessed=8 * (rows + keys) * HEADS * HEAD // parts,
            transcendentals=rows * keys * HEADS // parts,
        ),
    )(info, queries, mixed, grad_mixed, log_total, key_values, key_values, bias, *into)


def copy_all(copies):
    for copy in copies:
        copy.start()
    for copy in copies:
        copy.wait()


def merge_kernel(place_ref, own_ref, other_ref, out_ref, sems):
    rows = own_ref.shape[0]
    copies = []
    for which, source in enumerate((own_ref, other_ref)):
        first = pl.multiple_of(place_ref[which] * rows, rows)
        copies.append(
            pltpu.make_async_copy(source, out_ref.at[pl.ds(first, rows), :], sems.at[which])
        )
    copy_all(copies)


def merge(index, own, other):
    rows, width = own.shape
    return pl.pallas_call(
        merge_kernel,
        grid_spec=pltpu.PrefetchScalarGridSpec(
            num_scalar_prefetch=1,
            grid=(),
            in_specs=[any_block, any_block],
            out_specs=any_block,
            scratch_shapes=[pltpu.SemaphoreType.DMA((2,))],
        ),
        out_shape=jax.ShapeDtypeStruct((2 * rows, width), own.dtype),
        compiler_params=pltpu.CompilerParams(vmem_limit_bytes=4 * 1024 * 1024),
        cost_estimate=pl.CostEstimate(
            flops=0, bytes_accessed=8 * rows * width, transcendentals=0
        ),
    )(jnp.stack([index, 1 - index]).astype(jnp.int32), own, other)


def assemble_kernel(count, place_ref, *refs):
    shards, (four_ref, came_ref, out_ref, sems) = refs[:count], refs[count:]
    rows, part = shards[0].shape[0], four_ref.shape[0]
    seq, core = place_ref[0], place_ref[1]
    copies, left = [], 0
    for index, shard in enumerate(shards):
        own = out_ref.at[
            pl.ds(pl.multiple_of(seq * rows, rows), rows), pl.ds(left, shard.shape[1])
        ]
        copies.append(pltpu.make_async_copy(shard, own, sems.at[index]))
        left += shard.shape[1]
    for index, (source, half) in enumerate(((four_ref, core), (came_ref, 1 - core))):
        first = pl.multiple_of((1 - seq) * rows + half * part, part)
        copies.append(
            pltpu.make_async_copy(source, out_ref.at[pl.ds(first, part), :], sems.at[count + index])
        )
    copy_all(copies)


def assemble(seq, core, shards, four, came):
    count, width = len(shards), four.shape[1]
    rows = shards[0].shape[0]
    return pl.pallas_call(
        functools.partial(assemble_kernel, count),
        grid_spec=pltpu.PrefetchScalarGridSpec(
            num_scalar_prefetch=1,
            grid=(),
            in_specs=[any_block] * (count + 2),
            out_specs=any_block,
            scratch_shapes=[pltpu.SemaphoreType.DMA((count + 2,))],
        ),
        out_shape=jax.ShapeDtypeStruct((2 * rows, width), four.dtype),
        compiler_params=pltpu.CompilerParams(vmem_limit_bytes=4 * 1024 * 1024),
        cost_estimate=pl.CostEstimate(
            flops=0, bytes_accessed=8 * rows * width, transcendentals=0
        ),
    )(jnp.stack([seq, core]).astype(jnp.int32), *shards, four, came)


def ffn_kernel(half_steps, place_ref, *refs):
    normed, inner = refs[0:4], refs[4:8]
    outer_own, outer_other, bias_ref, bias_outer_ref, hidden_ref, cotangent_ref = refs[8:14]
    out_ref, grad_ref, column_ref, kept_outer, sent_outer, kept_inner, sent_inner = refs[14:21]
    total_ref, turned_ref = refs[21], refs[22]
    grad_sums = refs[23:27]
    step = pl.program_id(0)
    quarter = normed[0].shape[1]

    @pl.when(step == 0)
    def start():
        for index in range(4):
            turned_ref[index] = normed[index][...].T
            grad_sums[index][...] = jnp.zeros_like(grad_sums[index])
        total_ref[...] = hidden_ref[...] + bias_outer_ref[...]

    def run(outer_ref):
        inner_sum = bias_ref[...] + dot_nn(normed[0][...], inner[0][...])
        for index in range(1, 4):
            inner_sum = inner_sum + dot_nn(normed[index][...], inner[index][...])
        part = 0.5 + 0.5 * lax.erf(inner_sum * math.sqrt(0.5))
        active = (inner_sum * part).astype(jnp.bfloat16)
        slope = part + inner_sum * (
            jnp.exp(-0.5 * inner_sum * inner_sum) * (1.0 / math.sqrt(2.0 * math.pi))
        )
        cotangent = cotangent_ref[...]
        total_ref[...] += dot_nn(active, outer_ref[...])
        grad_inner = (dot_nt(cotangent, outer_ref[...]) * slope).astype(jnp.bfloat16)
        column_ref[...] = jnp.sum(grad_inner.astype(jnp.float32), axis=0, keepdims=True)
        for index in range(4):
            grad_sums[index][...] += dot_nt(grad_inner, inner[index][...])
        grad_outer = dot_tn(active, cotangent).astype(jnp.bfloat16)
        for which, out in ((0, kept_outer), (1, sent_outer)):

            def store(out=out):
                out[0] = grad_outer

            pl.when(step % 2 == which)(store)
        for index, (out, seq_at) in enumerate(
            ((kept_inner, 0), (sent_inner, 0), (kept_inner, 1), (sent_inner, 1))
        ):
            out[pl.ds(place_ref[seq_at], 1)] = dot_nn(turned_ref[index], grad_inner).astype(
                jnp.bfloat16
            )[None]

    pl.when(step < half_steps)(lambda: run(outer_own))
    pl.when(step >= half_steps)(lambda: run(outer_other))

    @pl.when(step == 2 * half_steps - 1)
    def finish():
        out_ref[...] = total_ref[...].astype(jnp.bfloat16)
        for index in range(4):
            first = pl.multiple_of(place_ref[4 + index] * quarter, quarter)
            grad_ref[:, pl.ds(first, quarter)] = grad_sums[index][...]


def ffn_both_ways(
    seq, core, normed, hidden, cotangent, inner_own, inner_other, outer_own, outer_other, bias, last
):
    rows, width = normed.shape
    units = inner_own.shape[1]
    chunk, quarter = 512, width // 4
    steps = units // chunk
    half_steps = steps // 2
    run = half_steps // 2
    order = []
    for step in range(steps):
        which, at = (seq, step) if step < half_steps else (1 - seq, step - half_steps)
        side = core if at % 2 == 0 else 1 - core
        order.append((which, side * run + at // 2))
    local = [at for _, at in order]
    whole = [which * half_steps + at for which, at in order]
    out_at = [which * run + step % half_steps // 2 for step, (which, _) in enumerate(order)]
    quarters = [seq * 2 + core, seq * 2 + 1 - core, (1 - seq) * 2 + core, (1 - seq) * 2 + 1 - core]
    place = jnp.stack(
        [seq, 1 - seq, core, 1 - core] + quarters + whole + local + out_at
    ).astype(jnp.int32)
    at_whole, at_local, at_out = 8, 8 + steps, 8 + 2 * steps
    fixed = lambda shape: pl.BlockSpec(shape, lambda step, place: (0,) * len(shape))
    normed_specs = [
        pl.BlockSpec((rows, quarter), lambda step, place, i=i: (0, place[4 + i])) for i in range(4)
    ]
    inner_specs = [
        pl.BlockSpec(
            (quarter, chunk), lambda step, place, i=i: (place[2 + i % 2], place[at_whole + step])
        )
        for i in range(4)
    ]
    own_at = lambda step, place: place[at_local + jnp.minimum(step, half_steps - 1)]
    other_at = lambda step, place: place[at_local + jnp.maximum(step, half_steps)]
    outer_shape = jax.ShapeDtypeStruct((2 * run, chunk, width), jnp.bfloat16)
    inner_shape = jax.ShapeDtypeStruct((2, quarter, units), jnp.bfloat16)
    outer_spec = pl.BlockSpec((1, chunk, width), lambda step, place: (place[at_out + step], 0, 0))
    inner_spec = pl.BlockSpec(
        (2, quarter, chunk), lambda step, place: (0, 0, place[at_whole + step])
    )
    row_spec = pl.BlockSpec((1, chunk), lambda step, place: (0, place[at_whole + step]))
    out, grad, column, kept_outer, sent_outer, kept_inner, sent_inner = pl.pallas_call(
        functools.partial(ffn_kernel, half_steps),
        grid_spec=pltpu.PrefetchScalarGridSpec(
            num_scalar_prefetch=1,
            grid=(steps,),
            in_specs=normed_specs
            + inner_specs
            + [
                pl.BlockSpec((chunk, width), lambda step, place: (own_at(step, place), 0)),
                pl.BlockSpec((chunk, width), lambda step, place: (other_at(step, place), 0)),
                row_spec,
                fixed((1, width)),
                fixed((rows, width)),
                fixed((rows, width)),
            ],
            out_specs=[
                fixed((rows, width)),
                fixed((rows, width)),
                row_spec,
                outer_spec,
                outer_spec,
                inner_spec,
                inner_spec,
            ],
            scratch_shapes=[
                pltpu.VMEM((rows, width), jnp.float32),
                pltpu.VMEM((4, quarter, rows), jnp.bfloat16),
            ]
            + [pltpu.VMEM((rows, quarter), jnp.float32)] * 4,
        ),
        out_shape=[
            jax.ShapeDtypeStruct((rows, width), jnp.bfloat16),
            jax.ShapeDtypeStruct((rows, width), jnp.float32),
            jax.ShapeDtypeStruct((1, units), jnp.float32),
            outer_shape,
            outer_shape,
            inner_shape,
            inner_shape,
        ],
        compiler_params=pltpu.CompilerParams(vmem_limit_bytes=56 * 1024 * 1024),
        cost_estimate=pl.CostEstimate(
            flops=12 * rows * width * units,
            bytes_accessed=4 * 2 * width * units + 12 * rows * width,
            transcendentals=2 * rows * units,
        ),
    )(
        place,
        *[normed] * 4,
        inner_own,
        inner_own,
        inner_other,
        inner_other,
        outer_own,
        outer_other,
        bias[None],
        last[None],
        hidden,
        cotangent,
    )
    split = lambda kept, sent: (kept.reshape(2, -1, kept.shape[2]), sent.reshape(2, -1, kept.shape[2]))
    return out, grad, column[0], split(kept_outer, sent_outer), (kept_inner, sent_inner)


def outer_group_kernel(count, place_ref, *refs):
    lefts, rights = refs[:count], refs[count : 2 * count]
    kept_ref, sent_ref = refs[2 * count :]
    part = kept_ref.shape[1]
    matrix, seq = pl.program_id(0), pl.program_id(1)

    def one(left_ref, right_ref):
        for which, out_ref in ((0, kept_ref), (1, sent_ref)):
            first = pl.multiple_of((seq * 2 + place_ref[which]) * part, part)
            left = left_ref[:, pl.ds(first, part)]
            out_ref[0] = dot_tn(left, right_ref[...]).astype(jnp.bfloat16)

    for index in range(count):
        pl.when(matrix == index)(functools.partial(one, lefts[index], rights[index]))


def outer_group(core, pairs):
    count, width = len(pairs), pairs[0][0].shape[1]
    part = width // 4
    place = jnp.stack([core, 1 - core]).astype(jnp.int32)
    whole = lambda values: pl.BlockSpec(values.shape, lambda matrix, seq, place: (0, 0))
    out_spec = pl.BlockSpec((1, part, width), lambda matrix, seq, place: (seq, 0, matrix))
    shape = jax.ShapeDtypeStruct((2, part, count * width), jnp.bfloat16)
    lefts, rights = [pair[0] for pair in pairs], [pair[1] for pair in pairs]
    tokens = sum(left.shape[0] for left in lefts)
    return pl.pallas_call(
        functools.partial(outer_group_kernel, count),
        grid_spec=pltpu.PrefetchScalarGridSpec(
            num_scalar_prefetch=1,
            grid=(count, 2),
            in_specs=[whole(values) for values in lefts + rights],
            out_specs=[out_spec, out_spec],
        ),
        out_shape=[shape, shape],
        compiler_params=pltpu.CompilerParams(vmem_limit_bytes=vmem_bytes),
        cost_estimate=pl.CostEstimate(
            flops=2 * tokens * width * width,
            bytes_accessed=2 * (2 * tokens * width + count * width * width),
            transcendentals=0,
        ),
    )(place, *lefts, *rights)


def halve_kernel(place_ref, kept_a, came_a, kept_b, came_b, kept_ref, sent_ref):
    kept_ref[0] = (kept_a[0].astype(jnp.float32) + came_a[0].astype(jnp.float32)).astype(
        jnp.bfloat16
    )
    sent_ref[0] = (kept_b[0].astype(jnp.float32) + came_b[0].astype(jnp.float32)).astype(
        jnp.bfloat16
    )


def halve(keep_at, send_at, kept, came):
    blocks, rows, width = kept.shape
    count = blocks // 2
    place = jnp.stack(list(keep_at) + list(send_at)).astype(jnp.int32)
    spec = lambda first: pl.BlockSpec(
        (1, rows, width), lambda j, place: (place[first + j], 0, 0)
    )
    out_spec = pl.BlockSpec((1, rows, width), lambda j, place: (j, 0, 0))
    shape = jax.ShapeDtypeStruct((count, rows, width), jnp.bfloat16)
    return pl.pallas_call(
        halve_kernel,
        grid_spec=pltpu.PrefetchScalarGridSpec(
            num_scalar_prefetch=1,
            grid=(count,),
            in_specs=[spec(0), spec(0), spec(count), spec(count)],
            out_specs=[out_spec, out_spec],
        ),
        out_shape=[shape, shape],
        compiler_params=pltpu.CompilerParams(vmem_limit_bytes=vmem_bytes),
        cost_estimate=pl.CostEstimate(
            flops=blocks * rows * width,
            bytes_accessed=6 * blocks * rows * width,
            transcendentals=0,
        ),
    )(place, kept, came, kept, came)


def layer_norm_back(values, norm_gain, grad):
    center = values - jnp.mean(values, axis=-1, keepdims=True)
    inverse = lax.rsqrt(jnp.mean(center * center, axis=-1, keepdims=True) + norm_epsilon)
    unit = center * inverse
    scaled = grad * norm_gain
    back = scaled - jnp.mean(scaled, axis=-1, keepdims=True)
    back = back - unit * jnp.mean(scaled * unit, axis=-1, keepdims=True)
    return back * inverse, jnp.sum(grad * unit, axis=0), jnp.sum(grad, axis=0)


def dot_back(gradient, weight):
    return dot_nt(gradient, weight)


def column_sum(values):
    return jnp.sum(values.astype(jnp.float32), axis=0)


def swap(values, axis_name):
    return lax.ppermute(values, axis_name, [(0, 1), (1, 0)])


flips = {"x": 4, "y": 1, "z": 8}
square = ("zlo", "x", "core", "seq")


def exchange(values, axes):
    flip = [flips[axis] for axis in axes]
    return lax.ppermute(values, square, [(i, i ^ flip[i // 2 % 2]) for i in range(16)])


def square_bits(turned):
    core, x, zlo = lax.axis_index("core"), lax.axis_index("x"), lax.axis_index("zlo")
    first = 1 - core if turned else core
    return core, jnp.where(first == 1, x, zlo), jnp.where(first == 1, zlo, x)


def after(values, *others):
    return lax.optimization_barrier((values,) + others)[0]


def first_piece(shards):
    piece_rows = shards[0].shape[0] // 8
    core, high, low = square_bits(False)
    place = (core * 2 + high) * 2 + low
    piece = [
        lax.dynamic_slice_in_dim(shard, place * piece_rows, piece_rows, axis=0) for shard in shards
    ]
    return swap(piece[0] if len(piece) == 1 else jnp.concatenate(piece, axis=1), "seq")


def second_piece(piece):
    return merge(square_bits(False)[2], piece, exchange(piece, "xz"))


def third_piece(two):
    return merge(square_bits(False)[1], two, exchange(two, "zx"))


class Total:
    def __init__(self, split, steps, turned):
        self.kept, sent = split
        self.core, self.first, self.second = square_bits(turned)
        self.seq, self.zhi = lax.axis_index("seq"), lax.axis_index("zhi")
        self.steps = steps
        self.along = ("x", "z") if turned else ("z", "x")
        on_seq = [axes == "y" for axes in steps[0]]
        self.starts = jnp.where(self.core == 0, on_seq[0], on_seq[1])
        self.came = swap(self.blocks(sent, 4), "core")
        self.kept = self.blocks(self.kept, 4)
        self.stage = 0

    def blocks(self, values, count):
        return values.reshape(count, -1, values.shape[-1])

    def step(self):
        if self.stage == 0:
            seq, first = self.seq, self.first
            keep = [jnp.where(self.starts, seq * 2 + j, j * 2 + first) for j in range(2)]
            send = [jnp.where(self.starts, (1 - seq) * 2 + j, j * 2 + 1 - first) for j in range(2)]
        else:
            bit = (jnp.where(self.starts, self.first, self.seq), self.second, self.zhi)
            bit = bit[self.stage - 1]
            keep, send = [bit], [1 - bit]
            self.kept, self.came = self.blocks(self.kept, 2), self.blocks(self.came, 2)
        self.kept, sent = halve(keep, send, self.kept, self.came)
        if self.stage < 3:
            self.came = exchange(sent, self.steps[self.stage])
        else:
            self.came = swap(sent, "zhi")
        self.stage += 1
        return sent

    def gather(self):
        if self.stage == 4:
            piece = self.kept[0].astype(jnp.float32) + self.came[0].astype(jnp.float32)
            self.part = piece.astype(jnp.bfloat16)
            self.came = swap(self.part, "zhi")
        elif self.stage == 5:
            self.part = merge(self.zhi, self.part, self.came)
            self.came = exchange(self.part, self.along[::-1])
        elif self.stage == 6:
            self.part = merge(self.second, self.part, self.came)
            self.came = exchange(self.part, self.along)
        else:
            self.part = merge(self.first, self.part, self.came)
            self.came = swap(self.part, "core")
        self.stage += 1
        return self.part

    def result(self):
        first = jnp.where(self.core == 0, self.part, self.came)
        second = jnp.where(self.core == 0, self.came, self.part)
        return jnp.concatenate([first, second]).astype(jnp.float32)


def sum_plain(terms):
    terms = lax.psum_scatter(terms.astype(jnp.bfloat16), "seq", scatter_dimension=0, tiled=True)
    return lax.psum(terms, page_axes)


page_axes = ("zhi", "zlo", "x", "core")


def sum_vectors(vectors):
    seq_count = lax.axis_size("seq")
    joined = jnp.concatenate([vector.reshape(seq_count, -1) for vector in vectors], axis=1)
    joined = joined.reshape(seq_count, -1, 128)
    seq = lax.axis_index("seq")
    if seq_count == 2:
        for axis in page_axes:
            if lax.axis_size(axis) == 2:
                joined = joined + swap(joined, axis)
            else:
                joined = lax.psum(joined, axis)
        own = lax.dynamic_index_in_dim(joined, seq, 0, keepdims=False)
        own = own + swap(lax.dynamic_index_in_dim(joined, 1 - seq, 0, keepdims=False), "seq")
    else:
        joined = lax.psum(joined, page_axes + ("seq",))
        own = lax.dynamic_index_in_dim(joined, seq, 0, keepdims=False)
    own = own.reshape(-1)
    out, start = [], 0
    for vector in vectors:
        size = vector.shape[0] // seq_count
        out.append(own[start : start + size])
        start += size
    return out


def on_device(
    tokens,
    patches,
    lengths,
    blank_mask,
    cotangent,
    first_gain,
    first_shift,
    self_query,
    self_query_bias,
    self_key,
    self_value,
    self_value_bias,
    self_output,
    self_output_bias,
    second_gain,
    second_shift,
    cross_query,
    cross_query_bias,
    cross_key,
    cross_value,
    cross_value_bias,
    cross_output,
    cross_output_bias,
    third_gain,
    third_shift,
    ffn_inner,
    ffn_inner_bias,
    ffn_outer,
    ffn_outer_bias,
):
    seq_count = lax.axis_size("seq")
    seq_index = lax.axis_index("seq")
    vectors = (
        first_gain,
        first_shift,
        self_query_bias,
        self_value_bias,
        self_output_bias,
        second_gain,
        second_shift,
        cross_query_bias,
        cross_value_bias,
        cross_output_bias,
        third_gain,
        third_shift,
        ffn_inner_bias,
        ffn_outer_bias,
    )
    two = seq_count == 2 and lax.axis_size("zhi") == 2
    joined = jnp.concatenate(vectors).reshape(-1, 128)
    if two:
        joined_other = swap(joined, "seq")
        gathered = jnp.where(
            seq_index == 0,
            jnp.stack([joined, joined_other]),
            jnp.stack([joined_other, joined]),
        )
    else:
        gathered = lax.all_gather(joined, "seq", axis=0, tiled=False)
    gathered = gathered.reshape(seq_count, -1)
    whole_vectors, start = [], 0
    for vector in vectors:
        part = gathered[:, start : start + vector.shape[0]].reshape(-1)
        whole_vectors.append(part.astype(jnp.float32))
        start += vector.shape[0]
    (
        gain_one,
        shift_one,
        bias_self_query,
        bias_self_value,
        bias_self_output,
        gain_two,
        shift_two,
        bias_cross_query,
        bias_cross_value,
        bias_cross_output,
        gain_three,
        shift_three,
        bias_inner,
        bias_outer,
    ) = whole_vectors
    tokens, patches, cotangent = tokens[0], patches[0], cotangent[0]
    tok_rows, width = tokens.shape
    patch_rows = patches.shape[0]
    query_scale = 1.0 / math.sqrt(HEAD)

    core = lax.axis_index("core")
    self_shards = [self_query, self_key, self_value, self_output]
    cross_shards = [cross_key, cross_value, cross_query, cross_output]
    if two:
        piece = first_piece(self_shards)
        tokens_other = lax.ppermute(after(tokens, piece), "seq", [(0, 1)])
        part = third_piece(second_piece(piece))
        cross_piece = first_piece([after(cross_key, part)] + cross_shards[1:])
        whole_self = assemble(seq_index, core, self_shards, part, swap(part, "core"))
        patches_other = swap(after(patches, whole_self), "seq")
        tokens_all = jnp.concatenate([tokens, after(tokens_other, whole_self)])
    else:
        gather = lambda shard: lax.all_gather(shard, "seq", axis=0, tiled=True)
        whole_self = gather(jnp.concatenate(self_shards, axis=1))
        whole_cross = gather(jnp.concatenate(cross_shards, axis=1))
        whole_ffn_inner, whole_ffn_outer = gather(ffn_inner), gather(ffn_outer)
        tokens_all, patches_all = gather(tokens), gather(patches)

    first_place = seq_index * tok_rows
    key_start = first_place if two else 0
    info = jnp.stack([first_place, lengths[0], key_start, seq_index]).astype(jnp.int32)
    self_plan = Plan(
        ("limit", "earlier") if two else ("limit",),
        tok_rows if two else tok_rows * seq_count,
        tok_rows,
        256,
        two,
    )
    cross_plan = Plan(("bias",), patch_rows * seq_count, tok_rows, 256, False)
    blank_bias = jnp.where(blank_mask[0] == 0, 0.0, masked_score).astype(jnp.float32)
    if two:
        halves = blank_bias.reshape(2, patch_rows)
        blank_bias = jnp.where(seq_index == 0, halves, halves[::-1]).reshape(-1)
    blank_bias = blank_bias[:, None]
    no_bias = jnp.zeros((self_plan.all_rows, 1), jnp.float32)

    zeros = jnp.zeros_like(bias_self_value)
    token_values = tokens.astype(jnp.float32)
    normed_all = layer_norm(tokens_all.astype(jnp.float32), gain_one, shift_one).astype(
        jnp.bfloat16
    )
    if two:
        normed_one = normed_all[:tok_rows]
    else:
        normed_one = layer_norm(token_values, gain_one, shift_one).astype(jnp.bfloat16)
    queries_self = (
        (dot_nn(normed_one, whole_self[:, :width]) + bias_self_query) * query_scale
    ).astype(jnp.bfloat16)
    self_bias = jnp.concatenate([zeros, bias_self_value])
    self_pairs = (dot_nn(normed_all, whole_self[:, width : 3 * width]) + self_bias).astype(
        jnp.bfloat16
    )
    attend_self = functools.partial(attend, self_plan, info)
    if two:
        first_half = attend_self(after(queries_self, cross_piece), self_pairs, no_bias, 0, 2)
        cross_part = second_piece(cross_piece)
        inner_piece = first_piece([after(ffn_inner, first_half[0])])
        mixed_self, log_self = attend_self(
            after(queries_self, cross_part), self_pairs, no_bias, 1, 2, first_half
        )
        cross_part = third_piece(cross_part)
    else:
        mixed_self, log_self = attend_self(queries_self, self_pairs, no_bias, 0, 1)
    hidden_one = token_values + dot_nn(mixed_self, whole_self[:, 3 * width :]) + bias_self_output
    normed_two = layer_norm(hidden_one, gain_two, shift_two).astype(jnp.bfloat16)
    if two:
        outer_piece = first_piece([after(ffn_outer, normed_two)])
        cross_came = swap(cross_part, "core")
        whole_cross = assemble(seq_index, core, cross_shards, cross_part, cross_came)
        patches_all = jnp.concatenate([patches, after(patches_other, whole_cross)])
    patch_bias = jnp.concatenate([zeros, bias_cross_value])
    patch_pairs = (dot_nn(patches_all, whole_cross[:, : 2 * width]) + patch_bias).astype(
        jnp.bfloat16
    )
    queries_cross = (
        (dot_nn(normed_two, whole_cross[:, 2 * width : 3 * width]) + bias_cross_query) * query_scale
    ).astype(jnp.bfloat16)
    attend_cross = functools.partial(attend, cross_plan, info)
    if two:
        first_half = attend_cross(after(queries_cross, inner_piece), patch_pairs, blank_bias, 0, 2)
        inner_part = second_piece(inner_piece)
        mixed_cross, log_cross = attend_cross(
            after(queries_cross, inner_part, outer_piece), patch_pairs, blank_bias, 1, 2, first_half
        )
        outer_part = second_piece(outer_piece)
        inner_part = third_piece(inner_part)
        inner_other = merge(core, inner_part, swap(inner_part, "core"))
        outer_part = third_piece(outer_part)
        outer_other = merge(core, outer_part, swap(outer_part, "core"))
    else:
        mixed_cross, log_cross = attend_cross(queries_cross, patch_pairs, blank_bias, 0, 1)
    hidden_two = hidden_one + dot_nn(mixed_cross, whole_cross[:, 3 * width :]) + bias_cross_output
    normed_three = layer_norm(hidden_two, gain_three, shift_three).astype(jnp.bfloat16)
    if two:
        outputs, grad_normed_three, column_inner, split_outer, split_inner = ffn_both_ways(
            seq_index,
            core,
            normed_three,
            hidden_two,
            cotangent,
            ffn_inner,
            inner_other,
            ffn_outer,
            outer_other,
            bias_inner,
            bias_outer,
        )
        total_outer = Total(split_outer, ("xy", "yz", "zx"), True)
        total_inner = Total(split_inner, ("zx", "yy", "xz"), False)
    else:
        inner_sum = dot_nn(normed_three, whole_ffn_inner) + bias_inner
        active = jax.nn.gelu(inner_sum, approximate=False).astype(jnp.bfloat16)
        outputs = (hidden_two + dot_nn(active, whole_ffn_outer) + bias_outer).astype(jnp.bfloat16)
        grad_active = dot_back(cotangent, whole_ffn_outer)
        gelu_pull = jax.vjp(lambda u: jax.nn.gelu(u, approximate=False), inner_sum)[1]
        grad_inner = gelu_pull(grad_active)[0].astype(jnp.bfloat16)
        column_inner = column_sum(grad_inner)
        grad_normed_three = dot_back(grad_inner, whole_ffn_inner)
    back_two, grad_gain_three, grad_shift_three = layer_norm_back(
        hidden_two, gain_three, grad_normed_three
    )
    grad_hidden_two = cotangent.astype(jnp.float32) + back_two
    branch_cross = grad_hidden_two.astype(jnp.bfloat16)
    grad_mixed_cross = dot_back(branch_cross, whole_cross[:, 3 * width :]).astype(jnp.bfloat16)
    back_cross = functools.partial(
        attend_back, cross_plan, info, queries_cross, mixed_cross
    )
    cross_rest = (log_cross, patch_pairs, blank_bias)
    if two:
        sent = (total_outer.step(), total_inner.step())
        cross_back = back_cross(after(grad_mixed_cross, *sent), *cross_rest, 0, 1)
    else:
        cross_back = back_cross(grad_mixed_cross, *cross_rest, 0, 1)
    scaled_cross, grad_patch_keys, grad_patch_values = cross_back
    back_one, grad_gain_two, grad_shift_two = layer_norm_back(
        hidden_one, gain_two, dot_back(scaled_cross, whole_cross[:, 2 * width : 3 * width])
    )
    grad_hidden_one = grad_hidden_two + back_one
    branch_self = grad_hidden_one.astype(jnp.bfloat16)
    grad_mixed_self = dot_back(branch_self, whole_self[:, 3 * width :]).astype(jnp.bfloat16)
    cross_products = [
        (normed_two, scaled_cross),
        (patches_all, grad_patch_keys),
        (patches_all, grad_patch_values),
        (mixed_cross, branch_cross),
    ]
    back_self = functools.partial(attend_back, self_plan, info, queries_self, mixed_self)
    self_rest = (log_self, self_pairs, no_bias)
    if two:
        total_cross = Total(outer_group(core, cross_products), ("xy", "yz", "zx"), True)
        sent = (total_outer.step(), total_inner.step(), total_cross.kept)
        first_half = back_self(after(grad_mixed_self, *sent), *self_rest, 0, 2)
        held = after(grad_mixed_self, first_half[0])
        total_outer.kept, total_inner.kept, total_cross.kept = (
            after(total.kept, first_half[0]) for total in (total_outer, total_inner, total_cross)
        )
        sent = (total_cross.step(), total_outer.step(), total_inner.step())
        self_back = back_self(after(held, *sent), *self_rest, 1, 2, first_half)
    else:
        self_back = back_self(grad_mixed_self, *self_rest, 0, 1)
    scaled_self, grad_keys, grad_values = self_back
    self_products = [
        (normed_one, scaled_self),
        (normed_all, grad_keys),
        (normed_all, grad_values),
        (mixed_self, branch_self),
    ]
    if two:
        total_self = Total(outer_group(core, self_products), ("xy", "yz", "zx"), True)
        scaled_late = after(scaled_self, total_self.kept)
    else:
        scaled_late = scaled_self
    normed_terms = dot_back(grad_keys, whole_self[:, width : 2 * width]) + dot_back(
        grad_values, whole_self[:, 2 * width : 3 * width]
    )
    patch_terms = dot_back(grad_patch_keys, whole_cross[:, :width]) + dot_back(
        grad_patch_values, whole_cross[:, width : 2 * width]
    )
    if two:
        normed_sent = normed_terms[tok_rows:].astype(jnp.bfloat16)
        normed_came = lax.ppermute(normed_sent, "seq", [(1, 0)])
        grad_normed = normed_terms[:tok_rows] + normed_came.astype(jnp.float32)
        patch_sent = patch_terms[patch_rows:].astype(jnp.bfloat16)
        grad_patches = patch_terms[:patch_rows] + swap(patch_sent, "seq").astype(jnp.float32)
    else:
        grad_patches, grad_normed = (
            lax.psum_scatter(
                terms.astype(jnp.bfloat16), "seq", scatter_dimension=0, tiled=True
            ).astype(jnp.float32)
            for terms in (patch_terms, normed_terms)
        )
    grad_normed = grad_normed + dot_back(scaled_late, whole_self[:, :width])
    back_zero, grad_gain_one, grad_shift_one = layer_norm_back(token_values, gain_one, grad_normed)
    grad_tokens = grad_hidden_one + back_zero
    small = sum_vectors(
        (
            grad_gain_one,
            grad_shift_one,
            column_sum(scaled_self),
            column_sum(grad_values),
            column_sum(branch_self),
            grad_gain_two,
            grad_shift_two,
            column_sum(scaled_cross),
            column_sum(grad_patch_values),
            column_sum(branch_cross),
            grad_gain_three,
            grad_shift_three,
            column_inner,
            column_sum(cotangent),
        )
    )
    if two:
        totals = (total_outer, total_inner, total_cross, total_self)
        for turn in range(9):
            for total in totals:
                if total.stage < 4:
                    total.step()
                elif total.stage < 8:
                    total.gather()
        grad_outer, grad_ffn_in, grad_cross, grad_self = (total.result() for total in totals)
        wide_cross, wide_self = jnp.split(grad_cross, 4, axis=1), jnp.split(grad_self, 4, axis=1)
    else:
        grad_outer = sum_plain(dot_tn(active, cotangent)).astype(jnp.float32)
        grad_ffn_in = sum_plain(dot_tn(normed_three, grad_inner)).astype(jnp.float32)
        wide_cross = [sum_plain(dot_tn(*product)).astype(jnp.float32) for product in cross_products]
        wide_self = [sum_plain(dot_tn(*product)).astype(jnp.float32) for product in self_products]
    totals = (
        small[0],
        small[1],
        wide_self[0],
        small[2],
        wide_self[1],
        wide_self[2],
        small[3],
        wide_self[3],
        small[4],
        small[5],
        small[6],
        wide_cross[0],
        small[7],
        wide_cross[1],
        wide_cross[2],
        small[8],
        wide_cross[3],
        small[9],
        small[10],
        small[11],
        grad_ffn_in,
        small[12],
        grad_outer,
        small[13],
    )
    return (outputs[None], grad_tokens[None], grad_patches[None]) + totals


def solution(mesh):
    page_count, seq_count = mesh.devices.shape
    mesh = Mesh(
        mesh.devices.reshape(page_count // 8, 2, 2, 2, seq_count),
        ("zhi", "zlo", "x", "core", "seq"),
    )
    page = ("zhi", "zlo", "x", "core")
    pages = P(page, "seq", None)
    rows, vector = P("seq", None), P("seq")
    layer = (
        (vector, vector)
        + (rows, vector, rows, rows, vector, rows, vector)
        + (vector, vector)
        + (rows, vector, rows, rows, vector, rows, vector)
        + (vector, vector)
        + (rows, vector, rows, vector)
    )
    return jax.shard_map(
        on_device,
        mesh=mesh,
        in_specs=(pages, pages, P(page), P(page, None), pages) + layer,
        out_specs=(pages, pages, pages) + layer,
        check_vma=False,
    )
```

```python
import functools
import math

import jax
import jax.numpy as jnp
from jax import lax
from jax.experimental import pallas as pl
from jax.experimental.pallas import tpu as pltpu
from jax.sharding import Mesh
from jax.sharding import PartitionSpec as P

HEADS = 16
HEAD = 64


norm_epsilon = 1e-05
masked_score = -1000000000.0


def layer_norm(values, norm_gain, norm_shift):
    center = values - jnp.mean(values, axis=-1, keepdims=True)
    spread = jnp.mean(center * center, axis=-1, keepdims=True)
    return center * lax.rsqrt(spread + norm_epsilon) * norm_gain + norm_shift


pair_width = 2 * HEAD
vmem_bytes = 60 * 1024 * 1024
light = pl.CostEstimate(flops=1, bytes_accessed=1, transcendentals=0)


def dot_nt(left_side, right_side):
    return lax.dot_general(
        left_side, right_side, (((1,), (1,)), ((), ())), preferred_element_type=jnp.float32
    )


def dot_nn(left_side, right_side):
    return jnp.dot(left_side, right_side, preferred_element_type=jnp.float32)


def dot_tn(left_side, right_side):
    return lax.dot_general(
        left_side, right_side, (((0,), (0,)), ((), ())), preferred_element_type=jnp.float32
    )


def one_head(values, head):
    lane = lax.broadcasted_iota(jnp.int32, values.shape, 1)
    return jnp.where((lane >= head * HEAD) & (lane < (head + 1) * HEAD), values, 0)


class Plan:
    def __init__(self, kinds, key_rows, query_rows, chunk, causal):
        self.kinds = kinds
        self.key_rows = key_rows
        self.all_rows = key_rows * len(kinds)
        self.query_rows = query_rows
        self.chunk = min(chunk, query_rows)
        self.causal = causal

    def blocks(self, start, segments):
        found = []
        for segment in segments:
            rows = self.key_rows
            if self.causal and self.kinds[segment] == "limit":
                rows = min(rows, start + self.chunk)
            found.append((self.kinds[segment], pl.ds(segment * self.key_rows, rows)))
        return found


def query_limit(info_ref, start, chunk):
    lane = lax.broadcasted_iota(jnp.int32, (1, chunk), 1) + start
    place = info_ref[0] + lane
    return jnp.minimum(place, info_ref[1] - 1) - info_ref[2]


def masked_block(kind, scores, limit, bias_ref):
    if kind == "limit":
        key = lax.broadcasted_iota(jnp.int32, scores.shape, 0)
        return jnp.where(key <= limit, scores, masked_score)
    if kind == "bias":
        return scores + bias_ref[...]
    return scores


def run_segments(plan, info_ref, body):
    every = list(range(len(plan.kinds)))
    needed = [segment for segment in every if plan.kinds[segment] != "earlier"]
    if len(needed) == len(every):
        body(every)
        return
    pl.when(info_ref[3] == 1)(lambda: body(every))
    pl.when(info_ref[3] != 1)(lambda: body(needed))


def attend_kernel(plan, info_ref, query_ref, key_ref, value_ref, bias_ref, mixed_ref, log_ref):
    def body(segments):
        for start in range(0, plan.query_rows, plan.chunk):
            limit = query_limit(info_ref, start, plan.chunk)
            lane = lax.broadcasted_iota(jnp.int32, (1, plan.chunk), 1) + start
            valid = (info_ref[0] + lane < info_ref[1]).astype(jnp.float32)
            query = query_ref[pl.ds(start, plan.chunk), :]
            parts = []
            for head in range(2):
                head_query = one_head(query, head)
                blocks = plan.blocks(start, segments)
                scores = [
                    masked_block(kind, dot_nt(key_ref[rows, :], head_query), limit, bias_ref)
                    for kind, rows in blocks
                ]
                peak = jnp.max(scores[0], axis=0, keepdims=True)
                for block in scores[1:]:
                    peak = jnp.maximum(peak, jnp.max(block, axis=0, keepdims=True))
                total = jnp.zeros_like(peak)
                mixed = jnp.zeros((pair_width, plan.chunk), jnp.float32)
                for (kind, rows), block in zip(blocks, scores):
                    weights = jnp.exp(block - peak)
                    total = total + jnp.sum(weights, axis=0, keepdims=True)
                    mixed = mixed + dot_tn(value_ref[rows, :], weights.astype(jnp.bfloat16))
                parts.append(mixed[head * HEAD : (head + 1) * HEAD] * (valid / total))
                log_ref[0, pl.ds(head, 1), pl.ds(start, plan.chunk)] = peak + jnp.log(total)
            joined = jnp.concatenate(parts, axis=0)
            mixed_ref[pl.ds(start, plan.chunk), :] = joined.T.astype(jnp.bfloat16)

    run_segments(plan, info_ref, body)


def attend_back_kernel(
    plan,
    info_ref,
    query_ref,
    mixed_ref,
    grad_ref,
    log_ref,
    key_ref,
    value_ref,
    bias_ref,
    grad_query_ref,
    grad_key_ref,
    grad_value_ref,
    key_sum,
    value_sum,
):
    def body(segments):
        key_sum[...] = jnp.zeros_like(key_sum)
        value_sum[...] = jnp.zeros_like(value_sum)
        for start in range(0, plan.query_rows, plan.chunk):
            limit = query_limit(info_ref, start, plan.chunk)
            rows_here = pl.ds(start, plan.chunk)
            row = lax.broadcasted_iota(jnp.int32, (plan.chunk, 1), 0) + start
            valid = info_ref[0] + row < info_ref[1]
            query = query_ref[rows_here, :]
            grad = jnp.where(valid, grad_ref[rows_here, :], 0).astype(jnp.bfloat16)
            product = grad.astype(jnp.float32) * mixed_ref[rows_here, :].astype(jnp.float32)
            product = product.T
            parts = []
            for head in range(2):
                own = slice(head * HEAD, (head + 1) * HEAD)
                head_query, head_grad = one_head(query, head), one_head(grad, head)
                weighted = jnp.sum(product[own], axis=0, keepdims=True)
                log_total = log_ref[0, pl.ds(head, 1), rows_here]
                grad_query = jnp.zeros((pair_width, plan.chunk), jnp.float32)
                for kind, rows in plan.blocks(start, segments):
                    keys = key_ref[rows, :]
                    scores = masked_block(kind, dot_nt(keys, head_query), limit, bias_ref)
                    shares = jnp.exp(scores - log_total)
                    grad_shares = dot_nt(value_ref[rows, :], head_grad)
                    grad_scores = (shares * (grad_shares - weighted)).astype(jnp.bfloat16)
                    value_sum[rows, :] += dot_nn(shares.astype(jnp.bfloat16), head_grad)
                    key_sum[rows, :] += dot_nn(grad_scores, head_query)
                    grad_query = grad_query + dot_tn(keys, grad_scores)
                parts.append(grad_query[own])
            joined = jnp.concatenate(parts, axis=0) * (1.0 / math.sqrt(HEAD))
            grad_query_ref[rows_here, :] = joined.T.astype(jnp.bfloat16)
        grad_key_ref[...] = key_sum[...].astype(jnp.bfloat16)
        grad_value_ref[...] = value_sum[...].astype(jnp.bfloat16)

    run_segments(plan, info_ref, body)


def column_block(rows, first):
    return pl.BlockSpec((rows, pair_width), lambda step, info: (0, first + step))


def log_block(rows, first):
    return pl.BlockSpec((1, 2, rows), lambda step, info: (first + step, 0, 0))


def key_specs(plan, first):
    return [
        column_block(plan.all_rows, first),
        column_block(plan.all_rows, HEADS // 2 + first),
        pl.BlockSpec((plan.all_rows, 1), lambda step, info: (0, 0)),
    ]


any_block = pl.BlockSpec(memory_space=pl.ANY)


def skip_refs(kernel, place, count):
    def run(*refs):
        kernel(*refs[:place], *refs[place + count :])

    return run


def attend(plan, info, queries, key_values, bias, part, parts, into=()):
    pairs = HEADS // 2
    count, first = pairs // parts, part * (pairs // parts)
    rows, keys = plan.query_rows, plan.all_rows
    return pl.pallas_call(
        skip_refs(functools.partial(attend_kernel, plan), 5, len(into)),
        grid_spec=pltpu.PrefetchScalarGridSpec(
            num_scalar_prefetch=1,
            grid=(count,),
            in_specs=[column_block(rows, first)] + key_specs(plan, first) + [any_block] * len(into),
            out_specs=[column_block(rows, first), log_block(rows, first)],
        ),
        out_shape=[
            jax.ShapeDtypeStruct((rows, HEADS * HEAD), jnp.bfloat16),
            jax.ShapeDtypeStruct((pairs, 2, rows), jnp.float32),
        ],
        input_output_aliases={5 + index: index for index in range(len(into))},
        compiler_params=pltpu.CompilerParams(vmem_limit_bytes=vmem_bytes),
        cost_estimate=light,
    )(info, queries, key_values, key_values, bias, *into)


def attend_back(
    plan, info, queries, mixed, grad_mixed, log_total, key_values, bias, part, parts, into=()
):
    pairs = HEADS // 2
    count, first = pairs // parts, part * (pairs // parts)
    rows, keys = plan.query_rows, plan.all_rows
    return pl.pallas_call(
        skip_refs(functools.partial(attend_back_kernel, plan), 8, len(into)),
        grid_spec=pltpu.PrefetchScalarGridSpec(
            num_scalar_prefetch=1,
            grid=(count,),
            in_specs=[column_block(rows, first)] * 3
            + [log_block(rows, first)]
            + key_specs(plan, first)
            + [any_block] * len(into),
            out_specs=[
                column_block(rows, first),
                column_block(keys, first),
                column_block(keys, first),
            ],
            scratch_shapes=[pltpu.VMEM((keys, pair_width), jnp.float32)] * 2,
        ),
        out_shape=[
            jax.ShapeDtypeStruct((rows, HEADS * HEAD), jnp.bfloat16),
            jax.ShapeDtypeStruct((keys, HEADS * HEAD), jnp.bfloat16),
            jax.ShapeDtypeStruct((keys, HEADS * HEAD), jnp.bfloat16),
        ],
        input_output_aliases={8 + index: index for index in range(len(into))},
        compiler_params=pltpu.CompilerParams(vmem_limit_bytes=vmem_bytes),
        cost_estimate=light,
    )(info, queries, mixed, grad_mixed, log_total, key_values, key_values, bias, *into)


def join_kernel(count, place_ref, *refs):
    out_ref = refs[count]
    for index, source in enumerate(refs[:count]):
        rows = source.shape[0]
        first = pl.multiple_of(place_ref[index] * rows, rows)
        out_ref[pl.ds(first, rows), :] = source[...]


def join(places, parts):
    count, (rows, width) = len(parts), parts[0].shape
    steps = 1 if count * rows * width <= 1024 * 1024 else 4
    wide = width // steps
    return pl.pallas_call(
        functools.partial(join_kernel, count),
        grid_spec=pltpu.PrefetchScalarGridSpec(
            num_scalar_prefetch=1,
            grid=(steps,),
            in_specs=[pl.BlockSpec((rows, wide), lambda i, place: (0, i))] * count,
            out_specs=pl.BlockSpec((count * rows, wide), lambda i, place: (0, i)),
        ),
        out_shape=jax.ShapeDtypeStruct((count * rows, width), parts[0].dtype),
        compiler_params=pltpu.CompilerParams(vmem_limit_bytes=vmem_bytes),
        cost_estimate=light,
    )(jnp.stack(places).astype(jnp.int32), *parts)


def merge(index, own, other):
    return join([index, 1 - index], [own, other])


def assemble_kernel(count, place_ref, *refs):
    shards, parts, out_ref = refs[:count], refs[count:-1], refs[-1]
    for index, part in enumerate(parts):
        rows = part.shape[0]
        first = pl.multiple_of(place_ref[1 + index] * rows, rows)
        out_ref[pl.ds(first, rows), :] = part[...]
    for index, shard in enumerate(shards):

        def store(shard=shard):
            rows = shard.shape[0]
            first = pl.multiple_of(place_ref[0] * rows, rows)
            out_ref[pl.ds(first, rows), :] = shard[...]

        pl.when(pl.program_id(0) == index)(store)


def assemble(seq, places, shards, parts):
    count, (rows, wide) = len(shards), shards[0].shape
    part_rows = parts[0].shape[0]
    places = [seq] + [(1 - seq) * len(parts) + place for place in places]
    return pl.pallas_call(
        functools.partial(assemble_kernel, count),
        grid_spec=pltpu.PrefetchScalarGridSpec(
            num_scalar_prefetch=1,
            grid=(count,),
            in_specs=[pl.BlockSpec((rows, wide), lambda i, place: (0, 0))] * count
            + [pl.BlockSpec((part_rows, wide), lambda i, place: (0, i))] * len(parts),
            out_specs=pl.BlockSpec((2 * rows, wide), lambda i, place: (0, i)),
        ),
        out_shape=jax.ShapeDtypeStruct((2 * rows, count * wide), shards[0].dtype),
        compiler_params=pltpu.CompilerParams(vmem_limit_bytes=vmem_bytes),
        cost_estimate=light,
    )(jnp.stack(places).astype(jnp.int32), *shards, *parts)


def row_sums_kernel(norms, plain, *refs):
    steps = refs[: 2 * norms + plain]
    out_ref = refs[-1]

    @pl.when(pl.program_id(0) == 0)
    def start():
        out_ref[...] = jnp.zeros_like(out_ref)

    for index in range(norms):
        values, grad = steps[2 * index][...].astype(jnp.float32), steps[2 * index + 1][...]
        center = values - jnp.mean(values, axis=-1, keepdims=True)
        spread = jnp.mean(center * center, axis=-1, keepdims=True)
        unit = center * lax.rsqrt(spread + norm_epsilon)
        out_ref[pl.ds(2 * index, 1), :] += jnp.sum(grad * unit, axis=0, keepdims=True)
        out_ref[pl.ds(2 * index + 1, 1), :] += jnp.sum(grad, axis=0, keepdims=True)
    for index in range(plain):
        values = steps[2 * norms + index][...].astype(jnp.float32)
        at = pl.ds(2 * norms + index, 1)
        out_ref[at, :] += jnp.sum(values, axis=0, keepdims=True)


def row_sums(norm_pairs, plain):
    arrays = [values for pair in norm_pairs for values in pair] + list(plain)
    width = arrays[0].shape[1]
    rows = -(-(2 * len(norm_pairs) + len(plain)) // 8) * 8
    return pl.pallas_call(
        functools.partial(row_sums_kernel, len(norm_pairs), len(plain)),
        grid=(4,),
        in_specs=[
            pl.BlockSpec((values.shape[0] // 4, width), lambda step: (step, 0)) for values in arrays
        ],
        out_specs=pl.BlockSpec((rows, width), lambda step: (0, 0)),
        out_shape=jax.ShapeDtypeStruct((rows, width), jnp.float32),
        compiler_params=pltpu.CompilerParams(vmem_limit_bytes=vmem_bytes),
        cost_estimate=light,
    )(*arrays)


def ffn_kernel(half_steps, place_ref, *refs):
    normed, inner = refs[0:4], refs[4:8]
    outer_own, outer_other, bias_ref, bias_outer_ref, hidden_ref, cotangent_ref = refs[8:14]
    out_ref, grad_ref, column_ref, kept_outer, sent_outer, kept_inner, sent_inner = refs[14:21]
    total_ref, turned_ref = refs[21], refs[22]
    grad_sums = refs[23:27]
    step = pl.program_id(0)
    quarter = normed[0].shape[1]

    @pl.when(step == 0)
    def start():
        for index in range(4):
            turned_ref[index] = normed[index][...].T
            grad_sums[index][...] = jnp.zeros_like(grad_sums[index])
        total_ref[...] = hidden_ref[...] + bias_outer_ref[...]

    def run(outer_ref):
        inner_sum = bias_ref[...] + dot_nn(normed[0][...], inner[0][...])
        for index in range(1, 4):
            inner_sum = inner_sum + dot_nn(normed[index][...], inner[index][...])
        part = 0.5 + 0.5 * lax.erf(inner_sum * math.sqrt(0.5))
        active = (inner_sum * part).astype(jnp.bfloat16)
        slope = part + inner_sum * (
            jnp.exp(-0.5 * inner_sum * inner_sum) * (1.0 / math.sqrt(2.0 * math.pi))
        )
        cotangent = cotangent_ref[...]
        total_ref[...] += dot_nn(active, outer_ref[...])
        grad_inner = (dot_nt(cotangent, outer_ref[...]) * slope).astype(jnp.bfloat16)
        column_ref[...] = jnp.sum(grad_inner.astype(jnp.float32), axis=0, keepdims=True)
        for index in range(4):
            grad_sums[index][...] += dot_nt(grad_inner, inner[index][...])
        grad_outer = dot_tn(active, cotangent).astype(jnp.bfloat16)
        for which, out in ((0, kept_outer), (1, sent_outer)):

            def store(out=out):
                out[0] = grad_outer

            pl.when(step % 2 == which)(store)
        for index, (out, seq_at) in enumerate(
            ((kept_inner, 0), (sent_inner, 0), (kept_inner, 1), (sent_inner, 1))
        ):
            out[pl.ds(place_ref[seq_at], 1)] = dot_nn(turned_ref[index], grad_inner).astype(
                jnp.bfloat16
            )[None]

    pl.when(step < half_steps)(lambda: run(outer_own))
    pl.when(step >= half_steps)(lambda: run(outer_other))

    @pl.when(step == 2 * half_steps - 1)
    def finish():
        out_ref[...] = total_ref[...].astype(jnp.bfloat16)
        for index in range(4):
            first = pl.multiple_of(place_ref[4 + index] * quarter, quarter)
            grad_ref[:, pl.ds(first, quarter)] = grad_sums[index][...]


def ffn_both_ways(
    seq, core, normed, hidden, cotangent, inner_own, inner_other, outer_own, outer_other, bias, last
):
    rows, width = normed.shape
    units = inner_own.shape[1]
    chunk, quarter = 512, width // 4
    steps = units // chunk
    half_steps = steps // 2
    run = half_steps // 2
    order = []
    for step in range(steps):
        which, at = (seq, step) if step < half_steps else (1 - seq, step - half_steps)
        side = core if at % 2 == 0 else 1 - core
        order.append((which, side * run + at // 2))
    local = [at for _, at in order]
    whole = [which * half_steps + at for which, at in order]
    out_at = [which * run + step % half_steps // 2 for step, (which, _) in enumerate(order)]
    quarters = [seq * 2 + core, seq * 2 + 1 - core, (1 - seq) * 2 + core, (1 - seq) * 2 + 1 - core]
    place = jnp.stack(
        [seq, 1 - seq, core, 1 - core] + quarters + whole + local + out_at
    ).astype(jnp.int32)
    at_whole, at_local, at_out = 8, 8 + steps, 8 + 2 * steps
    fixed = lambda shape: pl.BlockSpec(shape, lambda step, place: (0,) * len(shape))
    normed_specs = [
        pl.BlockSpec((rows, quarter), lambda step, place, i=i: (0, place[4 + i])) for i in range(4)
    ]
    inner_specs = [
        pl.BlockSpec(
            (quarter, chunk), lambda step, place, i=i: (place[2 + i % 2], place[at_whole + step])
        )
        for i in range(4)
    ]
    own_at = lambda step, place: place[at_local + jnp.minimum(step, half_steps - 1)]
    other_at = lambda step, place: place[at_local + jnp.maximum(step, half_steps)]
    outer_shape = jax.ShapeDtypeStruct((2 * run, chunk, width), jnp.bfloat16)
    inner_shape = jax.ShapeDtypeStruct((2, quarter, units), jnp.bfloat16)
    outer_spec = pl.BlockSpec((1, chunk, width), lambda step, place: (place[at_out + step], 0, 0))
    inner_spec = pl.BlockSpec(
        (2, quarter, chunk), lambda step, place: (0, 0, place[at_whole + step])
    )
    row_spec = pl.BlockSpec((1, chunk), lambda step, place: (0, place[at_whole + step]))
    out, grad, column, kept_outer, sent_outer, kept_inner, sent_inner = pl.pallas_call(
        functools.partial(ffn_kernel, half_steps),
        grid_spec=pltpu.PrefetchScalarGridSpec(
            num_scalar_prefetch=1,
            grid=(steps,),
            in_specs=normed_specs
            + inner_specs
            + [
                pl.BlockSpec((chunk, width), lambda step, place: (own_at(step, place), 0)),
                pl.BlockSpec((chunk, width), lambda step, place: (other_at(step, place), 0)),
                row_spec,
                fixed((1, width)),
                fixed((rows, width)),
                fixed((rows, width)),
            ],
            out_specs=[
                fixed((rows, width)),
                fixed((rows, width)),
                row_spec,
                outer_spec,
                outer_spec,
                inner_spec,
                inner_spec,
            ],
            scratch_shapes=[
                pltpu.VMEM((rows, width), jnp.float32),
                pltpu.VMEM((4, quarter, rows), jnp.bfloat16),
            ]
            + [pltpu.VMEM((rows, quarter), jnp.float32)] * 4,
        ),
        out_shape=[
            jax.ShapeDtypeStruct((rows, width), jnp.bfloat16),
            jax.ShapeDtypeStruct((rows, width), jnp.float32),
            jax.ShapeDtypeStruct((1, units), jnp.float32),
            outer_shape,
            outer_shape,
            inner_shape,
            inner_shape,
        ],
        compiler_params=pltpu.CompilerParams(vmem_limit_bytes=vmem_bytes),
        cost_estimate=light,
    )(
        place,
        *[normed] * 4,
        inner_own,
        inner_own,
        inner_other,
        inner_other,
        outer_own,
        outer_other,
        bias[None],
        last[None],
        hidden,
        cotangent,
    )
    split = lambda kept, sent: (kept.reshape(2, -1, kept.shape[2]), sent.reshape(2, -1, kept.shape[2]))
    return out, grad, column[0], split(kept_outer, sent_outer), (kept_inner, sent_inner)


def outer_group_kernel(products, count, place_ref, *refs):
    lefts, rights = refs[:count], refs[count : count + len(products)]
    kept_ref, sent_ref, turned_ref = refs[count + len(products) :]
    part = kept_ref.shape[1]
    step = pl.program_id(0)
    sides = [side for side, _ in products]
    start = 0
    for index, (side, blocks) in enumerate(products):
        left, right = lefts[side], rights[index]
        tokens = pl.ds(0, left.shape[0])
        if sides.index(side) == index:

            def turn(left=left, tokens=tokens):
                turned_ref[:, tokens] = left[...].T

            pl.when(step == start)(turn)

        def run(right=right, tokens=tokens):
            for seq in range(2):
                for which, out_ref in ((0, kept_ref), (1, sent_ref)):
                    first = pl.multiple_of((seq * 2 + place_ref[which]) * part, part)
                    rows = turned_ref[pl.ds(first, part), tokens]
                    out_ref[seq] = dot_nn(rows, right[...]).astype(jnp.bfloat16)

        pl.when((step >= start) & (step < start + blocks))(run)
        start += blocks


def outer_group(core, lefts, products):
    chunk = 512
    width = lefts[0].shape[1]
    part = width // 4
    tokens = max(left.shape[0] for left in lefts)
    specs, start = [], 0
    for _, right in products:
        blocks = right.shape[1] // chunk
        specs.append(
            pl.BlockSpec(
                (right.shape[0], chunk),
                lambda step, place, start=start, blocks=blocks: (
                    0,
                    jnp.clip(step - start, 0, blocks - 1),
                ),
            )
        )
        start += blocks
    out_spec = pl.BlockSpec((2, part, chunk), lambda step, place: (0, 0, step))
    shape = jax.ShapeDtypeStruct((2, part, start * chunk), jnp.bfloat16)
    kinds = [(side, right.shape[1] // chunk) for side, right in products]
    return pl.pallas_call(
        functools.partial(outer_group_kernel, kinds, len(lefts)),
        grid_spec=pltpu.PrefetchScalarGridSpec(
            num_scalar_prefetch=1,
            grid=(start,),
            in_specs=[pl.BlockSpec(left.shape, lambda step, place: (0, 0)) for left in lefts]
            + specs,
            out_specs=[out_spec, out_spec],
            scratch_shapes=[pltpu.VMEM((width, tokens), jnp.bfloat16)],
        ),
        out_shape=[shape, shape],
        compiler_params=pltpu.CompilerParams(vmem_limit_bytes=vmem_bytes),
        cost_estimate=light,
    )(
        jnp.stack([core, 1 - core]).astype(jnp.int32),
        *lefts,
        *[right for _, right in products],
    )


def halve_kernel(split, place_ref, kept_a, came_a, kept_b, came_b, kept_ref, *sent_refs):
    add = lambda kept, came: (kept[0].astype(jnp.float32) + came[0].astype(jnp.float32)).astype(
        jnp.bfloat16
    )
    kept_ref[0] = add(kept_a, came_a)
    if not split:
        sent_refs[0][0] = add(kept_b, came_b)
        return

    for index, sent_ref in enumerate(sent_refs):

        def store(sent_ref=sent_ref):
            sent_ref[0] = add(kept_b, came_b)

        pl.when(pl.program_id(0) == index)(store)


def halve(keep_at, send_at, kept, came, split=False):
    blocks, rows, width = kept.shape
    count = len(keep_at)
    place = jnp.stack(list(keep_at) + list(send_at)).astype(jnp.int32)
    tiles = 2 if rows * width >= 256 * 1024 else 1
    wide = width // tiles
    spec = lambda first: pl.BlockSpec(
        (1, rows, wide), lambda j, i, place: (place[first + j], 0, i)
    )
    out_spec = pl.BlockSpec((1, rows, wide), lambda j, i, place: (j, 0, i))
    one_spec = lambda at: pl.BlockSpec(
        (1, rows, wide),
        lambda j, i, place: (0, 0, jnp.where(j == at, i, jnp.where(j > at, tiles - 1, 0))),
    )
    shape = jax.ShapeDtypeStruct((count, rows, width), jnp.bfloat16)
    one = jax.ShapeDtypeStruct((1, rows, width), jnp.bfloat16)
    out = pl.pallas_call(
        functools.partial(halve_kernel, split),
        grid_spec=pltpu.PrefetchScalarGridSpec(
            num_scalar_prefetch=1,
            grid=(count, tiles),
            in_specs=[spec(0), spec(0), spec(count), spec(count)],
            out_specs=[out_spec]
            + ([one_spec(at) for at in range(count)] if split else [out_spec]),
        ),
        out_shape=[shape] + ([one] * count if split else [shape]),
        compiler_params=pltpu.CompilerParams(vmem_limit_bytes=vmem_bytes),
        cost_estimate=light,
    )(place, kept, came, kept, came)
    return out[0], out[1:]


def halve_late_kernel(place_ref, *refs):
    step = pl.program_id(0)
    for which in range(2):
        own_ref, early_ref, late_ref = refs[3 * which : 3 * which + 3]
        out_ref = refs[6 + which]
        for block, came_ref in enumerate((early_ref, late_ref)):

            def store(out_ref=out_ref, own_ref=own_ref, came_ref=came_ref):
                total = own_ref[0].astype(jnp.float32) + came_ref[0].astype(jnp.float32)
                out_ref[0] = total.astype(jnp.bfloat16)

            pl.when(place_ref[2 * which + step] // 2 == block)(store)


def halve_late(keep_at, send_at, kept, early, late):
    rows, width = kept.shape[1:]
    at = list(keep_at) + list(send_at)
    place = jnp.stack(at + [block % 2 for block in at]).astype(jnp.int32)
    spec = lambda first: pl.BlockSpec((1, rows, width), lambda j, place: (place[first + j], 0, 0))
    out_spec = pl.BlockSpec((1, rows, width), lambda j, place: (j, 0, 0))
    shape = jax.ShapeDtypeStruct((2, rows, width), jnp.bfloat16)
    return pl.pallas_call(
        halve_late_kernel,
        grid_spec=pltpu.PrefetchScalarGridSpec(
            num_scalar_prefetch=1,
            grid=(2,),
            in_specs=[spec(0), spec(4), spec(4), spec(2), spec(6), spec(6)],
            out_specs=[out_spec, out_spec],
        ),
        out_shape=[shape, shape],
        compiler_params=pltpu.CompilerParams(vmem_limit_bytes=vmem_bytes),
        cost_estimate=light,
    )(place, kept, early, late, kept, early, late)


def combine_kernel(place_ref, *refs):
    kept_ref, sent_refs = refs[8], refs[9:]

    def put(sources, out_ref):
        total = lambda kept, came: (
            kept[0].astype(jnp.float32) + came[0].astype(jnp.float32)
        ).astype(jnp.bfloat16)
        outer, inner = total(*sources[:2]), total(*sources[2:])
        tall, low = outer.shape[0] // 4, inner.shape[0] // 4
        wide = outer.shape[1]
        both = tall + inner.shape[1] // wide * low
        for piece in range(4):
            out_ref[0, pl.ds(piece * both, tall), :] = outer[piece * tall : (piece + 1) * tall]
            for block in range(inner.shape[1] // wide):
                out_ref[0, pl.ds(piece * both + tall + block * low, low), :] = inner[
                    piece * low : (piece + 1) * low, block * wide : (block + 1) * wide
                ]

    put(refs[:4], kept_ref)
    for index, sent_ref in enumerate(sent_refs):
        pl.when(pl.program_id(0) == index)(functools.partial(put, refs[4:8], sent_ref))


def combine(keep_at, send_at, outer, inner):
    place = jnp.stack(list(keep_at) + list(send_at)).astype(jnp.int32)
    spec = lambda values, first: pl.BlockSpec(
        (1,) + values.shape[1:], lambda j, place: (place[first + j], 0, 0)
    )
    arrays = list(outer) + list(inner)
    width = outer[0].shape[2]
    rows = outer[0].shape[1] + inner[0].shape[1] * inner[0].shape[2] // width
    one = jax.ShapeDtypeStruct((1, rows, width), jnp.bfloat16)
    one_spec = pl.BlockSpec((1, rows, width), lambda j, place: (0, 0, 0))
    return pl.pallas_call(
        combine_kernel,
        grid_spec=pltpu.PrefetchScalarGridSpec(
            num_scalar_prefetch=1,
            grid=(2,),
            in_specs=[spec(values, first) for first in (0, 2) for values in arrays],
            out_specs=[
                pl.BlockSpec((1, rows, width), lambda j, place: (j, 0, 0)),
                one_spec,
                one_spec,
            ],
        ),
        out_shape=[jax.ShapeDtypeStruct((2, rows, width), jnp.bfloat16), one, one],
        compiler_params=pltpu.CompilerParams(vmem_limit_bytes=vmem_bytes),
        cost_estimate=light,
    )(place, *arrays, *arrays)


def unpack_kernel(tall, inner_blocks, place_ref, own_ref, other_ref, *out_refs):
    def put(source):
        if not inner_blocks:
            for index, out_ref in enumerate(out_refs):
                wide = out_ref.shape[1]
                out_ref[...] = source[:, index * wide : (index + 1) * wide].astype(jnp.float32)
            return
        outer_ref, inner_ref = out_refs
        low, wide = inner_ref.shape[0], source.shape[1]
        outer_ref[...] = source[pl.ds(0, tall), :].astype(jnp.float32)
        for block in range(inner_blocks):
            rows = source[pl.ds(tall + block * low, low), :]
            inner_ref[:, block * wide : (block + 1) * wide] = rows.astype(jnp.float32)

    pl.when(pl.program_id(0) == 0)(lambda: put(own_ref))
    pl.when(pl.program_id(0) == 1)(lambda: put(other_ref))


def unpack(core, own, other, count=0, tall=0, inner_blocks=0):
    rows, width = own.shape
    if inner_blocks:
        steps, block = 8, rows // 8
        low = (block - tall) // inner_blocks
        shapes = [(16 * tall, width), (16 * low, inner_blocks * width)]
        blocks = [(tall, width), (low, inner_blocks * width)]
    else:
        steps, block = 2, rows // 2
        shapes = [(2 * rows, width // count)] * count
        blocks = [(block, width // count)] * count
    return pl.pallas_call(
        functools.partial(unpack_kernel, tall, inner_blocks),
        grid_spec=pltpu.PrefetchScalarGridSpec(
            num_scalar_prefetch=1,
            grid=(2, steps),
            in_specs=[
                pl.BlockSpec(
                    (block, width),
                    lambda side, i, place: (jnp.where(side == 0, i, steps - 1), 0),
                ),
                pl.BlockSpec((block, width), lambda side, i, place: (jnp.where(side == 1, i, 0), 0)),
            ],
            out_specs=[
                pl.BlockSpec(shape, lambda side, i, place: (place[side] * steps + i, 0))
                for shape in blocks
            ],
        ),
        out_shape=[jax.ShapeDtypeStruct(shape, jnp.float32) for shape in shapes],
        compiler_params=pltpu.CompilerParams(vmem_limit_bytes=vmem_bytes),
        cost_estimate=light,
    )(jnp.stack([core, 1 - core]).astype(jnp.int32), own, other)


def norm_unit(values):
    center = values - jnp.mean(values, axis=-1, keepdims=True)
    inverse = lax.rsqrt(jnp.mean(center * center, axis=-1, keepdims=True) + norm_epsilon)
    return center * inverse, inverse


def layer_norm_back(values, norm_gain, grad):
    unit, inverse = norm_unit(values)
    scaled = grad * norm_gain
    back = scaled - jnp.mean(scaled, axis=-1, keepdims=True)
    back = back - unit * jnp.mean(scaled * unit, axis=-1, keepdims=True)
    return back * inverse


def dot_back(gradient, weight):
    return dot_nt(gradient, weight)


def column_sum(values):
    return jnp.sum(values.astype(jnp.float32), axis=0)


def swap(values, axis_name):
    return lax.ppermute(values, axis_name, [(0, 1), (1, 0)])


flips = {"x": 4, "y": 1, "z": 8}
square = ("zlo", "x", "core", "seq")


def exchange(values, axes):
    flip = [flips[axis] for axis in axes]
    return lax.ppermute(values, square, [(i, i ^ flip[i // 2 % 2]) for i in range(16)])


def square_bits(turned):
    core, x, zlo = lax.axis_index("core"), lax.axis_index("x"), lax.axis_index("zlo")
    first = 1 - core if turned else core
    return core, jnp.where(first == 1, x, zlo), jnp.where(first == 1, zlo, x)


def after(values, *others):
    return lax.optimization_barrier((values,) + others)[0]


def first_piece(shards):
    piece_rows = shards[0].shape[0] // 8
    core, high, low = square_bits(False)
    place = (core * 2 + high) * 2 + low
    piece = [
        lax.dynamic_slice_in_dim(shard, place * piece_rows, piece_rows, axis=0) for shard in shards
    ]
    return swap(piece[0] if len(piece) == 1 else jnp.concatenate(piece, axis=1), "seq")


class Pieces:
    def __init__(self, piece):
        core, high, low = square_bits(False)
        self.own = piece
        place = lambda side, one, two: (side * 2 + one) * 2 + two
        self.places = [
            place(core, high, low),
            place(core, high, 1 - low),
            place(core, 1 - high, low),
            place(core, 1 - high, 1 - low),
            place(1 - core, low, high),
            place(1 - core, low, 1 - high),
            place(1 - core, 1 - low, high),
            place(1 - core, 1 - low, 1 - high),
        ]

    def first(self, *others):
        self.own = after(self.own, *others)
        self.low = exchange(self.own, "xz")
        self.high = exchange(self.own, "zx")
        self.core = swap(self.own, "core")
        return self.low, self.high, self.core

    def second(self, *others):
        low, high = after(self.low, *others), after(self.high, *others)
        self.both = exchange(low, "zx")
        self.core_low, self.core_high = swap(low, "core"), swap(high, "core")
        return self.both, self.core_low, self.core_high

    def third(self, *others):
        self.core_both = swap(after(self.both, *others), "core")
        return [self.core_both]

    def parts(self, *others):
        return [
            after(self.own, *others),
            self.low,
            self.high,
            self.both,
            self.core,
            self.core_low,
            self.core_high,
            self.core_both,
        ]


class Total:
    def __init__(self, split, steps, turned, halves, inner=None):
        kept, sent = split
        self.inner = None
        if inner is not None:
            self.inner = (inner[0], swap(self.blocks(inner[1], 4), "core"))
            self.tall, self.inner_blocks = kept.shape[1] // 8, inner[0].shape[2] // kept.shape[2]
        self.core, self.first, self.second = square_bits(turned)
        self.seq, self.zhi = lax.axis_index("seq"), lax.axis_index("zhi")
        self.steps, self.halves = steps, halves
        self.along = ("x", "z") if turned else ("z", "x")
        self.came = swap(self.blocks(sent, 4), "core")
        self.kept = self.blocks(kept, 4)
        self.stage = 0

    def blocks(self, values, count):
        return values.reshape(count, -1, values.shape[-1])

    def by_core(self, choose):
        both = [choose([axes[core] for axes in self.steps]) for core in range(2)]
        return [jnp.where(self.core == 0, *pair) for pair in zip(*both)]

    def bits(self):
        seq, first, second = self.seq, self.first, self.second

        def one(axes):
            if axes[0] == "y":
                return [seq * 2, seq * 2 + 1, 2 - seq * 2, 3 - seq * 2]
            return [first, 2 + first, 1 - first, 3 - first]

        def two(axes):
            if axes[0] != "y" and axes[1] != "y":
                return [second, 2 + second, 1 - second, 3 - second]
            bit = first if axes[0] == "y" else seq
            return [bit * 2, bit * 2 + 1, 2 - bit * 2, 3 - bit * 2]

        def three(axes):
            bit = seq if axes[2] == "y" else second
            return [bit, 1 - bit]

        def four(axes):
            return [self.zhi, 1 - self.zhi]

        at = self.by_core((one, two, three, four)[self.stage])
        return at[: len(at) // 2], at[len(at) // 2 :]

    def step(self, *others):
        self.kept = after(self.kept, *others)
        keep, send = self.bits()
        self.kept = self.blocks(self.kept, 2 * len(keep))
        if self.stage == 0 and self.inner is not None:
            kept, came = (self.blocks(values, 4) for values in self.inner)
            self.kept, *sent = combine(keep, send, (self.kept, self.came), (kept, came))
            self.came, self.rest = exchange(sent[0], self.steps[0]), sent[1]
            self.stage += 1
            return sent[0]
        if self.stage == 1 and self.halves:
            early, late = (self.blocks(came, 2) for came in self.came)
            self.kept, sent = halve_late(keep, send, self.kept, early, late)
        else:
            split = self.stage == 0 and self.halves
            came = self.blocks(self.came, 2 * len(keep))
            self.kept, sent = halve(keep, send, self.kept, came, split)
            if split:
                self.came, self.rest = exchange(sent[0], self.steps[0]), sent[1]
                self.stage += 1
                return sent[0]
            sent = sent[0]
        if self.stage < 3:
            self.came = exchange(sent, self.steps[self.stage])
        else:
            self.came = swap(sent, "zhi")
        self.stage += 1
        return sent

    def step_rest(self, *others):
        sent = after(self.rest, self.came, *others)
        self.came = (self.came, exchange(sent, self.steps[0]))
        return sent

    def gather(self, *others):
        if self.stage > 4:
            self.part = after(self.part, *others)
        if self.stage == 4:
            piece = self.kept[0].astype(jnp.float32) + self.came[0].astype(jnp.float32)
            self.part = piece.astype(jnp.bfloat16)
            self.came = swap(self.part, "zhi")
        elif self.stage == 5:
            self.part = merge(self.zhi, self.part, self.came)
            self.came = exchange(self.part, self.along[::-1])
        elif self.stage == 6:
            self.part = merge(self.second, self.part, self.came)
            self.came = exchange(self.part, self.along)
        else:
            self.part = merge(self.first, self.part, self.came)
            self.came = swap(self.part, "core")
        self.stage += 1
        return self.part

    def advance(self, *others):
        if self.stage < 4:
            return [self.step(*others)]
        return [self.gather(*others)] if self.stage < 8 else []

    def result(self, count, *others):
        part = after(self.part, *others)
        if self.inner is None:
            return unpack(self.core, part, self.came, count)
        return unpack(self.core, part, self.came, 2, self.tall, self.inner_blocks)


def sum_plain(terms):
    terms = lax.psum_scatter(terms.astype(jnp.bfloat16), "seq", scatter_dimension=0, tiled=True)
    return lax.psum(terms, page_axes)


page_axes = ("zhi", "zlo", "x", "core")


class VectorTotal:
    def __init__(self, values):
        self.values = values
        self.axes = [axis for axis in page_axes + ("seq",) if lax.axis_size(axis) == 2]
        rest = tuple(axis for axis in page_axes + ("seq",) if lax.axis_size(axis) != 2)
        if rest:
            self.values = lax.psum(self.values, rest)
        self.came = swap(self.values, self.axes.pop(0))

    def advance(self, *others):
        if self.came is None:
            return []
        self.values, self.came = after(self.values, *others) + self.came, None
        if self.axes:
            self.came = swap(self.values, self.axes.pop(0))
        return [self.values]

    def result(self):
        while self.came is not None:
            self.advance()
        return self.values


def on_device(
    tokens,
    patches,
    lengths,
    blank_mask,
    cotangent,
    first_gain,
    first_shift,
    self_query,
    self_query_bias,
    self_key,
    self_value,
    self_value_bias,
    self_output,
    self_output_bias,
    second_gain,
    second_shift,
    cross_query,
    cross_query_bias,
    cross_key,
    cross_value,
    cross_value_bias,
    cross_output,
    cross_output_bias,
    third_gain,
    third_shift,
    ffn_inner,
    ffn_inner_bias,
    ffn_outer,
    ffn_outer_bias,
):
    seq_count = lax.axis_size("seq")
    seq_index = lax.axis_index("seq")
    vectors = (
        first_gain,
        first_shift,
        self_query_bias,
        self_value_bias,
        self_output_bias,
        second_gain,
        second_shift,
        cross_query_bias,
        cross_value_bias,
        cross_output_bias,
        third_gain,
        third_shift,
        ffn_inner_bias,
        ffn_outer_bias,
    )
    two = seq_count == 2 and lax.axis_size("zhi") == 2
    joined = jnp.concatenate(vectors).reshape(-1, 128)
    if two:
        joined_other = swap(joined, "seq")
        gathered = jnp.where(
            seq_index == 0,
            jnp.stack([joined, joined_other]),
            jnp.stack([joined_other, joined]),
        )
    else:
        gathered = lax.all_gather(joined, "seq", axis=0, tiled=False)
    gathered = gathered.reshape(seq_count, -1)
    whole_vectors, start = [], 0
    for vector in vectors:
        part = gathered[:, start : start + vector.shape[0]].reshape(-1)
        whole_vectors.append(part.astype(jnp.float32))
        start += vector.shape[0]
    (
        gain_one,
        shift_one,
        bias_self_query,
        bias_self_value,
        bias_self_output,
        gain_two,
        shift_two,
        bias_cross_query,
        bias_cross_value,
        bias_cross_output,
        gain_three,
        shift_three,
        bias_inner,
        bias_outer,
    ) = whole_vectors
    tokens, patches, cotangent = tokens[0], patches[0], cotangent[0]
    tok_rows, width = tokens.shape
    patch_rows = patches.shape[0]
    query_scale = 1.0 / math.sqrt(HEAD)

    core = lax.axis_index("core")
    self_shards = [self_query, self_key, self_value, self_output]
    cross_shards = [cross_key, cross_value, cross_query, cross_output]
    if two:
        pieces = Pieces(first_piece(self_shards))
        pieces.first(joined_other)
        tokens_other = lax.ppermute(after(tokens, pieces.own), "seq", [(0, 1)])
        pieces.second()
        cross_pieces = Pieces(first_piece([after(cross_key, pieces.low)] + cross_shards[1:]))
        pieces.third()
        whole_self = assemble(
            seq_index, pieces.places, self_shards, pieces.parts(tokens_other)
        )
        tokens_all = jnp.concatenate([tokens, after(tokens_other, whole_self)])
    else:
        gather = lambda shard: lax.all_gather(shard, "seq", axis=0, tiled=True)
        whole_self = gather(jnp.concatenate(self_shards, axis=1))
        whole_cross = gather(jnp.concatenate(cross_shards, axis=1))
        whole_ffn_inner, whole_ffn_outer = gather(ffn_inner), gather(ffn_outer)
        tokens_all, patches_all = gather(tokens), gather(patches)

    first_place = seq_index * tok_rows
    key_start = first_place if two else 0
    info = jnp.stack([first_place, lengths[0], key_start, seq_index]).astype(jnp.int32)
    self_plan = Plan(
        ("limit", "earlier") if two else ("limit",),
        tok_rows if two else tok_rows * seq_count,
        tok_rows,
        256,
        two,
    )
    cross_plan = Plan(("bias",), patch_rows * seq_count, tok_rows, 256, False)
    blank_bias = jnp.where(blank_mask[0] == 0, 0.0, masked_score).astype(jnp.float32)
    if two:
        halves = blank_bias.reshape(2, patch_rows)
        blank_bias = jnp.where(seq_index == 0, halves, halves[::-1]).reshape(-1)
    blank_bias = blank_bias[:, None]
    no_bias = jnp.zeros((self_plan.all_rows, 1), jnp.float32)

    zeros = jnp.zeros_like(bias_self_value)
    token_values = tokens.astype(jnp.float32)
    normed_all = layer_norm(tokens_all.astype(jnp.float32), gain_one, shift_one).astype(
        jnp.bfloat16
    )
    if two:
        normed_one = normed_all[:tok_rows]
    else:
        normed_one = layer_norm(token_values, gain_one, shift_one).astype(jnp.bfloat16)
    queries_self = (
        (dot_nn(normed_one, whole_self[:, :width]) + bias_self_query) * query_scale
    ).astype(jnp.bfloat16)
    self_bias = jnp.concatenate([zeros, bias_self_value])
    self_pairs = (dot_nn(normed_all, whole_self[:, width : 3 * width]) + self_bias).astype(
        jnp.bfloat16
    )
    attend_self = functools.partial(attend, self_plan, info)
    if two:
        sent = cross_pieces.first(queries_self)
        patches_other = swap(after(patches, cross_pieces.own), "seq")
        mixed_self, log_self = attend_self(
            after(queries_self, *sent), self_pairs, no_bias, 0, 1
        )
        sent = cross_pieces.second(mixed_self)
        mixed_self = after(mixed_self, patches_other, *sent)
        inner_pieces = Pieces(first_piece([after(ffn_inner, patches_other)]))
    else:
        mixed_self, log_self = attend_self(queries_self, self_pairs, no_bias, 0, 1)
    hidden_one = token_values + dot_nn(mixed_self, whole_self[:, 3 * width :]) + bias_self_output
    normed_two = layer_norm(hidden_one, gain_two, shift_two).astype(jnp.bfloat16)
    if two:
        cross_pieces.third()
        whole_cross = assemble(
            seq_index, cross_pieces.places, cross_shards, cross_pieces.parts(normed_two)
        )
        patches_all = jnp.concatenate([patches, patches_other])
        patches_all = after(patches_all, whole_cross, inner_pieces.own)
        outer_pieces = Pieces(first_piece([after(ffn_outer, inner_pieces.own)]))
    patch_bias = jnp.concatenate([zeros, bias_cross_value])
    patch_pairs = (dot_nn(patches_all, whole_cross[:, : 2 * width]) + patch_bias).astype(
        jnp.bfloat16
    )
    queries_cross = (
        (dot_nn(normed_two, whole_cross[:, 2 * width : 3 * width]) + bias_cross_query) * query_scale
    ).astype(jnp.bfloat16)
    attend_cross = functools.partial(attend, cross_plan, info)
    if two:
        keys = (patch_pairs, blank_bias)
        sent = inner_pieces.first(queries_cross) + (outer_pieces.own,)
        done = attend_cross(after(queries_cross, *sent), *keys, 0, 2)
        sent = inner_pieces.second(done[0]) + outer_pieces.first(done[0])
        done = attend_cross(after(queries_cross, *sent), *keys, 1, 2, done)
        inner_pieces.third(done[0])
        sent = outer_pieces.second(done[0])
        inner_other = join(inner_pieces.places, inner_pieces.parts(done[0], *sent))
        mixed_cross, log_cross = done
        outer_pieces.third(inner_other)
        mixed_cross = after(mixed_cross, inner_other)
    else:
        mixed_cross, log_cross = attend_cross(queries_cross, patch_pairs, blank_bias, 0, 1)
    hidden_two = hidden_one + dot_nn(mixed_cross, whole_cross[:, 3 * width :]) + bias_cross_output
    normed_three = layer_norm(hidden_two, gain_three, shift_three).astype(jnp.bfloat16)
    if two:
        outer_other = join(outer_pieces.places, outer_pieces.parts(normed_three))
        outputs, grad_normed_three, column_inner, split_outer, split_inner = ffn_both_ways(
            seq_index,
            core,
            normed_three,
            hidden_two,
            cotangent,
            ffn_inner,
            inner_other,
            ffn_outer,
            outer_other,
            bias_inner,
            bias_outer,
        )
        total_ffn = Total(split_outer, ("xy", "yz", "zx"), True, True, split_inner)
    else:
        inner_sum = dot_nn(normed_three, whole_ffn_inner) + bias_inner
        active = jax.nn.gelu(inner_sum, approximate=False).astype(jnp.bfloat16)
        outputs = (hidden_two + dot_nn(active, whole_ffn_outer) + bias_outer).astype(jnp.bfloat16)
        grad_active = dot_back(cotangent, whole_ffn_outer)
        gelu_pull = jax.vjp(lambda u: jax.nn.gelu(u, approximate=False), inner_sum)[1]
        grad_inner = gelu_pull(grad_active)[0].astype(jnp.bfloat16)
        column_inner = column_sum(grad_inner)
        grad_normed_three = dot_back(grad_inner, whole_ffn_inner)
    back_two = layer_norm_back(hidden_two, gain_three, grad_normed_three)
    grad_hidden_two = cotangent.astype(jnp.float32) + back_two
    branch_cross = grad_hidden_two.astype(jnp.bfloat16)
    grad_mixed_cross = dot_back(branch_cross, whole_cross[:, 3 * width :]).astype(jnp.bfloat16)
    back_cross = functools.partial(
        attend_back, cross_plan, info, queries_cross, mixed_cross
    )
    cross_rest = (log_cross, patch_pairs, blank_bias)
    if two:
        sent = total_ffn.step(grad_mixed_cross)
        cross_back = back_cross(after(grad_mixed_cross, sent), *cross_rest, 0, 1)
    else:
        cross_back = back_cross(grad_mixed_cross, *cross_rest, 0, 1)
    scaled_cross, grad_patch_keys, grad_patch_values = cross_back
    cross_products = [
        (normed_two, scaled_cross),
        (patches_all, grad_patch_keys),
        (patches_all, grad_patch_values),
        (mixed_cross, branch_cross),
    ]
    if two:
        scaled_cross = after(scaled_cross, total_ffn.step_rest(scaled_cross))
    grad_normed_two = dot_back(scaled_cross, whole_cross[:, 2 * width : 3 * width])
    back_one = layer_norm_back(hidden_one, gain_two, grad_normed_two)
    grad_hidden_one = grad_hidden_two + back_one
    branch_self = grad_hidden_one.astype(jnp.bfloat16)
    grad_mixed_self = dot_back(branch_self, whole_self[:, 3 * width :]).astype(jnp.bfloat16)
    back_self = functools.partial(attend_back, self_plan, info, queries_self, mixed_self)
    self_rest = (log_self, self_pairs, no_bias)
    if two:
        products = [
            (0, scaled_cross),
            (1, grad_patch_keys),
            (1, grad_patch_values),
            (2, branch_cross),
            (3, branch_self),
        ]
        lefts = [after(normed_two, grad_mixed_self), patches_all, mixed_cross, mixed_self]
        kept, sent = outer_group(core, lefts, products)
        late = total_ffn.step(kept)
        total_mid = Total((kept, after(sent, late)), ("zx", "yz", "xy"), False, True)
        sent = total_mid.step(late)
        self_back = back_self(after(grad_mixed_self, sent), *self_rest, 0, 1)
    else:
        self_back = back_self(grad_mixed_self, *self_rest, 0, 1)
    scaled_self, grad_keys, grad_values = self_back
    self_products = [
        (normed_one, scaled_self),
        (normed_all, grad_keys),
        (normed_all, grad_values),
        (mixed_self, branch_self),
    ]
    if two:
        late = (total_ffn.step(scaled_self), total_mid.step_rest(scaled_self))
        products = [(0, scaled_self), (1, grad_keys), (1, grad_values)]
        lefts = [after(normed_one, *late), normed_all]
        kept, sent = outer_group(core, lefts, products)
        late = (total_ffn.step(kept), total_mid.step(kept))
        total_last = Total((kept, after(sent, *late)), ("yz", "xy", "zx"), True, False)
        grad_keys, scaled_self = (after(values, *late) for values in (grad_keys, scaled_self))
    normed_terms = dot_back(grad_keys, whole_self[:, width : 2 * width]) + dot_back(
        grad_values, whole_self[:, 2 * width : 3 * width]
    )
    if two:
        sent = total_last.advance(normed_terms)
        for total in (total_mid, total_ffn):
            sent = sent + total.advance(sent[0])
        grad_patch_keys = after(grad_patch_keys, *sent)
    patch_terms = dot_back(grad_patch_keys, whole_cross[:, :width]) + dot_back(
        grad_patch_values, whole_cross[:, width : 2 * width]
    )
    if two:
        normed_sent = normed_terms[tok_rows:].astype(jnp.bfloat16)
        normed_came = lax.ppermute(normed_sent, "seq", [(1, 0)])
        grad_normed = normed_terms[:tok_rows] + normed_came.astype(jnp.float32)
        patch_sent = patch_terms[patch_rows:].astype(jnp.bfloat16)
        grad_patches = patch_terms[:patch_rows] + swap(patch_sent, "seq").astype(jnp.float32)
    else:
        grad_patches, grad_normed = (
            lax.psum_scatter(
                terms.astype(jnp.bfloat16), "seq", scatter_dimension=0, tiled=True
            ).astype(jnp.float32)
            for terms in (patch_terms, normed_terms)
        )
    grad_normed = grad_normed + dot_back(scaled_self, whole_self[:, :width])
    grad_tokens = grad_hidden_one + layer_norm_back(token_values, gain_one, grad_normed)
    norm_pairs = (
        (token_values, grad_normed),
        (hidden_one, grad_normed_two),
        (hidden_two, grad_normed_three),
    )
    plain = (
        scaled_self,
        grad_values,
        branch_self,
        scaled_cross,
        grad_patch_values,
        branch_cross,
        cotangent,
    )
    if two:
        late = total_last.advance(patch_terms)
        for total in (total_mid, total_ffn):
            late = late + total.advance(late[0])
        norm_pairs = ((after(token_values, *late), grad_normed),) + norm_pairs[1:]
    sums = row_sums(norm_pairs, plain)
    vector_sums = jnp.concatenate([sums, column_inner.reshape(-1, width)])
    if two:
        totals = (total_mid, total_ffn, total_last)
        late = [vector_sums]
        while any(total.stage < 8 for total in totals):
            ahead = total_last.advance(*late)
            late = ahead
            for total in totals[:-1]:
                late = late + total.advance(*ahead)
        vector_total = VectorTotal(after(vector_sums, *late))
        grad_outer, grad_ffn_in = total_ffn.result(2, *late)
        late = vector_total.advance(grad_outer)
        *wide_cross, wide_output = total_mid.result(5, *late)
        late = vector_total.advance(wide_output)
        wide_self = [*total_last.result(3, *late), wide_output]
    else:
        grad_outer = sum_plain(dot_tn(active, cotangent)).astype(jnp.float32)
        grad_ffn_in = sum_plain(dot_tn(normed_three, grad_inner)).astype(jnp.float32)
        wide_cross = [
            sum_plain(dot_tn(*product)).astype(jnp.float32) for product in cross_products
        ]
        wide_self = [sum_plain(dot_tn(*product)).astype(jnp.float32) for product in self_products]
        vector_total = VectorTotal(vector_sums)
    sums = vector_total.result()
    small_width = width // seq_count
    own_sums = lax.dynamic_slice_in_dim(sums[:-4], seq_index * small_width, small_width, axis=1)
    inner_rows = sums[-(column_inner.shape[0] // width) :].reshape(-1)
    inner_width = column_inner.shape[0] // seq_count
    own_inner = lax.dynamic_slice_in_dim(inner_rows, seq_index * inner_width, inner_width, axis=0)
    order = (0, 1, 6, 7, 8, 2, 3, 9, 10, 11, 4, 5, None, 12)
    small = [own_inner if at is None else own_sums[at] for at in order]
    totals = (
        small[0],
        small[1],
        wide_self[0],
        small[2],
        wide_self[1],
        wide_self[2],
        small[3],
        wide_self[3],
        small[4],
        small[5],
        small[6],
        wide_cross[0],
        small[7],
        wide_cross[1],
        wide_cross[2],
        small[8],
        wide_cross[3],
        small[9],
        small[10],
        small[11],
        grad_ffn_in,
        small[12],
        grad_outer,
        small[13],
    )
    return (outputs[None], grad_tokens[None], grad_patches[None]) + totals


def solution(mesh):
    page_count, seq_count = mesh.devices.shape
    mesh = Mesh(
        mesh.devices.reshape(page_count // 8, 2, 2, 2, seq_count),
        ("zhi", "zlo", "x", "core", "seq"),
    )
    page = ("zhi", "zlo", "x", "core")
    pages = P(page, "seq", None)
    rows, vector = P("seq", None), P("seq")
    layer = (
        (vector, vector)
        + (rows, vector, rows, rows, vector, rows, vector)
        + (vector, vector)
        + (rows, vector, rows, rows, vector, rows, vector)
        + (vector, vector)
        + (rows, vector, rows, vector)
    )
    return jax.shard_map(
        on_device,
        mesh=mesh,
        in_specs=(pages, pages, P(page), P(page, None), pages) + layer,
        out_specs=(pages, pages, pages) + layer,
        check_vma=False,
    )
```

```python
import functools
import math

import jax
import jax.numpy as jnp
from jax import lax
from jax.experimental import pallas as pl
from jax.experimental.pallas import tpu as pltpu
from jax.sharding import Mesh
from jax.sharding import PartitionSpec as P

HEADS = 16
HEAD = 64


norm_epsilon = 1e-05
masked_score = -1000000000.0


def layer_norm(values, norm_gain, norm_shift):
    center = values - jnp.mean(values, axis=-1, keepdims=True)
    spread = jnp.mean(center * center, axis=-1, keepdims=True)
    return center * lax.rsqrt(spread + norm_epsilon) * norm_gain + norm_shift


pair_width = 2 * HEAD
vmem_bytes = 60 * 1024 * 1024
light = pl.CostEstimate(flops=1, bytes_accessed=1, transcendentals=0)


def dot_nt(left_side, right_side):
    return lax.dot_general(
        left_side, right_side, (((1,), (1,)), ((), ())), preferred_element_type=jnp.float32
    )


def dot_nn(left_side, right_side):
    return jnp.dot(left_side, right_side, preferred_element_type=jnp.float32)


def dot_tn(left_side, right_side):
    return lax.dot_general(
        left_side, right_side, (((0,), (0,)), ((), ())), preferred_element_type=jnp.float32
    )


def one_head(values, head):
    lane = lax.broadcasted_iota(jnp.int32, values.shape, 1)
    return jnp.where((lane >= head * HEAD) & (lane < (head + 1) * HEAD), values, 0)


class Plan:
    def __init__(self, kinds, key_rows, query_rows, chunk, causal):
        self.kinds = kinds
        self.key_rows = key_rows
        self.all_rows = key_rows * len(kinds)
        self.query_rows = query_rows
        self.chunk = min(chunk, query_rows)
        self.causal = causal

    def blocks(self, start, segments):
        found = []
        for segment in segments:
            rows = self.key_rows
            if self.causal and self.kinds[segment] == "limit":
                rows = min(rows, start + self.chunk)
            found.append((self.kinds[segment], pl.ds(segment * self.key_rows, rows)))
        return found


def query_limit(info_ref, start, chunk):
    lane = lax.broadcasted_iota(jnp.int32, (1, chunk), 1) + start
    place = info_ref[0] + lane
    return jnp.minimum(place, info_ref[1] - 1) - info_ref[2]


def masked_block(kind, scores, limit, bias_ref):
    if kind == "limit":
        key = lax.broadcasted_iota(jnp.int32, scores.shape, 0)
        return jnp.where(key <= limit, scores, masked_score)
    if kind == "bias":
        return scores + bias_ref[...]
    return scores


def run_segments(plan, info_ref, body):
    every = list(range(len(plan.kinds)))
    needed = [segment for segment in every if plan.kinds[segment] != "earlier"]
    if len(needed) == len(every):
        body(every)
        return
    pl.when(info_ref[3] == 1)(lambda: body(every))
    pl.when(info_ref[3] != 1)(lambda: body(needed))


def attend_kernel(plan, info_ref, query_ref, key_ref, value_ref, bias_ref, mixed_ref, log_ref):
    def body(segments):
        for start in range(0, plan.query_rows, plan.chunk):
            limit = query_limit(info_ref, start, plan.chunk)
            lane = lax.broadcasted_iota(jnp.int32, (1, plan.chunk), 1) + start
            valid = (info_ref[0] + lane < info_ref[1]).astype(jnp.float32)
            query = query_ref[pl.ds(start, plan.chunk), :]
            parts = []
            for head in range(2):
                head_query = one_head(query, head)
                blocks = plan.blocks(start, segments)
                scores = [
                    masked_block(kind, dot_nt(key_ref[rows, :], head_query), limit, bias_ref)
                    for kind, rows in blocks
                ]
                peak = jnp.max(scores[0], axis=0, keepdims=True)
                for block in scores[1:]:
                    peak = jnp.maximum(peak, jnp.max(block, axis=0, keepdims=True))
                total = jnp.zeros_like(peak)
                mixed = jnp.zeros((pair_width, plan.chunk), jnp.float32)
                for (kind, rows), block in zip(blocks, scores):
                    weights = jnp.exp(block - peak)
                    total = total + jnp.sum(weights, axis=0, keepdims=True)
                    mixed = mixed + dot_tn(value_ref[rows, :], weights.astype(jnp.bfloat16))
                parts.append(mixed[head * HEAD : (head + 1) * HEAD] * (valid / total))
                log_ref[0, pl.ds(head, 1), pl.ds(start, plan.chunk)] = peak + jnp.log(total)
            joined = jnp.concatenate(parts, axis=0)
            mixed_ref[pl.ds(start, plan.chunk), :] = joined.T.astype(jnp.bfloat16)

    run_segments(plan, info_ref, body)


def attend_back_kernel(
    plan,
    info_ref,
    query_ref,
    mixed_ref,
    grad_ref,
    log_ref,
    key_ref,
    value_ref,
    bias_ref,
    grad_query_ref,
    grad_key_ref,
    grad_value_ref,
    key_sum,
    value_sum,
):
    def body(segments):
        key_sum[...] = jnp.zeros_like(key_sum)
        value_sum[...] = jnp.zeros_like(value_sum)
        for start in range(0, plan.query_rows, plan.chunk):
            limit = query_limit(info_ref, start, plan.chunk)
            rows_here = pl.ds(start, plan.chunk)
            row = lax.broadcasted_iota(jnp.int32, (plan.chunk, 1), 0) + start
            valid = info_ref[0] + row < info_ref[1]
            query = query_ref[rows_here, :]
            grad = jnp.where(valid, grad_ref[rows_here, :], 0).astype(jnp.bfloat16)
            product = grad.astype(jnp.float32) * mixed_ref[rows_here, :].astype(jnp.float32)
            product = product.T
            parts = []
            for head in range(2):
                own = slice(head * HEAD, (head + 1) * HEAD)
                head_query, head_grad = one_head(query, head), one_head(grad, head)
                weighted = jnp.sum(product[own], axis=0, keepdims=True)
                log_total = log_ref[0, pl.ds(head, 1), rows_here]
                grad_query = jnp.zeros((pair_width, plan.chunk), jnp.float32)
                for kind, rows in plan.blocks(start, segments):
                    keys = key_ref[rows, :]
                    scores = masked_block(kind, dot_nt(keys, head_query), limit, bias_ref)
                    shares = jnp.exp(scores - log_total)
                    grad_shares = dot_nt(value_ref[rows, :], head_grad)
                    grad_scores = (shares * (grad_shares - weighted)).astype(jnp.bfloat16)
                    value_sum[rows, :] += dot_nn(shares.astype(jnp.bfloat16), head_grad)
                    key_sum[rows, :] += dot_nn(grad_scores, head_query)
                    grad_query = grad_query + dot_tn(keys, grad_scores)
                parts.append(grad_query[own])
            joined = jnp.concatenate(parts, axis=0) * (1.0 / math.sqrt(HEAD))
            grad_query_ref[rows_here, :] = joined.T.astype(jnp.bfloat16)
        grad_key_ref[...] = key_sum[...].astype(jnp.bfloat16)
        grad_value_ref[...] = value_sum[...].astype(jnp.bfloat16)

    run_segments(plan, info_ref, body)


def column_block(rows, first):
    return pl.BlockSpec((rows, pair_width), lambda step, info: (0, first + step))


def log_block(rows, first):
    return pl.BlockSpec((1, 2, rows), lambda step, info: (first + step, 0, 0))


def key_specs(plan, first):
    return [
        column_block(plan.all_rows, first),
        column_block(plan.all_rows, HEADS // 2 + first),
        pl.BlockSpec((plan.all_rows, 1), lambda step, info: (0, 0)),
    ]


any_block = pl.BlockSpec(memory_space=pl.ANY)


def skip_refs(kernel, place, count):
    def run(*refs):
        kernel(*refs[:place], *refs[place + count :])

    return run


def attend(plan, info, queries, key_values, bias, part, parts, into=()):
    pairs = HEADS // 2
    count, first = pairs // parts, part * (pairs // parts)
    rows, keys = plan.query_rows, plan.all_rows
    return pl.pallas_call(
        skip_refs(functools.partial(attend_kernel, plan), 5, len(into)),
        grid_spec=pltpu.PrefetchScalarGridSpec(
            num_scalar_prefetch=1,
            grid=(count,),
            in_specs=[column_block(rows, first)] + key_specs(plan, first) + [any_block] * len(into),
            out_specs=[column_block(rows, first), log_block(rows, first)],
        ),
        out_shape=[
            jax.ShapeDtypeStruct((rows, HEADS * HEAD), jnp.bfloat16),
            jax.ShapeDtypeStruct((pairs, 2, rows), jnp.float32),
        ],
        input_output_aliases={5 + index: index for index in range(len(into))},
        compiler_params=pltpu.CompilerParams(vmem_limit_bytes=vmem_bytes),
        cost_estimate=light,
    )(info, queries, key_values, key_values, bias, *into)


def attend_back(
    plan, info, queries, mixed, grad_mixed, log_total, key_values, bias, part, parts, into=()
):
    pairs = HEADS // 2
    count, first = pairs // parts, part * (pairs // parts)
    rows, keys = plan.query_rows, plan.all_rows
    return pl.pallas_call(
        skip_refs(functools.partial(attend_back_kernel, plan), 8, len(into)),
        grid_spec=pltpu.PrefetchScalarGridSpec(
            num_scalar_prefetch=1,
            grid=(count,),
            in_specs=[column_block(rows, first)] * 3
            + [log_block(rows, first)]
            + key_specs(plan, first)
            + [any_block] * len(into),
            out_specs=[
                column_block(rows, first),
                column_block(keys, first),
                column_block(keys, first),
            ],
            scratch_shapes=[pltpu.VMEM((keys, pair_width), jnp.float32)] * 2,
        ),
        out_shape=[
            jax.ShapeDtypeStruct((rows, HEADS * HEAD), jnp.bfloat16),
            jax.ShapeDtypeStruct((keys, HEADS * HEAD), jnp.bfloat16),
            jax.ShapeDtypeStruct((keys, HEADS * HEAD), jnp.bfloat16),
        ],
        input_output_aliases={8 + index: index for index in range(len(into))},
        compiler_params=pltpu.CompilerParams(vmem_limit_bytes=vmem_bytes),
        cost_estimate=light,
    )(info, queries, mixed, grad_mixed, log_total, key_values, key_values, bias, *into)


def join_kernel(count, place_ref, *refs):
    out_ref = refs[count]
    for index, source in enumerate(refs[:count]):
        rows = source.shape[0]
        first = pl.multiple_of(place_ref[index] * rows, rows)
        out_ref[pl.ds(first, rows), :] = source[...]


def join(places, parts):
    count, (rows, width) = len(parts), parts[0].shape
    steps = 1 if count * rows * width <= 1024 * 1024 else 4
    wide = width // steps
    return pl.pallas_call(
        functools.partial(join_kernel, count),
        grid_spec=pltpu.PrefetchScalarGridSpec(
            num_scalar_prefetch=1,
            grid=(steps,),
            in_specs=[pl.BlockSpec((rows, wide), lambda i, place: (0, i))] * count,
            out_specs=pl.BlockSpec((count * rows, wide), lambda i, place: (0, i)),
        ),
        out_shape=jax.ShapeDtypeStruct((count * rows, width), parts[0].dtype),
        compiler_params=pltpu.CompilerParams(vmem_limit_bytes=vmem_bytes),
        cost_estimate=light,
    )(jnp.stack(places).astype(jnp.int32), *parts)


def merge(index, own, other):
    return join([index, 1 - index], [own, other])


def assemble_kernel(count, place_ref, *refs):
    shards, parts, out_ref = refs[:count], refs[count:-1], refs[-1]
    for index, part in enumerate(parts):
        rows = part.shape[0]
        first = pl.multiple_of(place_ref[1 + index] * rows, rows)
        out_ref[pl.ds(first, rows), :] = part[...]
    for index, shard in enumerate(shards):

        def store(shard=shard):
            rows = shard.shape[0]
            first = pl.multiple_of(place_ref[0] * rows, rows)
            out_ref[pl.ds(first, rows), :] = shard[...]

        pl.when(pl.program_id(0) == index)(store)


def assemble(seq, places, shards, parts):
    count, (rows, wide) = len(shards), shards[0].shape
    part_rows = parts[0].shape[0]
    places = [seq] + [(1 - seq) * len(parts) + place for place in places]
    return pl.pallas_call(
        functools.partial(assemble_kernel, count),
        grid_spec=pltpu.PrefetchScalarGridSpec(
            num_scalar_prefetch=1,
            grid=(count,),
            in_specs=[pl.BlockSpec((rows, wide), lambda i, place: (0, 0))] * count
            + [pl.BlockSpec((part_rows, wide), lambda i, place: (0, i))] * len(parts),
            out_specs=pl.BlockSpec((2 * rows, wide), lambda i, place: (0, i)),
        ),
        out_shape=jax.ShapeDtypeStruct((2 * rows, count * wide), shards[0].dtype),
        compiler_params=pltpu.CompilerParams(vmem_limit_bytes=vmem_bytes),
        cost_estimate=light,
    )(jnp.stack(places).astype(jnp.int32), *shards, *parts)


def row_sums_kernel(norms, plain, *refs):
    steps = refs[: 2 * norms + plain]
    out_ref = refs[-1]

    @pl.when(pl.program_id(0) == 0)
    def start():
        out_ref[...] = jnp.zeros_like(out_ref)

    for index in range(norms):
        values, grad = steps[2 * index][...].astype(jnp.float32), steps[2 * index + 1][...]
        center = values - jnp.mean(values, axis=-1, keepdims=True)
        spread = jnp.mean(center * center, axis=-1, keepdims=True)
        unit = center * lax.rsqrt(spread + norm_epsilon)
        out_ref[pl.ds(2 * index, 1), :] += jnp.sum(grad * unit, axis=0, keepdims=True)
        out_ref[pl.ds(2 * index + 1, 1), :] += jnp.sum(grad, axis=0, keepdims=True)
    for index in range(plain):
        values = steps[2 * norms + index][...].astype(jnp.float32)
        at = pl.ds(2 * norms + index, 1)
        out_ref[at, :] += jnp.sum(values, axis=0, keepdims=True)


def row_sums(norm_pairs, plain):
    arrays = [values for pair in norm_pairs for values in pair] + list(plain)
    width = arrays[0].shape[1]
    rows = -(-(2 * len(norm_pairs) + len(plain)) // 8) * 8
    return pl.pallas_call(
        functools.partial(row_sums_kernel, len(norm_pairs), len(plain)),
        grid=(4,),
        in_specs=[
            pl.BlockSpec((values.shape[0] // 4, width), lambda step: (step, 0)) for values in arrays
        ],
        out_specs=pl.BlockSpec((rows, width), lambda step: (0, 0)),
        out_shape=jax.ShapeDtypeStruct((rows, width), jnp.float32),
        compiler_params=pltpu.CompilerParams(vmem_limit_bytes=vmem_bytes),
        cost_estimate=light,
    )(*arrays)


def ffn_kernel(half_steps, place_ref, *refs):
    normed, inner = refs[0:4], refs[4:8]
    outer_own, outer_other, bias_ref, bias_outer_ref, hidden_ref, cotangent_ref = refs[8:14]
    out_ref, grad_ref, column_ref, kept_outer, sent_outer, kept_inner, sent_inner = refs[14:21]
    total_ref, turned_ref = refs[21], refs[22]
    grad_sums = refs[23:27]
    step = pl.program_id(0)
    quarter = normed[0].shape[1]

    @pl.when(step == 0)
    def start():
        for index in range(4):
            turned_ref[index] = normed[index][...].T
            grad_sums[index][...] = jnp.zeros_like(grad_sums[index])
        total_ref[...] = hidden_ref[...] + bias_outer_ref[...]

    def run(outer_ref):
        inner_sum = bias_ref[...] + dot_nn(normed[0][...], inner[0][...])
        for index in range(1, 4):
            inner_sum = inner_sum + dot_nn(normed[index][...], inner[index][...])
        part = 0.5 + 0.5 * lax.erf(inner_sum * math.sqrt(0.5))
        active = (inner_sum * part).astype(jnp.bfloat16)
        slope = part + inner_sum * (
            jnp.exp(-0.5 * inner_sum * inner_sum) * (1.0 / math.sqrt(2.0 * math.pi))
        )
        cotangent = cotangent_ref[...]
        total_ref[...] += dot_nn(active, outer_ref[...])
        grad_inner = (dot_nt(cotangent, outer_ref[...]) * slope).astype(jnp.bfloat16)
        column_ref[...] = jnp.sum(grad_inner.astype(jnp.float32), axis=0, keepdims=True)
        for index in range(4):
            grad_sums[index][...] += dot_nt(grad_inner, inner[index][...])
        grad_outer = dot_tn(active, cotangent).astype(jnp.bfloat16)
        for which, out in ((0, kept_outer), (1, sent_outer)):

            def store(out=out):
                out[0] = grad_outer

            pl.when(step % 2 == which)(store)
        for index, (out, seq_at) in enumerate(
            ((kept_inner, 0), (sent_inner, 0), (kept_inner, 1), (sent_inner, 1))
        ):
            out[pl.ds(place_ref[seq_at], 1)] = dot_nn(turned_ref[index], grad_inner).astype(
                jnp.bfloat16
            )[None]

    pl.when(step < half_steps)(lambda: run(outer_own))
    pl.when(step >= half_steps)(lambda: run(outer_other))

    @pl.when(step == 2 * half_steps - 1)
    def finish():
        out_ref[...] = total_ref[...].astype(jnp.bfloat16)
        for index in range(4):
            first = pl.multiple_of(place_ref[4 + index] * quarter, quarter)
            grad_ref[:, pl.ds(first, quarter)] = grad_sums[index][...]


def ffn_both_ways(
    seq, core, normed, hidden, cotangent, inner_own, inner_other, outer_own, outer_other, bias, last
):
    rows, width = normed.shape
    units = inner_own.shape[1]
    chunk, quarter = units // 4, width // 4
    steps = units // chunk
    half_steps = steps // 2
    run = half_steps // 2
    order = []
    for step in range(steps):
        which, at = (seq, step) if step < half_steps else (1 - seq, step - half_steps)
        side = core if at % 2 == 0 else 1 - core
        order.append((which, side * run + at // 2))
    local = [at for _, at in order]
    whole = [which * half_steps + at for which, at in order]
    out_at = [which * run + step % half_steps // 2 for step, (which, _) in enumerate(order)]
    quarters = [seq * 2 + core, seq * 2 + 1 - core, (1 - seq) * 2 + core, (1 - seq) * 2 + 1 - core]
    place = jnp.stack(
        [seq, 1 - seq, core, 1 - core] + quarters + whole + local + out_at
    ).astype(jnp.int32)
    at_whole, at_local, at_out = 8, 8 + steps, 8 + 2 * steps
    fixed = lambda shape: pl.BlockSpec(shape, lambda step, place: (0,) * len(shape))
    normed_specs = [
        pl.BlockSpec((rows, quarter), lambda step, place, i=i: (0, place[4 + i])) for i in range(4)
    ]
    inner_specs = [
        pl.BlockSpec(
            (quarter, chunk), lambda step, place, i=i: (place[2 + i % 2], place[at_whole + step])
        )
        for i in range(4)
    ]
    own_at = lambda step, place: place[at_local + jnp.minimum(step, half_steps - 1)]
    other_at = lambda step, place: place[at_local + jnp.maximum(step, half_steps)]
    outer_shape = jax.ShapeDtypeStruct((2 * run, chunk, width), jnp.bfloat16)
    inner_shape = jax.ShapeDtypeStruct((2, quarter, units), jnp.bfloat16)
    outer_spec = pl.BlockSpec((1, chunk, width), lambda step, place: (place[at_out + step], 0, 0))
    inner_spec = pl.BlockSpec(
        (2, quarter, chunk), lambda step, place: (0, 0, place[at_whole + step])
    )
    row_spec = pl.BlockSpec((1, chunk), lambda step, place: (0, place[at_whole + step]))
    out, grad, column, kept_outer, sent_outer, kept_inner, sent_inner = pl.pallas_call(
        functools.partial(ffn_kernel, half_steps),
        grid_spec=pltpu.PrefetchScalarGridSpec(
            num_scalar_prefetch=1,
            grid=(steps,),
            in_specs=normed_specs
            + inner_specs
            + [
                pl.BlockSpec((chunk, width), lambda step, place: (own_at(step, place), 0)),
                pl.BlockSpec((chunk, width), lambda step, place: (other_at(step, place), 0)),
                row_spec,
                fixed((1, width)),
                fixed((rows, width)),
                fixed((rows, width)),
            ],
            out_specs=[
                fixed((rows, width)),
                fixed((rows, width)),
                row_spec,
                outer_spec,
                outer_spec,
                inner_spec,
                inner_spec,
            ],
            scratch_shapes=[
                pltpu.VMEM((rows, width), jnp.float32),
                pltpu.VMEM((4, quarter, rows), jnp.bfloat16),
            ]
            + [pltpu.VMEM((rows, quarter), jnp.float32)] * 4,
        ),
        out_shape=[
            jax.ShapeDtypeStruct((rows, width), jnp.bfloat16),
            jax.ShapeDtypeStruct((rows, width), jnp.float32),
            jax.ShapeDtypeStruct((1, units), jnp.float32),
            outer_shape,
            outer_shape,
            inner_shape,
            inner_shape,
        ],
        compiler_params=pltpu.CompilerParams(vmem_limit_bytes=vmem_bytes),
        cost_estimate=light,
    )(
        place,
        *[normed] * 4,
        inner_own,
        inner_own,
        inner_other,
        inner_other,
        outer_own,
        outer_other,
        bias[None],
        last[None],
        hidden,
        cotangent,
    )
    split = lambda kept, sent: (kept.reshape(2, -1, kept.shape[2]), sent.reshape(2, -1, kept.shape[2]))
    return out, grad, column[0], split(kept_outer, sent_outer), (kept_inner, sent_inner)


def outer_group_kernel(products, count, place_ref, *refs):
    lefts, rights = refs[:count], refs[count : count + len(products)]
    kept_ref, sent_ref, turned_ref = refs[count + len(products) :]
    part = kept_ref.shape[1]
    step = pl.program_id(0)
    sides = [side for side, _ in products]
    start = 0
    for index, (side, blocks) in enumerate(products):
        left, right = lefts[side], rights[index]
        tokens = pl.ds(0, left.shape[0])
        if sides.index(side) == index:

            def turn(left=left, tokens=tokens):
                turned_ref[:, tokens] = left[...].T

            pl.when(step == start)(turn)

        def run(right=right, tokens=tokens):
            for seq in range(2):
                for which, out_ref in ((0, kept_ref), (1, sent_ref)):
                    first = pl.multiple_of((seq * 2 + place_ref[which]) * part, part)
                    rows = turned_ref[pl.ds(first, part), tokens]
                    out_ref[seq] = dot_nn(rows, right[...]).astype(jnp.bfloat16)

        pl.when((step >= start) & (step < start + blocks))(run)
        start += blocks


def outer_group(core, lefts, products):
    chunk = 512
    width = lefts[0].shape[1]
    part = width // 4
    tokens = max(left.shape[0] for left in lefts)
    specs, start = [], 0
    for _, right in products:
        blocks = right.shape[1] // chunk
        specs.append(
            pl.BlockSpec(
                (right.shape[0], chunk),
                lambda step, place, start=start, blocks=blocks: (
                    0,
                    jnp.clip(step - start, 0, blocks - 1),
                ),
            )
        )
        start += blocks
    out_spec = pl.BlockSpec((2, part, chunk), lambda step, place: (0, 0, step))
    shape = jax.ShapeDtypeStruct((2, part, start * chunk), jnp.bfloat16)
    kinds = [(side, right.shape[1] // chunk) for side, right in products]
    return pl.pallas_call(
        functools.partial(outer_group_kernel, kinds, len(lefts)),
        grid_spec=pltpu.PrefetchScalarGridSpec(
            num_scalar_prefetch=1,
            grid=(start,),
            in_specs=[pl.BlockSpec(left.shape, lambda step, place: (0, 0)) for left in lefts]
            + specs,
            out_specs=[out_spec, out_spec],
            scratch_shapes=[pltpu.VMEM((width, tokens), jnp.bfloat16)],
        ),
        out_shape=[shape, shape],
        compiler_params=pltpu.CompilerParams(vmem_limit_bytes=vmem_bytes),
        cost_estimate=light,
    )(
        jnp.stack([core, 1 - core]).astype(jnp.int32),
        *lefts,
        *[right for _, right in products],
    )


def halve_kernel(split, place_ref, kept_a, came_a, kept_b, came_b, kept_ref, *sent_refs):
    add = lambda kept, came: (kept[0].astype(jnp.float32) + came[0].astype(jnp.float32)).astype(
        jnp.bfloat16
    )
    kept_ref[0] = add(kept_a, came_a)
    if not split:
        sent_refs[0][0] = add(kept_b, came_b)
        return

    for index, sent_ref in enumerate(sent_refs):

        def store(sent_ref=sent_ref):
            sent_ref[0] = add(kept_b, came_b)

        pl.when(pl.program_id(0) == index)(store)


def halve(keep_at, send_at, kept, came, split=False):
    blocks, rows, width = kept.shape
    count = len(keep_at)
    place = jnp.stack(list(keep_at) + list(send_at)).astype(jnp.int32)
    tiles = 2 if rows * width >= 256 * 1024 else 1
    wide = width // tiles
    spec = lambda first: pl.BlockSpec(
        (1, rows, wide), lambda j, i, place: (place[first + j], 0, i)
    )
    out_spec = pl.BlockSpec((1, rows, wide), lambda j, i, place: (j, 0, i))
    one_spec = lambda at: pl.BlockSpec(
        (1, rows, wide),
        lambda j, i, place: (0, 0, jnp.where(j == at, i, jnp.where(j > at, tiles - 1, 0))),
    )
    shape = jax.ShapeDtypeStruct((count, rows, width), jnp.bfloat16)
    one = jax.ShapeDtypeStruct((1, rows, width), jnp.bfloat16)
    out = pl.pallas_call(
        functools.partial(halve_kernel, split),
        grid_spec=pltpu.PrefetchScalarGridSpec(
            num_scalar_prefetch=1,
            grid=(count, tiles),
            in_specs=[spec(0), spec(0), spec(count), spec(count)],
            out_specs=[out_spec]
            + ([one_spec(at) for at in range(count)] if split else [out_spec]),
        ),
        out_shape=[shape] + ([one] * count if split else [shape]),
        compiler_params=pltpu.CompilerParams(vmem_limit_bytes=vmem_bytes),
        cost_estimate=light,
    )(place, kept, came, kept, came)
    return out[0], out[1:]


def halve_late_kernel(place_ref, *refs):
    step = pl.program_id(0)
    for which in range(2):
        own_ref, early_ref, late_ref = refs[3 * which : 3 * which + 3]
        out_ref = refs[6 + which]
        for block, came_ref in enumerate((early_ref, late_ref)):

            def store(out_ref=out_ref, own_ref=own_ref, came_ref=came_ref):
                total = own_ref[0].astype(jnp.float32) + came_ref[0].astype(jnp.float32)
                out_ref[0] = total.astype(jnp.bfloat16)

            pl.when(place_ref[2 * which + step] // 2 == block)(store)


def halve_late(keep_at, send_at, kept, early, late):
    rows, width = kept.shape[1:]
    at = list(keep_at) + list(send_at)
    place = jnp.stack(at + [block % 2 for block in at]).astype(jnp.int32)
    spec = lambda first: pl.BlockSpec((1, rows, width), lambda j, place: (place[first + j], 0, 0))
    out_spec = pl.BlockSpec((1, rows, width), lambda j, place: (j, 0, 0))
    shape = jax.ShapeDtypeStruct((2, rows, width), jnp.bfloat16)
    return pl.pallas_call(
        halve_late_kernel,
        grid_spec=pltpu.PrefetchScalarGridSpec(
            num_scalar_prefetch=1,
            grid=(2,),
            in_specs=[spec(0), spec(4), spec(4), spec(2), spec(6), spec(6)],
            out_specs=[out_spec, out_spec],
        ),
        out_shape=[shape, shape],
        compiler_params=pltpu.CompilerParams(vmem_limit_bytes=vmem_bytes),
        cost_estimate=light,
    )(place, kept, early, late, kept, early, late)


def combine_kernel(place_ref, *refs):
    kept_ref, sent_refs = refs[8], refs[9:]

    def put(sources, out_ref):
        total = lambda kept, came: (
            kept[0].astype(jnp.float32) + came[0].astype(jnp.float32)
        ).astype(jnp.bfloat16)
        outer, inner = total(*sources[:2]), total(*sources[2:])
        tall, low = outer.shape[0] // 4, inner.shape[0] // 4
        wide = outer.shape[1]
        both = tall + inner.shape[1] // wide * low
        for piece in range(4):
            out_ref[0, pl.ds(piece * both, tall), :] = outer[piece * tall : (piece + 1) * tall]
            for block in range(inner.shape[1] // wide):
                out_ref[0, pl.ds(piece * both + tall + block * low, low), :] = inner[
                    piece * low : (piece + 1) * low, block * wide : (block + 1) * wide
                ]

    put(refs[:4], kept_ref)
    for index, sent_ref in enumerate(sent_refs):
        pl.when(pl.program_id(0) == index)(functools.partial(put, refs[4:8], sent_ref))


def combine(keep_at, send_at, outer, inner):
    place = jnp.stack(list(keep_at) + list(send_at)).astype(jnp.int32)
    spec = lambda values, first: pl.BlockSpec(
        (1,) + values.shape[1:], lambda j, place: (place[first + j], 0, 0)
    )
    arrays = list(outer) + list(inner)
    width = outer[0].shape[2]
    rows = outer[0].shape[1] + inner[0].shape[1] * inner[0].shape[2] // width
    one = jax.ShapeDtypeStruct((1, rows, width), jnp.bfloat16)
    one_spec = pl.BlockSpec((1, rows, width), lambda j, place: (0, 0, 0))
    return pl.pallas_call(
        combine_kernel,
        grid_spec=pltpu.PrefetchScalarGridSpec(
            num_scalar_prefetch=1,
            grid=(2,),
            in_specs=[spec(values, first) for first in (0, 2) for values in arrays],
            out_specs=[
                pl.BlockSpec((1, rows, width), lambda j, place: (j, 0, 0)),
                one_spec,
                one_spec,
            ],
        ),
        out_shape=[jax.ShapeDtypeStruct((2, rows, width), jnp.bfloat16), one, one],
        compiler_params=pltpu.CompilerParams(vmem_limit_bytes=vmem_bytes),
        cost_estimate=light,
    )(place, *arrays, *arrays)


def unpack_kernel(tall, inner_blocks, place_ref, own_ref, other_ref, *out_refs):
    def put(source):
        if not inner_blocks:
            for index, out_ref in enumerate(out_refs):
                wide = out_ref.shape[1]
                out_ref[...] = source[:, index * wide : (index + 1) * wide].astype(jnp.float32)
            return
        outer_ref, inner_ref = out_refs
        low, wide = inner_ref.shape[0], source.shape[1]
        outer_ref[...] = source[pl.ds(0, tall), :].astype(jnp.float32)
        for block in range(inner_blocks):
            rows = source[pl.ds(tall + block * low, low), :]
            inner_ref[:, block * wide : (block + 1) * wide] = rows.astype(jnp.float32)

    pl.when(pl.program_id(0) == 0)(lambda: put(own_ref))
    pl.when(pl.program_id(0) == 1)(lambda: put(other_ref))


def unpack(core, own, other, count=0, tall=0, inner_blocks=0):
    rows, width = own.shape
    if inner_blocks:
        steps, block = 8, rows // 8
        low = (block - tall) // inner_blocks
        shapes = [(16 * tall, width), (16 * low, inner_blocks * width)]
        blocks = [(tall, width), (low, inner_blocks * width)]
    else:
        steps, block = 2, rows // 2
        shapes = [(2 * rows, width // count)] * count
        blocks = [(block, width // count)] * count
    return pl.pallas_call(
        functools.partial(unpack_kernel, tall, inner_blocks),
        grid_spec=pltpu.PrefetchScalarGridSpec(
            num_scalar_prefetch=1,
            grid=(2, steps),
            in_specs=[
                pl.BlockSpec(
                    (block, width),
                    lambda side, i, place: (jnp.where(side == 0, i, steps - 1), 0),
                ),
                pl.BlockSpec((block, width), lambda side, i, place: (jnp.where(side == 1, i, 0), 0)),
            ],
            out_specs=[
                pl.BlockSpec(shape, lambda side, i, place: (place[side] * steps + i, 0))
                for shape in blocks
            ],
        ),
        out_shape=[jax.ShapeDtypeStruct(shape, jnp.float32) for shape in shapes],
        compiler_params=pltpu.CompilerParams(vmem_limit_bytes=vmem_bytes),
        cost_estimate=light,
    )(jnp.stack([core, 1 - core]).astype(jnp.int32), own, other)


def norm_unit(values):
    center = values - jnp.mean(values, axis=-1, keepdims=True)
    inverse = lax.rsqrt(jnp.mean(center * center, axis=-1, keepdims=True) + norm_epsilon)
    return center * inverse, inverse


def layer_norm_back(values, norm_gain, grad):
    unit, inverse = norm_unit(values)
    scaled = grad * norm_gain
    back = scaled - jnp.mean(scaled, axis=-1, keepdims=True)
    back = back - unit * jnp.mean(scaled * unit, axis=-1, keepdims=True)
    return back * inverse


def dot_back(gradient, weight):
    return dot_nt(gradient, weight)


def column_sum(values):
    return jnp.sum(values.astype(jnp.float32), axis=0)


def swap(values, axis_name):
    return lax.ppermute(values, axis_name, [(0, 1), (1, 0)])


flips = {"x": 4, "y": 1, "z": 8}
square = ("zlo", "x", "core", "seq")


def exchange(values, axes):
    flip = [flips[axis] for axis in axes]
    return lax.ppermute(values, square, [(i, i ^ flip[i // 2 % 2]) for i in range(16)])


def square_bits(turned):
    core, x, zlo = lax.axis_index("core"), lax.axis_index("x"), lax.axis_index("zlo")
    first = 1 - core if turned else core
    return core, jnp.where(first == 1, x, zlo), jnp.where(first == 1, zlo, x)


def after(values, *others):
    return lax.optimization_barrier((values,) + others)[0]


def first_piece(shards):
    piece_rows = shards[0].shape[0] // 8
    core, high, low = square_bits(False)
    place = (core * 2 + high) * 2 + low
    piece = [
        lax.dynamic_slice_in_dim(shard, place * piece_rows, piece_rows, axis=0) for shard in shards
    ]
    return swap(piece[0] if len(piece) == 1 else jnp.concatenate(piece, axis=1), "seq")


class Pieces:
    def __init__(self, piece):
        core, high, low = square_bits(False)
        self.own = piece
        place = lambda side, one, two: (side * 2 + one) * 2 + two
        self.places = [
            place(core, high, low),
            place(core, high, 1 - low),
            place(core, 1 - high, low),
            place(core, 1 - high, 1 - low),
            place(1 - core, low, high),
            place(1 - core, low, 1 - high),
            place(1 - core, 1 - low, high),
            place(1 - core, 1 - low, 1 - high),
        ]

    def first(self, *others):
        self.own = after(self.own, *others)
        self.low = exchange(self.own, "xz")
        self.high = exchange(self.own, "zx")
        self.core = swap(self.own, "core")
        return self.low, self.high, self.core

    def second(self, *others):
        low, high = after(self.low, *others), after(self.high, *others)
        self.both = exchange(low, "zx")
        self.core_low, self.core_high = swap(low, "core"), swap(high, "core")
        return self.both, self.core_low, self.core_high

    def third(self, *others):
        self.core_both = swap(after(self.both, *others), "core")
        return [self.core_both]

    def parts(self, *others):
        return [
            after(self.own, *others),
            self.low,
            self.high,
            self.both,
            self.core,
            self.core_low,
            self.core_high,
            self.core_both,
        ]


class Total:
    def __init__(self, split, steps, turned, halves, inner=None):
        kept, sent = split
        self.inner = None
        if inner is not None:
            self.inner = (inner[0], swap(self.blocks(inner[1], 4), "core"))
            self.tall, self.inner_blocks = kept.shape[1] // 8, inner[0].shape[2] // kept.shape[2]
        self.core, self.first, self.second = square_bits(turned)
        self.seq, self.zhi = lax.axis_index("seq"), lax.axis_index("zhi")
        self.steps, self.halves = steps, halves
        self.along = ("x", "z") if turned else ("z", "x")
        self.came = swap(self.blocks(sent, 4), "core")
        self.kept = self.blocks(kept, 4)
        self.stage = 0

    def blocks(self, values, count):
        return values.reshape(count, -1, values.shape[-1])

    def by_core(self, choose):
        both = [choose([axes[core] for axes in self.steps]) for core in range(2)]
        return [jnp.where(self.core == 0, *pair) for pair in zip(*both)]

    def bits(self):
        seq, first, second = self.seq, self.first, self.second

        def one(axes):
            if axes[0] == "y":
                return [seq * 2, seq * 2 + 1, 2 - seq * 2, 3 - seq * 2]
            return [first, 2 + first, 1 - first, 3 - first]

        def two(axes):
            if axes[0] != "y" and axes[1] != "y":
                return [second, 2 + second, 1 - second, 3 - second]
            bit = first if axes[0] == "y" else seq
            return [bit * 2, bit * 2 + 1, 2 - bit * 2, 3 - bit * 2]

        def three(axes):
            bit = seq if axes[2] == "y" else second
            return [bit, 1 - bit]

        def four(axes):
            return [self.zhi, 1 - self.zhi]

        at = self.by_core((one, two, three, four)[self.stage])
        return at[: len(at) // 2], at[len(at) // 2 :]

    def step(self, *others):
        self.kept = after(self.kept, *others)
        keep, send = self.bits()
        self.kept = self.blocks(self.kept, 2 * len(keep))
        if self.stage == 0 and self.inner is not None:
            kept, came = (self.blocks(values, 4) for values in self.inner)
            self.kept, *sent = combine(keep, send, (self.kept, self.came), (kept, came))
            self.came, self.rest = exchange(sent[0], self.steps[0]), sent[1]
            self.stage += 1
            return sent[0]
        if self.stage == 1 and self.halves:
            early, late = (self.blocks(came, 2) for came in self.came)
            self.kept, sent = halve_late(keep, send, self.kept, early, late)
        else:
            split = self.stage == 0 and self.halves
            came = self.blocks(self.came, 2 * len(keep))
            self.kept, sent = halve(keep, send, self.kept, came, split)
            if split:
                self.came, self.rest = exchange(sent[0], self.steps[0]), sent[1]
                self.stage += 1
                return sent[0]
            sent = sent[0]
        if self.stage < 3:
            self.came = exchange(sent, self.steps[self.stage])
        else:
            self.came = swap(sent, "zhi")
        self.stage += 1
        return sent

    def step_rest(self, *others):
        sent = after(self.rest, self.came, *others)
        self.came = (self.came, exchange(sent, self.steps[0]))
        return sent

    def gather(self, *others):
        if self.stage > 4:
            self.part = after(self.part, *others)
        if self.stage == 4:
            piece = self.kept[0].astype(jnp.float32) + self.came[0].astype(jnp.float32)
            self.part = piece.astype(jnp.bfloat16)
            self.came = swap(self.part, "zhi")
        elif self.stage == 5:
            self.part = merge(self.zhi, self.part, self.came)
            self.came = exchange(self.part, self.along[::-1])
        elif self.stage == 6:
            self.part = merge(self.second, self.part, self.came)
            self.came = exchange(self.part, self.along)
        else:
            self.part = merge(self.first, self.part, self.came)
            self.came = swap(self.part, "core")
        self.stage += 1
        return self.part

    def advance(self, *others):
        if self.stage < 4:
            return [self.step(*others)]
        return [self.gather(*others)] if self.stage < 8 else []

    def result(self, count, *others):
        part = after(self.part, *others)
        if self.inner is None:
            return unpack(self.core, part, self.came, count)
        return unpack(self.core, part, self.came, 2, self.tall, self.inner_blocks)


def sum_plain(terms):
    terms = lax.psum_scatter(terms.astype(jnp.bfloat16), "seq", scatter_dimension=0, tiled=True)
    return lax.psum(terms, page_axes)


page_axes = ("zhi", "zlo", "x", "core")


class VectorTotal:
    def __init__(self, values):
        self.values = values
        self.axes = [axis for axis in page_axes + ("seq",) if lax.axis_size(axis) == 2]
        rest = tuple(axis for axis in page_axes + ("seq",) if lax.axis_size(axis) != 2)
        if rest:
            self.values = lax.psum(self.values, rest)
        self.came = swap(self.values, self.axes.pop(0))

    def advance(self, *others):
        if self.came is None:
            return []
        self.values, self.came = after(self.values, *others) + self.came, None
        if self.axes:
            self.came = swap(self.values, self.axes.pop(0))
        return [self.values]

    def result(self):
        while self.came is not None:
            self.advance()
        return self.values


def on_device(
    tokens,
    patches,
    lengths,
    blank_mask,
    cotangent,
    first_gain,
    first_shift,
    self_query,
    self_query_bias,
    self_key,
    self_value,
    self_value_bias,
    self_output,
    self_output_bias,
    second_gain,
    second_shift,
    cross_query,
    cross_query_bias,
    cross_key,
    cross_value,
    cross_value_bias,
    cross_output,
    cross_output_bias,
    third_gain,
    third_shift,
    ffn_inner,
    ffn_inner_bias,
    ffn_outer,
    ffn_outer_bias,
):
    seq_count = lax.axis_size("seq")
    seq_index = lax.axis_index("seq")
    vectors = (
        first_gain,
        first_shift,
        self_query_bias,
        self_value_bias,
        self_output_bias,
        second_gain,
        second_shift,
        cross_query_bias,
        cross_value_bias,
        cross_output_bias,
        third_gain,
        third_shift,
        ffn_inner_bias,
        ffn_outer_bias,
    )
    two = seq_count == 2 and lax.axis_size("zhi") == 2
    joined = jnp.concatenate(vectors).reshape(-1, 128)
    if two:
        joined_other = swap(joined, "seq")
        gathered = jnp.where(
            seq_index == 0,
            jnp.stack([joined, joined_other]),
            jnp.stack([joined_other, joined]),
        )
    else:
        gathered = lax.all_gather(joined, "seq", axis=0, tiled=False)
    gathered = gathered.reshape(seq_count, -1)
    whole_vectors, start = [], 0
    for vector in vectors:
        part = gathered[:, start : start + vector.shape[0]].reshape(-1)
        whole_vectors.append(part.astype(jnp.float32))
        start += vector.shape[0]
    (
        gain_one,
        shift_one,
        bias_self_query,
        bias_self_value,
        bias_self_output,
        gain_two,
        shift_two,
        bias_cross_query,
        bias_cross_value,
        bias_cross_output,
        gain_three,
        shift_three,
        bias_inner,
        bias_outer,
    ) = whole_vectors
    tokens, patches, cotangent = tokens[0], patches[0], cotangent[0]
    tok_rows, width = tokens.shape
    patch_rows = patches.shape[0]
    query_scale = 1.0 / math.sqrt(HEAD)

    core = lax.axis_index("core")
    self_shards = [self_query, self_key, self_value, self_output]
    cross_shards = [cross_key, cross_value, cross_query, cross_output]
    if two:
        pieces = Pieces(first_piece(self_shards))
        pieces.first(joined_other)
        tokens_other = lax.ppermute(after(tokens, pieces.own), "seq", [(0, 1)])
        pieces.second()
        cross_pieces = Pieces(first_piece([after(cross_key, pieces.low)] + cross_shards[1:]))
        pieces.third()
        whole_self = assemble(
            seq_index, pieces.places, self_shards, pieces.parts(tokens_other)
        )
        tokens_all = jnp.concatenate([tokens, after(tokens_other, whole_self)])
    else:
        gather = lambda shard: lax.all_gather(shard, "seq", axis=0, tiled=True)
        whole_self = gather(jnp.concatenate(self_shards, axis=1))
        whole_cross = gather(jnp.concatenate(cross_shards, axis=1))
        whole_ffn_inner, whole_ffn_outer = gather(ffn_inner), gather(ffn_outer)
        tokens_all, patches_all = gather(tokens), gather(patches)

    first_place = seq_index * tok_rows
    key_start = first_place if two else 0
    info = jnp.stack([first_place, lengths[0], key_start, seq_index]).astype(jnp.int32)
    self_plan = Plan(
        ("limit", "earlier") if two else ("limit",),
        tok_rows if two else tok_rows * seq_count,
        tok_rows,
        256,
        two,
    )
    cross_plan = Plan(("bias",), patch_rows * seq_count, tok_rows, 256, False)
    blank_bias = jnp.where(blank_mask[0] == 0, 0.0, masked_score).astype(jnp.float32)
    if two:
        halves = blank_bias.reshape(2, patch_rows)
        blank_bias = jnp.where(seq_index == 0, halves, halves[::-1]).reshape(-1)
    blank_bias = blank_bias[:, None]
    no_bias = jnp.zeros((self_plan.all_rows, 1), jnp.float32)

    zeros = jnp.zeros_like(bias_self_value)
    token_values = tokens.astype(jnp.float32)
    normed_all = layer_norm(tokens_all.astype(jnp.float32), gain_one, shift_one).astype(
        jnp.bfloat16
    )
    if two:
        normed_one = normed_all[:tok_rows]
    else:
        normed_one = layer_norm(token_values, gain_one, shift_one).astype(jnp.bfloat16)
    queries_self = (
        (dot_nn(normed_one, whole_self[:, :width]) + bias_self_query) * query_scale
    ).astype(jnp.bfloat16)
    self_bias = jnp.concatenate([zeros, bias_self_value])
    self_pairs = (dot_nn(normed_all, whole_self[:, width : 3 * width]) + self_bias).astype(
        jnp.bfloat16
    )
    attend_self = functools.partial(attend, self_plan, info)
    if two:
        sent = cross_pieces.first(queries_self)
        patches_other = swap(after(patches, cross_pieces.own), "seq")
        mixed_self, log_self = attend_self(
            after(queries_self, *sent), self_pairs, no_bias, 0, 1
        )
        mixed_self = after(mixed_self, patches_other, *cross_pieces.second())
        inner_pieces = Pieces(first_piece([after(ffn_inner, patches_other)]))
    else:
        mixed_self, log_self = attend_self(queries_self, self_pairs, no_bias, 0, 1)
    hidden_one = token_values + dot_nn(mixed_self, whole_self[:, 3 * width :]) + bias_self_output
    normed_two = layer_norm(hidden_one, gain_two, shift_two).astype(jnp.bfloat16)
    if two:
        cross_pieces.third()
        whole_cross = assemble(
            seq_index, cross_pieces.places, cross_shards, cross_pieces.parts(normed_two)
        )
        patches_all = jnp.concatenate([patches, patches_other])
        patches_all = after(patches_all, whole_cross, inner_pieces.own)
        outer_pieces = Pieces(first_piece([after(ffn_outer, inner_pieces.own)]))
    patch_bias = jnp.concatenate([zeros, bias_cross_value])
    patch_pairs = (dot_nn(patches_all, whole_cross[:, : 2 * width]) + patch_bias).astype(
        jnp.bfloat16
    )
    queries_cross = (
        (dot_nn(normed_two, whole_cross[:, 2 * width : 3 * width]) + bias_cross_query) * query_scale
    ).astype(jnp.bfloat16)
    attend_cross = functools.partial(attend, cross_plan, info)
    if two:
        keys = (patch_pairs, blank_bias)
        sent = inner_pieces.first(queries_cross) + (outer_pieces.own,)
        done = attend_cross(after(queries_cross, *sent), *keys, 0, 2)
        sent = inner_pieces.second() + outer_pieces.first()
        sent = [after(values, done[0]) for values in sent]
        inner_pieces.both, inner_pieces.core_low, inner_pieces.core_high = sent[:3]
        outer_pieces.low, outer_pieces.high, outer_pieces.core = sent[3:]
        inner_pieces.third()
        outer_pieces.second()
        done = attend_cross(after(queries_cross, *sent), *keys, 1, 2, done)
        late = [after(values, done[0]) for values in (outer_pieces.both, inner_pieces.core_both)]
        outer_pieces.both, inner_pieces.core_both = late
        inner_other = join(inner_pieces.places, inner_pieces.parts(done[0]))
        mixed_cross, log_cross = done
        outer_pieces.third()
        mixed_cross = after(mixed_cross, inner_other)
    else:
        mixed_cross, log_cross = attend_cross(queries_cross, patch_pairs, blank_bias, 0, 1)
    hidden_two = hidden_one + dot_nn(mixed_cross, whole_cross[:, 3 * width :]) + bias_cross_output
    normed_three = layer_norm(hidden_two, gain_three, shift_three).astype(jnp.bfloat16)
    if two:
        outer_other = join(outer_pieces.places, outer_pieces.parts(normed_three))
        outputs, grad_normed_three, column_inner, split_outer, split_inner = ffn_both_ways(
            seq_index,
            core,
            normed_three,
            hidden_two,
            cotangent,
            ffn_inner,
            inner_other,
            ffn_outer,
            outer_other,
            bias_inner,
            bias_outer,
        )
        total_ffn = Total(split_outer, ("xy", "yz", "zx"), True, True, split_inner)
    else:
        inner_sum = dot_nn(normed_three, whole_ffn_inner) + bias_inner
        active = jax.nn.gelu(inner_sum, approximate=False).astype(jnp.bfloat16)
        outputs = (hidden_two + dot_nn(active, whole_ffn_outer) + bias_outer).astype(jnp.bfloat16)
        grad_active = dot_back(cotangent, whole_ffn_outer)
        gelu_pull = jax.vjp(lambda u: jax.nn.gelu(u, approximate=False), inner_sum)[1]
        grad_inner = gelu_pull(grad_active)[0].astype(jnp.bfloat16)
        column_inner = column_sum(grad_inner)
        grad_normed_three = dot_back(grad_inner, whole_ffn_inner)
    back_two = layer_norm_back(hidden_two, gain_three, grad_normed_three)
    grad_hidden_two = cotangent.astype(jnp.float32) + back_two
    branch_cross = grad_hidden_two.astype(jnp.bfloat16)
    grad_mixed_cross = dot_back(branch_cross, whole_cross[:, 3 * width :]).astype(jnp.bfloat16)
    back_cross = functools.partial(
        attend_back, cross_plan, info, queries_cross, mixed_cross
    )
    cross_rest = (log_cross, patch_pairs, blank_bias)
    if two:
        sent = total_ffn.step(grad_mixed_cross)
        cross_back = back_cross(after(grad_mixed_cross, sent), *cross_rest, 0, 1)
    else:
        cross_back = back_cross(grad_mixed_cross, *cross_rest, 0, 1)
    scaled_cross, grad_patch_keys, grad_patch_values = cross_back
    cross_products = [
        (normed_two, scaled_cross),
        (patches_all, grad_patch_keys),
        (patches_all, grad_patch_values),
        (mixed_cross, branch_cross),
    ]
    if two:
        scaled_cross = after(scaled_cross, total_ffn.step_rest(scaled_cross))
    grad_normed_two = dot_back(scaled_cross, whole_cross[:, 2 * width : 3 * width])
    back_one = layer_norm_back(hidden_one, gain_two, grad_normed_two)
    grad_hidden_one = grad_hidden_two + back_one
    branch_self = grad_hidden_one.astype(jnp.bfloat16)
    grad_mixed_self = dot_back(branch_self, whole_self[:, 3 * width :]).astype(jnp.bfloat16)
    back_self = functools.partial(attend_back, self_plan, info, queries_self, mixed_self)
    self_rest = (log_self, self_pairs, no_bias)
    if two:
        products = [
            (0, scaled_cross),
            (1, grad_patch_keys),
            (1, grad_patch_values),
            (2, branch_cross),
            (3, branch_self),
        ]
        lefts = [after(normed_two, grad_mixed_self), patches_all, mixed_cross, mixed_self]
        kept, sent = outer_group(core, lefts, products)
        late = total_ffn.step(kept)
        total_mid = Total((kept, after(sent, late)), ("zx", "yz", "xy"), False, True)
        sent = total_mid.step(late)
        self_back = back_self(after(grad_mixed_self, sent), *self_rest, 0, 1)
    else:
        self_back = back_self(grad_mixed_self, *self_rest, 0, 1)
    scaled_self, grad_keys, grad_values = self_back
    self_products = [
        (normed_one, scaled_self),
        (normed_all, grad_keys),
        (normed_all, grad_values),
        (mixed_self, branch_self),
    ]
    if two:
        late = (total_ffn.step(scaled_self), total_mid.step_rest(scaled_self))
        products = [(0, scaled_self), (1, grad_keys), (1, grad_values)]
        lefts = [after(normed_one, *late), normed_all]
        kept, sent = outer_group(core, lefts, products)
        late = (total_ffn.step(kept), total_mid.step(kept))
        total_last = Total((kept, after(sent, *late)), ("yz", "xy", "zx"), True, False)
        grad_keys, scaled_self = (after(values, *late) for values in (grad_keys, scaled_self))
    normed_terms = dot_back(grad_keys, whole_self[:, width : 2 * width]) + dot_back(
        grad_values, whole_self[:, 2 * width : 3 * width]
    )
    if two:
        sent = total_last.advance(normed_terms)
        for total in (total_mid, total_ffn):
            sent = sent + total.advance(sent[0])
        grad_patch_keys = after(grad_patch_keys, *sent)
    patch_terms = dot_back(grad_patch_keys, whole_cross[:, :width]) + dot_back(
        grad_patch_values, whole_cross[:, width : 2 * width]
    )
    if two:
        normed_sent = normed_terms[tok_rows:].astype(jnp.bfloat16)
        normed_came = lax.ppermute(normed_sent, "seq", [(1, 0)])
        grad_normed = normed_terms[:tok_rows] + normed_came.astype(jnp.float32)
        patch_sent = patch_terms[patch_rows:].astype(jnp.bfloat16)
        grad_patches = patch_terms[:patch_rows] + swap(patch_sent, "seq").astype(jnp.float32)
    else:
        grad_patches, grad_normed = (
            lax.psum_scatter(
                terms.astype(jnp.bfloat16), "seq", scatter_dimension=0, tiled=True
            ).astype(jnp.float32)
            for terms in (patch_terms, normed_terms)
        )
    grad_normed = grad_normed + dot_back(scaled_self, whole_self[:, :width])
    grad_tokens = grad_hidden_one + layer_norm_back(token_values, gain_one, grad_normed)
    norm_pairs = (
        (token_values, grad_normed),
        (hidden_one, grad_normed_two),
        (hidden_two, grad_normed_three),
    )
    plain = (
        scaled_self,
        grad_values,
        branch_self,
        scaled_cross,
        grad_patch_values,
        branch_cross,
        cotangent,
    )
    if two:
        late = total_last.advance(patch_terms)
        for total in (total_mid, total_ffn):
            late = late + total.advance(late[0])
        norm_pairs = ((after(token_values, *late), grad_normed),) + norm_pairs[1:]
    sums = row_sums(norm_pairs, plain)
    vector_sums = jnp.concatenate([sums, column_inner.reshape(-1, width)])
    if two:
        totals = (total_mid, total_ffn, total_last)
        late = [vector_sums]
        while any(total.stage < 8 for total in totals):
            ahead = total_last.advance(*late)
            late = ahead
            for total in totals[:-1]:
                late = late + total.advance(*ahead)
        vector_total = VectorTotal(after(vector_sums, *late))
        grad_outer, grad_ffn_in = total_ffn.result(2, *late)
        late = vector_total.advance(grad_outer)
        *wide_cross, wide_output = total_mid.result(5, *late)
        late = vector_total.advance(wide_output)
        wide_self = [*total_last.result(3, *late), wide_output]
    else:
        grad_outer = sum_plain(dot_tn(active, cotangent)).astype(jnp.float32)
        grad_ffn_in = sum_plain(dot_tn(normed_three, grad_inner)).astype(jnp.float32)
        wide_cross = [
            sum_plain(dot_tn(*product)).astype(jnp.float32) for product in cross_products
        ]
        wide_self = [sum_plain(dot_tn(*product)).astype(jnp.float32) for product in self_products]
        vector_total = VectorTotal(vector_sums)
    sums = vector_total.result()
    small_width = width // seq_count
    own_sums = lax.dynamic_slice_in_dim(sums[:-4], seq_index * small_width, small_width, axis=1)
    inner_rows = sums[-(column_inner.shape[0] // width) :].reshape(-1)
    inner_width = column_inner.shape[0] // seq_count
    own_inner = lax.dynamic_slice_in_dim(inner_rows, seq_index * inner_width, inner_width, axis=0)
    order = (0, 1, 6, 7, 8, 2, 3, 9, 10, 11, 4, 5, None, 12)
    small = [own_inner if at is None else own_sums[at] for at in order]
    totals = (
        small[0],
        small[1],
        wide_self[0],
        small[2],
        wide_self[1],
        wide_self[2],
        small[3],
        wide_self[3],
        small[4],
        small[5],
        small[6],
        wide_cross[0],
        small[7],
        wide_cross[1],
        wide_cross[2],
        small[8],
        wide_cross[3],
        small[9],
        small[10],
        small[11],
        grad_ffn_in,
        small[12],
        grad_outer,
        small[13],
    )
    return (outputs[None], grad_tokens[None], grad_patches[None]) + totals


def solution(mesh):
    page_count, seq_count = mesh.devices.shape
    mesh = Mesh(
        mesh.devices.reshape(page_count // 8, 2, 2, 2, seq_count),
        ("zhi", "zlo", "x", "core", "seq"),
    )
    page = ("zhi", "zlo", "x", "core")
    pages = P(page, "seq", None)
    rows, vector = P("seq", None), P("seq")
    layer = (
        (vector, vector)
        + (rows, vector, rows, rows, vector, rows, vector)
        + (vector, vector)
        + (rows, vector, rows, rows, vector, rows, vector)
        + (vector, vector)
        + (rows, vector, rows, vector)
    )
    return jax.shard_map(
        on_device,
        mesh=mesh,
        in_specs=(pages, pages, P(page), P(page, None), pages) + layer,
        out_specs=(pages, pages, pages) + layer,
        check_vma=False,
    )
```

```python
import functools
import math

import jax
import jax.numpy as jnp
from jax import lax
from jax.experimental import pallas as pl
from jax.experimental.pallas import tpu as pltpu
from jax.sharding import Mesh
from jax.sharding import PartitionSpec as P

HEADS = 16
HEAD = 64


norm_epsilon = 1e-05
masked_score = -1000000000.0


def layer_norm(values, norm_gain, norm_shift):
    center = values - jnp.mean(values, axis=-1, keepdims=True)
    spread = jnp.mean(center * center, axis=-1, keepdims=True)
    return center * lax.rsqrt(spread + norm_epsilon) * norm_gain + norm_shift


pair_width = 2 * HEAD
vmem_bytes = 60 * 1024 * 1024
light = pl.CostEstimate(flops=1, bytes_accessed=1, transcendentals=0)


def dot_nt(left_side, right_side):
    return lax.dot_general(
        left_side, right_side, (((1,), (1,)), ((), ())), preferred_element_type=jnp.float32
    )


def dot_nn(left_side, right_side):
    return jnp.dot(left_side, right_side, preferred_element_type=jnp.float32)


def dot_tn(left_side, right_side):
    return lax.dot_general(
        left_side, right_side, (((0,), (0,)), ((), ())), preferred_element_type=jnp.float32
    )


def one_head(values, head):
    lane = lax.broadcasted_iota(jnp.int32, values.shape, 1)
    return jnp.where((lane >= head * HEAD) & (lane < (head + 1) * HEAD), values, 0)


class Plan:
    def __init__(self, kinds, key_rows, query_rows, chunk, causal):
        self.kinds = kinds
        self.key_rows = key_rows
        self.all_rows = key_rows * len(kinds)
        self.query_rows = query_rows
        self.chunk = min(chunk, query_rows)
        self.causal = causal

    def blocks(self, start, segments):
        found = []
        for segment in segments:
            rows = self.key_rows
            if self.causal and self.kinds[segment] == "limit":
                rows = min(rows, start + self.chunk)
            found.append((self.kinds[segment], pl.ds(segment * self.key_rows, rows)))
        return found


def query_limit(info_ref, start, chunk):
    lane = lax.broadcasted_iota(jnp.int32, (1, chunk), 1) + start
    place = info_ref[0] + lane
    return jnp.minimum(place, info_ref[1] - 1) - info_ref[2]


def masked_block(kind, scores, limit, bias_ref):
    if kind == "limit":
        key = lax.broadcasted_iota(jnp.int32, scores.shape, 0)
        return jnp.where(key <= limit, scores, masked_score)
    if kind == "bias":
        return scores + bias_ref[...]
    return scores


def run_segments(plan, info_ref, body):
    every = list(range(len(plan.kinds)))
    needed = [segment for segment in every if plan.kinds[segment] != "earlier"]
    if len(needed) == len(every):
        body(every)
        return
    pl.when(info_ref[3] == 1)(lambda: body(every))
    pl.when(info_ref[3] != 1)(lambda: body(needed))


def attend_kernel(plan, info_ref, query_ref, key_ref, value_ref, bias_ref, mixed_ref, log_ref):
    def body(segments):
        for start in range(0, plan.query_rows, plan.chunk):
            limit = query_limit(info_ref, start, plan.chunk)
            lane = lax.broadcasted_iota(jnp.int32, (1, plan.chunk), 1) + start
            valid = (info_ref[0] + lane < info_ref[1]).astype(jnp.float32)
            query = query_ref[pl.ds(start, plan.chunk), :]
            parts = []
            for head in range(2):
                head_query = one_head(query, head)
                blocks = plan.blocks(start, segments)
                scores = [
                    masked_block(kind, dot_nt(key_ref[rows, :], head_query), limit, bias_ref)
                    for kind, rows in blocks
                ]
                peak = jnp.max(scores[0], axis=0, keepdims=True)
                for block in scores[1:]:
                    peak = jnp.maximum(peak, jnp.max(block, axis=0, keepdims=True))
                total = jnp.zeros_like(peak)
                mixed = jnp.zeros((pair_width, plan.chunk), jnp.float32)
                for (kind, rows), block in zip(blocks, scores):
                    weights = jnp.exp(block - peak)
                    total = total + jnp.sum(weights, axis=0, keepdims=True)
                    mixed = mixed + dot_tn(value_ref[rows, :], weights.astype(jnp.bfloat16))
                parts.append(mixed[head * HEAD : (head + 1) * HEAD] * (valid / total))
                log_ref[0, pl.ds(head, 1), pl.ds(start, plan.chunk)] = peak + jnp.log(total)
            joined = jnp.concatenate(parts, axis=0)
            mixed_ref[pl.ds(start, plan.chunk), :] = joined.T.astype(jnp.bfloat16)

    run_segments(plan, info_ref, body)


def attend_back_kernel(
    plan,
    info_ref,
    query_ref,
    mixed_ref,
    grad_ref,
    log_ref,
    key_ref,
    value_ref,
    bias_ref,
    grad_query_ref,
    grad_key_ref,
    grad_value_ref,
    key_sum,
    value_sum,
):
    def body(segments):
        key_sum[...] = jnp.zeros_like(key_sum)
        value_sum[...] = jnp.zeros_like(value_sum)
        for start in range(0, plan.query_rows, plan.chunk):
            limit = query_limit(info_ref, start, plan.chunk)
            rows_here = pl.ds(start, plan.chunk)
            row = lax.broadcasted_iota(jnp.int32, (plan.chunk, 1), 0) + start
            valid = info_ref[0] + row < info_ref[1]
            query = query_ref[rows_here, :]
            grad = jnp.where(valid, grad_ref[rows_here, :], 0).astype(jnp.bfloat16)
            product = grad.astype(jnp.float32) * mixed_ref[rows_here, :].astype(jnp.float32)
            product = product.T
            parts = []
            for head in range(2):
                own = slice(head * HEAD, (head + 1) * HEAD)
                head_query, head_grad = one_head(query, head), one_head(grad, head)
                weighted = jnp.sum(product[own], axis=0, keepdims=True)
                log_total = log_ref[0, pl.ds(head, 1), rows_here]
                grad_query = jnp.zeros((pair_width, plan.chunk), jnp.float32)
                for kind, rows in plan.blocks(start, segments):
                    keys = key_ref[rows, :]
                    scores = masked_block(kind, dot_nt(keys, head_query), limit, bias_ref)
                    shares = jnp.exp(scores - log_total)
                    grad_shares = dot_nt(value_ref[rows, :], head_grad)
                    grad_scores = (shares * (grad_shares - weighted)).astype(jnp.bfloat16)
                    value_sum[rows, :] += dot_nn(shares.astype(jnp.bfloat16), head_grad)
                    key_sum[rows, :] += dot_nn(grad_scores, head_query)
                    grad_query = grad_query + dot_tn(keys, grad_scores)
                parts.append(grad_query[own])
            joined = jnp.concatenate(parts, axis=0) * (1.0 / math.sqrt(HEAD))
            grad_query_ref[rows_here, :] = joined.T.astype(jnp.bfloat16)
        grad_key_ref[...] = key_sum[...].astype(jnp.bfloat16)
        grad_value_ref[...] = value_sum[...].astype(jnp.bfloat16)

    run_segments(plan, info_ref, body)


def column_block(rows, first):
    return pl.BlockSpec((rows, pair_width), lambda step, info: (0, first + step))


def log_block(rows, first):
    return pl.BlockSpec((1, 2, rows), lambda step, info: (first + step, 0, 0))


def key_specs(plan, first):
    return [
        column_block(plan.all_rows, first),
        column_block(plan.all_rows, HEADS // 2 + first),
        pl.BlockSpec((plan.all_rows, 1), lambda step, info: (0, 0)),
    ]


any_block = pl.BlockSpec(memory_space=pl.ANY)


def skip_refs(kernel, place, count):
    def run(*refs):
        kernel(*refs[:place], *refs[place + count :])

    return run


def attend(plan, info, queries, key_values, bias, part, parts, into=()):
    pairs = HEADS // 2
    count, first = pairs // parts, part * (pairs // parts)
    rows, keys = plan.query_rows, plan.all_rows
    return pl.pallas_call(
        skip_refs(functools.partial(attend_kernel, plan), 5, len(into)),
        grid_spec=pltpu.PrefetchScalarGridSpec(
            num_scalar_prefetch=1,
            grid=(count,),
            in_specs=[column_block(rows, first)] + key_specs(plan, first) + [any_block] * len(into),
            out_specs=[column_block(rows, first), log_block(rows, first)],
        ),
        out_shape=[
            jax.ShapeDtypeStruct((rows, HEADS * HEAD), jnp.bfloat16),
            jax.ShapeDtypeStruct((pairs, 2, rows), jnp.float32),
        ],
        input_output_aliases={5 + index: index for index in range(len(into))},
        compiler_params=pltpu.CompilerParams(vmem_limit_bytes=vmem_bytes),
        cost_estimate=light,
    )(info, queries, key_values, key_values, bias, *into)


def attend_back(
    plan, info, queries, mixed, grad_mixed, log_total, key_values, bias, part, parts, into=()
):
    pairs = HEADS // 2
    count, first = pairs // parts, part * (pairs // parts)
    rows, keys = plan.query_rows, plan.all_rows
    return pl.pallas_call(
        skip_refs(functools.partial(attend_back_kernel, plan), 8, len(into)),
        grid_spec=pltpu.PrefetchScalarGridSpec(
            num_scalar_prefetch=1,
            grid=(count,),
            in_specs=[column_block(rows, first)] * 3
            + [log_block(rows, first)]
            + key_specs(plan, first)
            + [any_block] * len(into),
            out_specs=[
                column_block(rows, first),
                column_block(keys, first),
                column_block(keys, first),
            ],
            scratch_shapes=[pltpu.VMEM((keys, pair_width), jnp.float32)] * 2,
        ),
        out_shape=[
            jax.ShapeDtypeStruct((rows, HEADS * HEAD), jnp.bfloat16),
            jax.ShapeDtypeStruct((keys, HEADS * HEAD), jnp.bfloat16),
            jax.ShapeDtypeStruct((keys, HEADS * HEAD), jnp.bfloat16),
        ],
        input_output_aliases={8 + index: index for index in range(len(into))},
        compiler_params=pltpu.CompilerParams(vmem_limit_bytes=vmem_bytes),
        cost_estimate=light,
    )(info, queries, mixed, grad_mixed, log_total, key_values, key_values, bias, *into)


def join_kernel(count, place_ref, *refs):
    out_ref = refs[count]
    for index, source in enumerate(refs[:count]):
        rows = source.shape[0]
        first = pl.multiple_of(place_ref[index] * rows, rows)
        out_ref[pl.ds(first, rows), :] = source[...]


def join(places, parts):
    count, (rows, width) = len(parts), parts[0].shape
    steps = 1 if count * rows * width <= 1024 * 1024 else 4
    wide = width // steps
    return pl.pallas_call(
        functools.partial(join_kernel, count),
        grid_spec=pltpu.PrefetchScalarGridSpec(
            num_scalar_prefetch=1,
            grid=(steps,),
            in_specs=[pl.BlockSpec((rows, wide), lambda i, place: (0, i))] * count,
            out_specs=pl.BlockSpec((count * rows, wide), lambda i, place: (0, i)),
        ),
        out_shape=jax.ShapeDtypeStruct((count * rows, width), parts[0].dtype),
        compiler_params=pltpu.CompilerParams(vmem_limit_bytes=vmem_bytes),
        cost_estimate=light,
    )(jnp.stack(places).astype(jnp.int32), *parts)


def merge(index, own, other):
    return join([index, 1 - index], [own, other])


def assemble_kernel(count, place_ref, *refs):
    shards, parts, out_ref = refs[:count], refs[count:-1], refs[-1]
    for index, part in enumerate(parts):
        rows = part.shape[0]
        first = pl.multiple_of(place_ref[1 + index] * rows, rows)
        out_ref[pl.ds(first, rows), :] = part[...]
    for index, shard in enumerate(shards):

        def store(shard=shard):
            rows = shard.shape[0]
            first = pl.multiple_of(place_ref[0] * rows, rows)
            out_ref[pl.ds(first, rows), :] = shard[...]

        pl.when(pl.program_id(0) == index)(store)


def assemble(seq, places, shards, parts):
    count, (rows, wide) = len(shards), shards[0].shape
    part_rows = parts[0].shape[0]
    places = [seq] + [(1 - seq) * len(parts) + place for place in places]
    return pl.pallas_call(
        functools.partial(assemble_kernel, count),
        grid_spec=pltpu.PrefetchScalarGridSpec(
            num_scalar_prefetch=1,
            grid=(count,),
            in_specs=[pl.BlockSpec((rows, wide), lambda i, place: (0, 0))] * count
            + [pl.BlockSpec((part_rows, wide), lambda i, place: (0, i))] * len(parts),
            out_specs=pl.BlockSpec((2 * rows, wide), lambda i, place: (0, i)),
        ),
        out_shape=jax.ShapeDtypeStruct((2 * rows, count * wide), shards[0].dtype),
        compiler_params=pltpu.CompilerParams(vmem_limit_bytes=vmem_bytes),
        cost_estimate=light,
    )(jnp.stack(places).astype(jnp.int32), *shards, *parts)


def row_sums_kernel(norms, plain, *refs):
    steps = refs[: 2 * norms + plain]
    out_ref = refs[-1]

    @pl.when(pl.program_id(0) == 0)
    def start():
        out_ref[...] = jnp.zeros_like(out_ref)

    for index in range(norms):
        values, grad = steps[2 * index][...].astype(jnp.float32), steps[2 * index + 1][...]
        center = values - jnp.mean(values, axis=-1, keepdims=True)
        spread = jnp.mean(center * center, axis=-1, keepdims=True)
        unit = center * lax.rsqrt(spread + norm_epsilon)
        out_ref[pl.ds(2 * index, 1), :] += jnp.sum(grad * unit, axis=0, keepdims=True)
        out_ref[pl.ds(2 * index + 1, 1), :] += jnp.sum(grad, axis=0, keepdims=True)
    for index in range(plain):
        values = steps[2 * norms + index][...].astype(jnp.float32)
        at = pl.ds(2 * norms + index, 1)
        out_ref[at, :] += jnp.sum(values, axis=0, keepdims=True)


def row_sums(norm_pairs, plain):
    arrays = [values for pair in norm_pairs for values in pair] + list(plain)
    width = arrays[0].shape[1]
    rows = -(-(2 * len(norm_pairs) + len(plain)) // 8) * 8
    return pl.pallas_call(
        functools.partial(row_sums_kernel, len(norm_pairs), len(plain)),
        grid=(4,),
        in_specs=[
            pl.BlockSpec((values.shape[0] // 4, width), lambda step: (step, 0)) for values in arrays
        ],
        out_specs=pl.BlockSpec((rows, width), lambda step: (0, 0)),
        out_shape=jax.ShapeDtypeStruct((rows, width), jnp.float32),
        compiler_params=pltpu.CompilerParams(vmem_limit_bytes=vmem_bytes),
        cost_estimate=light,
    )(*arrays)


def ffn_kernel(half_steps, place_ref, *refs):
    normed, inner = refs[0:4], refs[4:8]
    outer_own, outer_other, bias_ref, bias_outer_ref, hidden_ref, cotangent_ref = refs[8:14]
    out_ref, grad_ref, column_ref, kept_outer, sent_outer, kept_inner, sent_inner = refs[14:21]
    total_ref, turned_ref = refs[21], refs[22]
    grad_sums = refs[23:27]
    step = pl.program_id(0)
    quarter = normed[0].shape[1]

    @pl.when(step == 0)
    def start():
        for index in range(4):
            turned_ref[index] = normed[index][...].T
            grad_sums[index][...] = jnp.zeros_like(grad_sums[index])
        total_ref[...] = hidden_ref[...] + bias_outer_ref[...]

    def run(outer_ref):
        inner_sum = bias_ref[...] + dot_nn(normed[0][...], inner[0][...])
        for index in range(1, 4):
            inner_sum = inner_sum + dot_nn(normed[index][...], inner[index][...])
        part = 0.5 + 0.5 * lax.erf(inner_sum * math.sqrt(0.5))
        active = (inner_sum * part).astype(jnp.bfloat16)
        slope = part + inner_sum * (
            jnp.exp(-0.5 * inner_sum * inner_sum) * (1.0 / math.sqrt(2.0 * math.pi))
        )
        cotangent = cotangent_ref[...]
        total_ref[...] += dot_nn(active, outer_ref[...])
        grad_inner = (dot_nt(cotangent, outer_ref[...]) * slope).astype(jnp.bfloat16)
        column_ref[...] = jnp.sum(grad_inner.astype(jnp.float32), axis=0, keepdims=True)
        for index in range(4):
            grad_sums[index][...] += dot_nt(grad_inner, inner[index][...])
        grad_outer = dot_tn(active, cotangent).astype(jnp.bfloat16)
        for which, out in ((0, kept_outer), (1, sent_outer)):

            def store(out=out):
                out[0] = grad_outer

            pl.when(step % 2 == which)(store)
        for index, (out, seq_at) in enumerate(
            ((kept_inner, 0), (sent_inner, 0), (kept_inner, 1), (sent_inner, 1))
        ):
            out[pl.ds(place_ref[seq_at], 1)] = dot_nn(turned_ref[index], grad_inner).astype(
                jnp.bfloat16
            )[None]

    pl.when(step < half_steps)(lambda: run(outer_own))
    pl.when(step >= half_steps)(lambda: run(outer_other))

    @pl.when(step == 2 * half_steps - 1)
    def finish():
        out_ref[...] = total_ref[...].astype(jnp.bfloat16)
        for index in range(4):
            first = pl.multiple_of(place_ref[4 + index] * quarter, quarter)
            grad_ref[:, pl.ds(first, quarter)] = grad_sums[index][...]


def ffn_both_ways(
    seq, core, normed, hidden, cotangent, inner_own, inner_other, outer_own, outer_other, bias, last
):
    rows, width = normed.shape
    units = inner_own.shape[1]
    chunk, quarter = units // 4, width // 4
    steps = units // chunk
    half_steps = steps // 2
    run = half_steps // 2
    order = []
    for step in range(steps):
        which, at = (seq, step) if step < half_steps else (1 - seq, step - half_steps)
        side = core if at % 2 == 0 else 1 - core
        order.append((which, side * run + at // 2))
    local = [at for _, at in order]
    whole = [which * half_steps + at for which, at in order]
    out_at = [which * run + step % half_steps // 2 for step, (which, _) in enumerate(order)]
    quarters = [seq * 2 + core, seq * 2 + 1 - core, (1 - seq) * 2 + core, (1 - seq) * 2 + 1 - core]
    place = jnp.stack(
        [seq, 1 - seq, core, 1 - core] + quarters + whole + local + out_at
    ).astype(jnp.int32)
    at_whole, at_local, at_out = 8, 8 + steps, 8 + 2 * steps
    fixed = lambda shape: pl.BlockSpec(shape, lambda step, place: (0,) * len(shape))
    normed_specs = [
        pl.BlockSpec((rows, quarter), lambda step, place, i=i: (0, place[4 + i])) for i in range(4)
    ]
    inner_specs = [
        pl.BlockSpec(
            (quarter, chunk), lambda step, place, i=i: (place[2 + i % 2], place[at_whole + step])
        )
        for i in range(4)
    ]
    own_at = lambda step, place: place[at_local + jnp.minimum(step, half_steps - 1)]
    other_at = lambda step, place: place[at_local + jnp.maximum(step, half_steps)]
    outer_shape = jax.ShapeDtypeStruct((2 * run, chunk, width), jnp.bfloat16)
    inner_shape = jax.ShapeDtypeStruct((2, quarter, units), jnp.bfloat16)
    outer_spec = pl.BlockSpec((1, chunk, width), lambda step, place: (place[at_out + step], 0, 0))
    inner_spec = pl.BlockSpec(
        (2, quarter, chunk), lambda step, place: (0, 0, place[at_whole + step])
    )
    row_spec = pl.BlockSpec((1, chunk), lambda step, place: (0, place[at_whole + step]))
    out, grad, column, kept_outer, sent_outer, kept_inner, sent_inner = pl.pallas_call(
        functools.partial(ffn_kernel, half_steps),
        grid_spec=pltpu.PrefetchScalarGridSpec(
            num_scalar_prefetch=1,
            grid=(steps,),
            in_specs=normed_specs
            + inner_specs
            + [
                pl.BlockSpec((chunk, width), lambda step, place: (own_at(step, place), 0)),
                pl.BlockSpec((chunk, width), lambda step, place: (other_at(step, place), 0)),
                row_spec,
                fixed((1, width)),
                fixed((rows, width)),
                fixed((rows, width)),
            ],
            out_specs=[
                fixed((rows, width)),
                fixed((rows, width)),
                row_spec,
                outer_spec,
                outer_spec,
                inner_spec,
                inner_spec,
            ],
            scratch_shapes=[
                pltpu.VMEM((rows, width), jnp.float32),
                pltpu.VMEM((4, quarter, rows), jnp.bfloat16),
            ]
            + [pltpu.VMEM((rows, quarter), jnp.float32)] * 4,
        ),
        out_shape=[
            jax.ShapeDtypeStruct((rows, width), jnp.bfloat16),
            jax.ShapeDtypeStruct((rows, width), jnp.float32),
            jax.ShapeDtypeStruct((1, units), jnp.float32),
            outer_shape,
            outer_shape,
            inner_shape,
            inner_shape,
        ],
        compiler_params=pltpu.CompilerParams(vmem_limit_bytes=vmem_bytes),
        cost_estimate=light,
    )(
        place,
        *[normed] * 4,
        inner_own,
        inner_own,
        inner_other,
        inner_other,
        outer_own,
        outer_other,
        bias[None],
        last[None],
        hidden,
        cotangent,
    )
    split = lambda kept, sent: (kept.reshape(2, -1, kept.shape[2]), sent.reshape(2, -1, kept.shape[2]))
    return out, grad, column[0], split(kept_outer, sent_outer), (kept_inner, sent_inner)


def outer_group_kernel(products, count, place_ref, *refs):
    lefts, rights = refs[:count], refs[count : count + len(products)]
    kept_ref, sent_ref, turned_ref = refs[count + len(products) :]
    part = kept_ref.shape[1]
    step = pl.program_id(0)
    sides = [side for side, _ in products]
    start = 0
    for index, (side, blocks) in enumerate(products):
        left, right = lefts[side], rights[index]
        tokens = pl.ds(0, left.shape[0])
        if sides.index(side) == index:

            def turn(left=left, tokens=tokens):
                turned_ref[:, tokens] = left[...].T

            pl.when(step == start)(turn)

        def run(right=right, tokens=tokens):
            for seq in range(2):
                for which, out_ref in ((0, kept_ref), (1, sent_ref)):
                    first = pl.multiple_of((seq * 2 + place_ref[which]) * part, part)
                    rows = turned_ref[pl.ds(first, part), tokens]
                    out_ref[seq] = dot_nn(rows, right[...]).astype(jnp.bfloat16)

        pl.when((step >= start) & (step < start + blocks))(run)
        start += blocks


def outer_group(core, lefts, products):
    chunk = 512
    width = lefts[0].shape[1]
    part = width // 4
    tokens = max(left.shape[0] for left in lefts)
    specs, start = [], 0
    for _, right in products:
        blocks = right.shape[1] // chunk
        specs.append(
            pl.BlockSpec(
                (right.shape[0], chunk),
                lambda step, place, start=start, blocks=blocks: (
                    0,
                    jnp.clip(step - start, 0, blocks - 1),
                ),
            )
        )
        start += blocks
    out_spec = pl.BlockSpec((2, part, chunk), lambda step, place: (0, 0, step))
    shape = jax.ShapeDtypeStruct((2, part, start * chunk), jnp.bfloat16)
    kinds = [(side, right.shape[1] // chunk) for side, right in products]
    return pl.pallas_call(
        functools.partial(outer_group_kernel, kinds, len(lefts)),
        grid_spec=pltpu.PrefetchScalarGridSpec(
            num_scalar_prefetch=1,
            grid=(start,),
            in_specs=[pl.BlockSpec(left.shape, lambda step, place: (0, 0)) for left in lefts]
            + specs,
            out_specs=[out_spec, out_spec],
            scratch_shapes=[pltpu.VMEM((width, tokens), jnp.bfloat16)],
        ),
        out_shape=[shape, shape],
        compiler_params=pltpu.CompilerParams(vmem_limit_bytes=vmem_bytes),
        cost_estimate=light,
    )(
        jnp.stack([core, 1 - core]).astype(jnp.int32),
        *lefts,
        *[right for _, right in products],
    )


def halve_kernel(split, place_ref, kept_a, came_a, kept_b, came_b, kept_ref, *sent_refs):
    add = lambda kept, came: (kept[0].astype(jnp.float32) + came[0].astype(jnp.float32)).astype(
        jnp.bfloat16
    )
    kept_ref[0] = add(kept_a, came_a)
    if not split:
        sent_refs[0][0] = add(kept_b, came_b)
        return

    for index, sent_ref in enumerate(sent_refs):

        def store(sent_ref=sent_ref):
            sent_ref[0] = add(kept_b, came_b)

        pl.when(pl.program_id(0) == index)(store)


def halve(keep_at, send_at, kept, came, split=False):
    blocks, rows, width = kept.shape
    count = len(keep_at)
    place = jnp.stack(list(keep_at) + list(send_at)).astype(jnp.int32)
    tiles = 2 if rows * width >= 256 * 1024 else 1
    wide = width // tiles
    spec = lambda first: pl.BlockSpec(
        (1, rows, wide), lambda j, i, place: (place[first + j], 0, i)
    )
    out_spec = pl.BlockSpec((1, rows, wide), lambda j, i, place: (j, 0, i))
    one_spec = lambda at: pl.BlockSpec(
        (1, rows, wide),
        lambda j, i, place: (0, 0, jnp.where(j == at, i, jnp.where(j > at, tiles - 1, 0))),
    )
    shape = jax.ShapeDtypeStruct((count, rows, width), jnp.bfloat16)
    one = jax.ShapeDtypeStruct((1, rows, width), jnp.bfloat16)
    out = pl.pallas_call(
        functools.partial(halve_kernel, split),
        grid_spec=pltpu.PrefetchScalarGridSpec(
            num_scalar_prefetch=1,
            grid=(count, tiles),
            in_specs=[spec(0), spec(0), spec(count), spec(count)],
            out_specs=[out_spec]
            + ([one_spec(at) for at in range(count)] if split else [out_spec]),
        ),
        out_shape=[shape] + ([one] * count if split else [shape]),
        compiler_params=pltpu.CompilerParams(vmem_limit_bytes=vmem_bytes),
        cost_estimate=light,
    )(place, kept, came, kept, came)
    return out[0], out[1:]


def halve_late_kernel(place_ref, *refs):
    step = pl.program_id(0)
    for which in range(2):
        own_ref, early_ref, late_ref = refs[3 * which : 3 * which + 3]
        out_ref = refs[6 + which]
        for block, came_ref in enumerate((early_ref, late_ref)):

            def store(out_ref=out_ref, own_ref=own_ref, came_ref=came_ref):
                total = own_ref[0].astype(jnp.float32) + came_ref[0].astype(jnp.float32)
                out_ref[0] = total.astype(jnp.bfloat16)

            pl.when(place_ref[2 * which + step] // 2 == block)(store)


def halve_late(keep_at, send_at, kept, early, late):
    rows, width = kept.shape[1:]
    at = list(keep_at) + list(send_at)
    place = jnp.stack(at + [block % 2 for block in at]).astype(jnp.int32)
    spec = lambda first: pl.BlockSpec((1, rows, width), lambda j, place: (place[first + j], 0, 0))
    out_spec = pl.BlockSpec((1, rows, width), lambda j, place: (j, 0, 0))
    shape = jax.ShapeDtypeStruct((2, rows, width), jnp.bfloat16)
    return pl.pallas_call(
        halve_late_kernel,
        grid_spec=pltpu.PrefetchScalarGridSpec(
            num_scalar_prefetch=1,
            grid=(2,),
            in_specs=[spec(0), spec(4), spec(4), spec(2), spec(6), spec(6)],
            out_specs=[out_spec, out_spec],
        ),
        out_shape=[shape, shape],
        compiler_params=pltpu.CompilerParams(vmem_limit_bytes=vmem_bytes),
        cost_estimate=light,
    )(place, kept, early, late, kept, early, late)


def combine_kernel(place_ref, *refs):
    kept_ref, sent_refs = refs[8], refs[9:]

    def put(sources, out_ref):
        total = lambda kept, came: (
            kept[0].astype(jnp.float32) + came[0].astype(jnp.float32)
        ).astype(jnp.bfloat16)
        outer, inner = total(*sources[:2]), total(*sources[2:])
        tall, low = outer.shape[0] // 4, inner.shape[0] // 4
        wide = outer.shape[1]
        both = tall + inner.shape[1] // wide * low
        for piece in range(4):
            out_ref[0, pl.ds(piece * both, tall), :] = outer[piece * tall : (piece + 1) * tall]
            for block in range(inner.shape[1] // wide):
                out_ref[0, pl.ds(piece * both + tall + block * low, low), :] = inner[
                    piece * low : (piece + 1) * low, block * wide : (block + 1) * wide
                ]

    put(refs[:4], kept_ref)
    for index, sent_ref in enumerate(sent_refs):
        pl.when(pl.program_id(0) == index)(functools.partial(put, refs[4:8], sent_ref))


def combine(keep_at, send_at, outer, inner):
    place = jnp.stack(list(keep_at) + list(send_at)).astype(jnp.int32)
    spec = lambda values, first: pl.BlockSpec(
        (1,) + values.shape[1:], lambda j, place: (place[first + j], 0, 0)
    )
    arrays = list(outer) + list(inner)
    width = outer[0].shape[2]
    rows = outer[0].shape[1] + inner[0].shape[1] * inner[0].shape[2] // width
    one = jax.ShapeDtypeStruct((1, rows, width), jnp.bfloat16)
    one_spec = pl.BlockSpec((1, rows, width), lambda j, place: (0, 0, 0))
    return pl.pallas_call(
        combine_kernel,
        grid_spec=pltpu.PrefetchScalarGridSpec(
            num_scalar_prefetch=1,
            grid=(2,),
            in_specs=[spec(values, first) for first in (0, 2) for values in arrays],
            out_specs=[
                pl.BlockSpec((1, rows, width), lambda j, place: (j, 0, 0)),
                one_spec,
                one_spec,
            ],
        ),
        out_shape=[jax.ShapeDtypeStruct((2, rows, width), jnp.bfloat16), one, one],
        compiler_params=pltpu.CompilerParams(vmem_limit_bytes=vmem_bytes),
        cost_estimate=light,
    )(place, *arrays, *arrays)


def unpack_kernel(tall, inner_blocks, place_ref, own_ref, other_ref, *out_refs):
    def put(source):
        if not inner_blocks:
            for index, out_ref in enumerate(out_refs):
                wide = out_ref.shape[1]
                out_ref[...] = source[:, index * wide : (index + 1) * wide].astype(jnp.float32)
            return
        outer_ref, inner_ref = out_refs
        low, wide = inner_ref.shape[0], source.shape[1]
        outer_ref[...] = source[pl.ds(0, tall), :].astype(jnp.float32)
        for block in range(inner_blocks):
            rows = source[pl.ds(tall + block * low, low), :]
            inner_ref[:, block * wide : (block + 1) * wide] = rows.astype(jnp.float32)

    pl.when(pl.program_id(0) == 0)(lambda: put(own_ref))
    pl.when(pl.program_id(0) == 1)(lambda: put(other_ref))


def unpack(core, own, other, count=0, tall=0, inner_blocks=0):
    rows, width = own.shape
    if inner_blocks:
        steps, block = 8, rows // 8
        low = (block - tall) // inner_blocks
        shapes = [(16 * tall, width), (16 * low, inner_blocks * width)]
        blocks = [(tall, width), (low, inner_blocks * width)]
    else:
        steps, block = 2, rows // 2
        shapes = [(2 * rows, width // count)] * count
        blocks = [(block, width // count)] * count
    return pl.pallas_call(
        functools.partial(unpack_kernel, tall, inner_blocks),
        grid_spec=pltpu.PrefetchScalarGridSpec(
            num_scalar_prefetch=1,
            grid=(2, steps),
            in_specs=[
                pl.BlockSpec(
                    (block, width),
                    lambda side, i, place: (jnp.where(side == 0, i, steps - 1), 0),
                ),
                pl.BlockSpec((block, width), lambda side, i, place: (jnp.where(side == 1, i, 0), 0)),
            ],
            out_specs=[
                pl.BlockSpec(shape, lambda side, i, place: (place[side] * steps + i, 0))
                for shape in blocks
            ],
        ),
        out_shape=[jax.ShapeDtypeStruct(shape, jnp.float32) for shape in shapes],
        compiler_params=pltpu.CompilerParams(vmem_limit_bytes=vmem_bytes),
        cost_estimate=light,
    )(jnp.stack([core, 1 - core]).astype(jnp.int32), own, other)


def norm_unit(values):
    center = values - jnp.mean(values, axis=-1, keepdims=True)
    inverse = lax.rsqrt(jnp.mean(center * center, axis=-1, keepdims=True) + norm_epsilon)
    return center * inverse, inverse


def layer_norm_back(values, norm_gain, grad):
    unit, inverse = norm_unit(values)
    scaled = grad * norm_gain
    back = scaled - jnp.mean(scaled, axis=-1, keepdims=True)
    back = back - unit * jnp.mean(scaled * unit, axis=-1, keepdims=True)
    return back * inverse


def dot_back(gradient, weight):
    return dot_nt(gradient, weight)


def column_sum(values):
    return jnp.sum(values.astype(jnp.float32), axis=0)


def swap(values, axis_name):
    return lax.ppermute(values, axis_name, [(0, 1), (1, 0)])


flips = {"x": 4, "y": 1, "z": 8}
square = ("zlo", "x", "core", "seq")


def exchange(values, axes):
    flip = [flips[axis] for axis in axes]
    return lax.ppermute(values, square, [(i, i ^ flip[i // 2 % 2]) for i in range(16)])


def square_bits(turned):
    core, x, zlo = lax.axis_index("core"), lax.axis_index("x"), lax.axis_index("zlo")
    first = 1 - core if turned else core
    return core, jnp.where(first == 1, x, zlo), jnp.where(first == 1, zlo, x)


def after(values, *others):
    return lax.optimization_barrier((values,) + others)[0]


def first_piece(shards):
    piece_rows = shards[0].shape[0] // 8
    core, high, low = square_bits(False)
    place = (core * 2 + high) * 2 + low
    piece = [
        lax.dynamic_slice_in_dim(shard, place * piece_rows, piece_rows, axis=0) for shard in shards
    ]
    return swap(piece[0] if len(piece) == 1 else jnp.concatenate(piece, axis=1), "seq")


class Pieces:
    def __init__(self, piece):
        core, high, low = square_bits(False)
        self.own = piece
        place = lambda side, one, two: (side * 2 + one) * 2 + two
        self.places = [
            place(core, high, low),
            place(core, high, 1 - low),
            place(core, 1 - high, low),
            place(core, 1 - high, 1 - low),
            place(1 - core, low, high),
            place(1 - core, low, 1 - high),
            place(1 - core, 1 - low, high),
            place(1 - core, 1 - low, 1 - high),
        ]

    def first(self, *others):
        self.own = after(self.own, *others)
        self.low = exchange(self.own, "xz")
        self.high = exchange(self.own, "zx")
        self.core = swap(self.own, "core")
        return self.low, self.high, self.core

    def second(self, *others):
        low, high = after(self.low, *others), after(self.high, *others)
        self.both = exchange(low, "zx")
        self.core_low, self.core_high = swap(low, "core"), swap(high, "core")
        return self.both, self.core_low, self.core_high

    def third(self, *others):
        self.core_both = swap(after(self.both, *others), "core")
        return [self.core_both]

    def parts(self, *others):
        return [
            after(self.own, *others),
            self.low,
            self.high,
            self.both,
            self.core,
            self.core_low,
            self.core_high,
            self.core_both,
        ]


class Total:
    def __init__(self, split, steps, turned, halves, inner=None):
        kept, sent = split
        self.inner = None
        if inner is not None:
            self.inner = (inner[0], swap(self.blocks(inner[1], 4), "core"))
            self.tall, self.inner_blocks = kept.shape[1] // 8, inner[0].shape[2] // kept.shape[2]
        self.core, self.first, self.second = square_bits(turned)
        self.seq, self.zhi = lax.axis_index("seq"), lax.axis_index("zhi")
        self.steps, self.halves = steps, halves
        self.along = ("x", "z") if turned else ("z", "x")
        self.came = swap(self.blocks(sent, 4), "core")
        self.kept = self.blocks(kept, 4)
        self.stage = 0

    def blocks(self, values, count):
        return values.reshape(count, -1, values.shape[-1])

    def by_core(self, choose):
        both = [choose([axes[core] for axes in self.steps]) for core in range(2)]
        return [jnp.where(self.core == 0, *pair) for pair in zip(*both)]

    def bits(self):
        seq, first, second = self.seq, self.first, self.second

        def one(axes):
            if axes[0] == "y":
                return [seq * 2, seq * 2 + 1, 2 - seq * 2, 3 - seq * 2]
            return [first, 2 + first, 1 - first, 3 - first]

        def two(axes):
            if axes[0] != "y" and axes[1] != "y":
                return [second, 2 + second, 1 - second, 3 - second]
            bit = first if axes[0] == "y" else seq
            return [bit * 2, bit * 2 + 1, 2 - bit * 2, 3 - bit * 2]

        def three(axes):
            bit = seq if axes[2] == "y" else second
            return [bit, 1 - bit]

        def four(axes):
            return [self.zhi, 1 - self.zhi]

        at = self.by_core((one, two, three, four)[self.stage])
        return at[: len(at) // 2], at[len(at) // 2 :]

    def step(self, *others):
        self.kept = after(self.kept, *others)
        keep, send = self.bits()
        self.kept = self.blocks(self.kept, 2 * len(keep))
        if self.stage == 0 and self.inner is not None:
            kept, came = (self.blocks(values, 4) for values in self.inner)
            self.kept, *sent = combine(keep, send, (self.kept, self.came), (kept, came))
            self.came, self.rest = exchange(sent[0], self.steps[0]), sent[1]
            self.stage += 1
            return sent[0]
        if self.stage == 1 and self.halves:
            early, late = (self.blocks(came, 2) for came in self.came)
            self.kept, sent = halve_late(keep, send, self.kept, early, late)
        else:
            split = self.stage == 0 and self.halves
            came = self.blocks(self.came, 2 * len(keep))
            self.kept, sent = halve(keep, send, self.kept, came, split)
            if split:
                self.came, self.rest = exchange(sent[0], self.steps[0]), sent[1]
                self.stage += 1
                return sent[0]
            sent = sent[0]
        if self.stage < 3:
            self.came = exchange(sent, self.steps[self.stage])
        else:
            self.came = swap(sent, "zhi")
        self.stage += 1
        return sent

    def step_rest(self, *others):
        sent = after(self.rest, self.came, *others)
        self.came = (self.came, exchange(sent, self.steps[0]))
        return sent

    def gather(self, *others):
        if self.stage > 4:
            self.part = after(self.part, *others)
        else:
            self.kept = after(self.kept, *others)
        if self.stage == 4:
            piece = self.kept[0].astype(jnp.float32) + self.came[0].astype(jnp.float32)
            self.part = piece.astype(jnp.bfloat16)
            self.came = swap(self.part, "zhi")
        elif self.stage == 5:
            self.part = merge(self.zhi, self.part, self.came)
            self.came = exchange(self.part, self.along[::-1])
        elif self.stage == 6:
            self.part = merge(self.second, self.part, self.came)
            self.came = exchange(self.part, self.along)
        else:
            self.part = merge(self.first, self.part, self.came)
            self.came = swap(self.part, "core")
        self.stage += 1
        return self.part

    def advance(self, *others):
        if self.stage < 4:
            return [self.step(*others)]
        return [self.gather(*others)] if self.stage < 8 else []

    def result(self, count, *others):
        part = after(self.part, *others)
        if self.inner is None:
            return unpack(self.core, part, self.came, count)
        return unpack(self.core, part, self.came, 2, self.tall, self.inner_blocks)


def sum_plain(terms):
    terms = lax.psum_scatter(terms.astype(jnp.bfloat16), "seq", scatter_dimension=0, tiled=True)
    return lax.psum(terms, page_axes)


page_axes = ("zhi", "zlo", "x", "core")


class VectorTotal:
    def __init__(self, values):
        self.values = values
        self.axes = [axis for axis in page_axes + ("seq",) if lax.axis_size(axis) == 2]
        rest = tuple(axis for axis in page_axes + ("seq",) if lax.axis_size(axis) != 2)
        if rest:
            self.values = lax.psum(self.values, rest)
        self.came = swap(self.values, self.axes.pop(0))

    def advance(self, *others):
        if self.came is None:
            return []
        self.values, self.came = after(self.values, *others) + self.came, None
        if self.axes:
            self.came = swap(self.values, self.axes.pop(0))
        return [self.values]

    def result(self):
        while self.came is not None:
            self.advance()
        return self.values


def on_device(
    tokens,
    patches,
    lengths,
    blank_mask,
    cotangent,
    first_gain,
    first_shift,
    self_query,
    self_query_bias,
    self_key,
    self_value,
    self_value_bias,
    self_output,
    self_output_bias,
    second_gain,
    second_shift,
    cross_query,
    cross_query_bias,
    cross_key,
    cross_value,
    cross_value_bias,
    cross_output,
    cross_output_bias,
    third_gain,
    third_shift,
    ffn_inner,
    ffn_inner_bias,
    ffn_outer,
    ffn_outer_bias,
):
    seq_count = lax.axis_size("seq")
    seq_index = lax.axis_index("seq")
    vectors = (
        first_gain,
        first_shift,
        self_query_bias,
        self_value_bias,
        self_output_bias,
        second_gain,
        second_shift,
        cross_query_bias,
        cross_value_bias,
        cross_output_bias,
        third_gain,
        third_shift,
        ffn_inner_bias,
        ffn_outer_bias,
    )
    two = seq_count == 2 and lax.axis_size("zhi") == 2
    joined = jnp.concatenate(vectors).reshape(-1, 128)
    if two:
        joined_other = swap(joined, "seq")
        gathered = jnp.where(
            seq_index == 0,
            jnp.stack([joined, joined_other]),
            jnp.stack([joined_other, joined]),
        )
    else:
        gathered = lax.all_gather(joined, "seq", axis=0, tiled=False)
    gathered = gathered.reshape(seq_count, -1)
    whole_vectors, start = [], 0
    for vector in vectors:
        part = gathered[:, start : start + vector.shape[0]].reshape(-1)
        whole_vectors.append(part.astype(jnp.float32))
        start += vector.shape[0]
    (
        gain_one,
        shift_one,
        bias_self_query,
        bias_self_value,
        bias_self_output,
        gain_two,
        shift_two,
        bias_cross_query,
        bias_cross_value,
        bias_cross_output,
        gain_three,
        shift_three,
        bias_inner,
        bias_outer,
    ) = whole_vectors
    tokens, patches, cotangent = tokens[0], patches[0], cotangent[0]
    tok_rows, width = tokens.shape
    patch_rows = patches.shape[0]
    query_scale = 1.0 / math.sqrt(HEAD)

    core = lax.axis_index("core")
    self_shards = [self_query, self_key, self_value, self_output]
    cross_shards = [cross_key, cross_value, cross_query, cross_output]
    if two:
        pieces = Pieces(first_piece(self_shards))
        pieces.first(joined_other)
        tokens_other = lax.ppermute(after(tokens, pieces.own), "seq", [(0, 1)])
        pieces.second()
        cross_pieces = Pieces(first_piece([after(cross_key, pieces.low)] + cross_shards[1:]))
        pieces.third()
        whole_self = assemble(
            seq_index, pieces.places, self_shards, pieces.parts(tokens_other)
        )
        tokens_all = jnp.concatenate([tokens, after(tokens_other, whole_self)])
    else:
        gather = lambda shard: lax.all_gather(shard, "seq", axis=0, tiled=True)
        whole_self = gather(jnp.concatenate(self_shards, axis=1))
        whole_cross = gather(jnp.concatenate(cross_shards, axis=1))
        whole_ffn_inner, whole_ffn_outer = gather(ffn_inner), gather(ffn_outer)
        tokens_all, patches_all = gather(tokens), gather(patches)

    first_place = seq_index * tok_rows
    key_start = first_place if two else 0
    info = jnp.stack([first_place, lengths[0], key_start, seq_index]).astype(jnp.int32)
    self_plan = Plan(
        ("limit", "earlier") if two else ("limit",),
        tok_rows if two else tok_rows * seq_count,
        tok_rows,
        256,
        two,
    )
    cross_plan = Plan(("bias",), patch_rows * seq_count, tok_rows, 256, False)
    blank_bias = jnp.where(blank_mask[0] == 0, 0.0, masked_score).astype(jnp.float32)
    if two:
        halves = blank_bias.reshape(2, patch_rows)
        blank_bias = jnp.where(seq_index == 0, halves, halves[::-1]).reshape(-1)
    blank_bias = blank_bias[:, None]
    no_bias = jnp.zeros((self_plan.all_rows, 1), jnp.float32)

    zeros = jnp.zeros_like(bias_self_value)
    token_values = tokens.astype(jnp.float32)
    normed_all = layer_norm(tokens_all.astype(jnp.float32), gain_one, shift_one).astype(
        jnp.bfloat16
    )
    if two:
        normed_one = normed_all[:tok_rows]
    else:
        normed_one = layer_norm(token_values, gain_one, shift_one).astype(jnp.bfloat16)
    queries_self = (
        (dot_nn(normed_one, whole_self[:, :width]) + bias_self_query) * query_scale
    ).astype(jnp.bfloat16)
    self_bias = jnp.concatenate([zeros, bias_self_value])
    self_pairs = (dot_nn(normed_all, whole_self[:, width : 3 * width]) + self_bias).astype(
        jnp.bfloat16
    )
    attend_self = functools.partial(attend, self_plan, info)
    if two:
        sent = cross_pieces.first(queries_self)
        patches_other = swap(after(patches, cross_pieces.own), "seq")
        mixed_self, log_self = attend_self(
            after(queries_self, *sent), self_pairs, no_bias, 0, 1
        )
        mixed_self = after(mixed_self, patches_other, *cross_pieces.second())
        inner_pieces = Pieces(first_piece([after(ffn_inner, patches_other)]))
    else:
        mixed_self, log_self = attend_self(queries_self, self_pairs, no_bias, 0, 1)
    hidden_one = token_values + dot_nn(mixed_self, whole_self[:, 3 * width :]) + bias_self_output
    normed_two = layer_norm(hidden_one, gain_two, shift_two).astype(jnp.bfloat16)
    if two:
        cross_pieces.third()
        whole_cross = assemble(
            seq_index, cross_pieces.places, cross_shards, cross_pieces.parts(normed_two)
        )
        patches_all = jnp.concatenate([patches, patches_other])
        patches_all = after(patches_all, whole_cross, inner_pieces.own)
        outer_pieces = Pieces(first_piece([after(ffn_outer, inner_pieces.own)]))
    patch_bias = jnp.concatenate([zeros, bias_cross_value])
    patch_pairs = (dot_nn(patches_all, whole_cross[:, : 2 * width]) + patch_bias).astype(
        jnp.bfloat16
    )
    queries_cross = (
        (dot_nn(normed_two, whole_cross[:, 2 * width : 3 * width]) + bias_cross_query) * query_scale
    ).astype(jnp.bfloat16)
    attend_cross = functools.partial(attend, cross_plan, info)
    if two:
        keys = (patch_pairs, blank_bias)
        sent = inner_pieces.first(queries_cross) + (outer_pieces.own,)
        done = attend_cross(after(queries_cross, *sent), *keys, 0, 2)
        sent = inner_pieces.second() + outer_pieces.first()
        sent = [after(values, done[0]) for values in sent]
        inner_pieces.both, inner_pieces.core_low, inner_pieces.core_high = sent[:3]
        outer_pieces.low, outer_pieces.high, outer_pieces.core = sent[3:]
        inner_pieces.third()
        outer_pieces.second()
        done = attend_cross(after(queries_cross, *sent), *keys, 1, 2, done)
        late = [after(values, done[0]) for values in (outer_pieces.both, inner_pieces.core_both)]
        outer_pieces.both, inner_pieces.core_both = late
        inner_other = join(inner_pieces.places, inner_pieces.parts(done[0]))
        mixed_cross, log_cross = done
        outer_pieces.third()
        mixed_cross = after(mixed_cross, inner_other)
    else:
        mixed_cross, log_cross = attend_cross(queries_cross, patch_pairs, blank_bias, 0, 1)
    hidden_two = hidden_one + dot_nn(mixed_cross, whole_cross[:, 3 * width :]) + bias_cross_output
    normed_three = layer_norm(hidden_two, gain_three, shift_three).astype(jnp.bfloat16)
    if two:
        outer_other = join(outer_pieces.places, outer_pieces.parts(normed_three))
        outputs, grad_normed_three, column_inner, split_outer, split_inner = ffn_both_ways(
            seq_index,
            core,
            normed_three,
            hidden_two,
            cotangent,
            ffn_inner,
            inner_other,
            ffn_outer,
            outer_other,
            bias_inner,
            bias_outer,
        )
        total_ffn = Total(split_outer, ("xy", "yz", "zx"), True, True, split_inner)
    else:
        inner_sum = dot_nn(normed_three, whole_ffn_inner) + bias_inner
        active = jax.nn.gelu(inner_sum, approximate=False).astype(jnp.bfloat16)
        outputs = (hidden_two + dot_nn(active, whole_ffn_outer) + bias_outer).astype(jnp.bfloat16)
        grad_active = dot_back(cotangent, whole_ffn_outer)
        gelu_pull = jax.vjp(lambda u: jax.nn.gelu(u, approximate=False), inner_sum)[1]
        grad_inner = gelu_pull(grad_active)[0].astype(jnp.bfloat16)
        column_inner = column_sum(grad_inner)
        grad_normed_three = dot_back(grad_inner, whole_ffn_inner)
    back_two = layer_norm_back(hidden_two, gain_three, grad_normed_three)
    grad_hidden_two = cotangent.astype(jnp.float32) + back_two
    branch_cross = grad_hidden_two.astype(jnp.bfloat16)
    grad_mixed_cross = dot_back(branch_cross, whole_cross[:, 3 * width :]).astype(jnp.bfloat16)
    back_cross = functools.partial(
        attend_back, cross_plan, info, queries_cross, mixed_cross
    )
    cross_rest = (log_cross, patch_pairs, blank_bias)
    if two:
        sent = total_ffn.step(grad_mixed_cross)
        cross_back = back_cross(after(grad_mixed_cross, sent), *cross_rest, 0, 1)
    else:
        cross_back = back_cross(grad_mixed_cross, *cross_rest, 0, 1)
    scaled_cross, grad_patch_keys, grad_patch_values = cross_back
    cross_products = [
        (normed_two, scaled_cross),
        (patches_all, grad_patch_keys),
        (patches_all, grad_patch_values),
        (mixed_cross, branch_cross),
    ]
    if two:
        scaled_cross = after(scaled_cross, total_ffn.step_rest(scaled_cross))
    grad_normed_two = dot_back(scaled_cross, whole_cross[:, 2 * width : 3 * width])
    back_one = layer_norm_back(hidden_one, gain_two, grad_normed_two)
    grad_hidden_one = grad_hidden_two + back_one
    branch_self = grad_hidden_one.astype(jnp.bfloat16)
    grad_mixed_self = dot_back(branch_self, whole_self[:, 3 * width :]).astype(jnp.bfloat16)
    back_self = functools.partial(attend_back, self_plan, info, queries_self, mixed_self)
    self_rest = (log_self, self_pairs, no_bias)
    if two:
        products = [
            (0, scaled_cross),
            (1, grad_patch_keys),
            (1, grad_patch_values),
            (2, branch_cross),
            (3, branch_self),
        ]
        lefts = [after(normed_two, grad_mixed_self), patches_all, mixed_cross, mixed_self]
        kept, sent = outer_group(core, lefts, products)
        late = total_ffn.step(kept)
        total_mid = Total((kept, after(sent, late)), ("zx", "yz", "xy"), False, True)
        sent = total_mid.step(late)
        self_back = back_self(after(grad_mixed_self, sent), *self_rest, 0, 1)
    else:
        self_back = back_self(grad_mixed_self, *self_rest, 0, 1)
    scaled_self, grad_keys, grad_values = self_back
    self_products = [
        (normed_one, scaled_self),
        (normed_all, grad_keys),
        (normed_all, grad_values),
        (mixed_self, branch_self),
    ]
    if two:
        late = (total_ffn.step(scaled_self), total_mid.step_rest(scaled_self))
        products = [(0, scaled_self), (1, grad_keys), (1, grad_values)]
        lefts = [after(normed_one, *late), normed_all]
        kept, sent = outer_group(core, lefts, products)
        late = (total_ffn.step(kept), total_mid.step(kept))
        total_last = Total((kept, after(sent, *late)), ("yz", "xy", "zx"), True, False)
        late = total_last.advance(*late)
        late = late + total_ffn.advance(*late)
        grad_keys, scaled_self = (after(values, *late) for values in (grad_keys, scaled_self))
    normed_terms = dot_back(grad_keys, whole_self[:, width : 2 * width]) + dot_back(
        grad_values, whole_self[:, 2 * width : 3 * width]
    )
    if two:
        sent = total_mid.advance(normed_terms)
        sent = sent + total_ffn.advance(*sent)
        grad_patch_keys = after(grad_patch_keys, *sent)
    patch_terms = dot_back(grad_patch_keys, whole_cross[:, :width]) + dot_back(
        grad_patch_values, whole_cross[:, width : 2 * width]
    )
    if two:
        normed_sent = normed_terms[tok_rows:].astype(jnp.bfloat16)
        normed_came = lax.ppermute(normed_sent, "seq", [(1, 0)])
        grad_normed = normed_terms[:tok_rows] + normed_came.astype(jnp.float32)
        patch_sent = patch_terms[patch_rows:].astype(jnp.bfloat16)
        grad_patches = patch_terms[:patch_rows] + swap(patch_sent, "seq").astype(jnp.float32)
    else:
        grad_patches, grad_normed = (
            lax.psum_scatter(
                terms.astype(jnp.bfloat16), "seq", scatter_dimension=0, tiled=True
            ).astype(jnp.float32)
            for terms in (patch_terms, normed_terms)
        )
    grad_normed = grad_normed + dot_back(scaled_self, whole_self[:, :width])
    grad_tokens = grad_hidden_one + layer_norm_back(token_values, gain_one, grad_normed)
    norm_pairs = (
        (token_values, grad_normed),
        (hidden_one, grad_normed_two),
        (hidden_two, grad_normed_three),
    )
    plain = (
        scaled_self,
        grad_values,
        branch_self,
        scaled_cross,
        grad_patch_values,
        branch_cross,
        cotangent,
    )
    if two:
        late = total_last.advance(patch_terms)
        late = late + total_ffn.advance(*late)
        norm_pairs = ((after(token_values, *late), grad_normed),) + norm_pairs[1:]
    sums = row_sums(norm_pairs, plain)
    vector_sums = jnp.concatenate([sums, column_inner.reshape(-1, width)])
    if two:
        totals = (total_mid, total_ffn, total_last)
        late = total_mid.advance(vector_sums)
        late = late + total_ffn.advance(*late)
        late = total_last.advance(*late)
        grad_outer, grad_ffn_in = total_ffn.result(2, *late)
        late = total_mid.advance(grad_outer)
        while any(total.stage < 8 for total in totals):
            late = total_last.advance(*late) or late
            late = total_mid.advance(*late) or late
        vector_total = VectorTotal(after(vector_sums, *late))
        late = vector_total.advance(*late)
        *wide_cross, wide_output = total_mid.result(5, *late)
        late = vector_total.advance(wide_output)
        wide_self = [*total_last.result(3, *late), wide_output]
    else:
        grad_outer = sum_plain(dot_tn(active, cotangent)).astype(jnp.float32)
        grad_ffn_in = sum_plain(dot_tn(normed_three, grad_inner)).astype(jnp.float32)
        wide_cross = [
            sum_plain(dot_tn(*product)).astype(jnp.float32) for product in cross_products
        ]
        wide_self = [sum_plain(dot_tn(*product)).astype(jnp.float32) for product in self_products]
        vector_total = VectorTotal(vector_sums)
    sums = vector_total.result()
    small_width = width // seq_count
    own_sums = lax.dynamic_slice_in_dim(sums[:-4], seq_index * small_width, small_width, axis=1)
    inner_rows = sums[-(column_inner.shape[0] // width) :].reshape(-1)
    inner_width = column_inner.shape[0] // seq_count
    own_inner = lax.dynamic_slice_in_dim(inner_rows, seq_index * inner_width, inner_width, axis=0)
    order = (0, 1, 6, 7, 8, 2, 3, 9, 10, 11, 4, 5, None, 12)
    small = [own_inner if at is None else own_sums[at] for at in order]
    totals = (
        small[0],
        small[1],
        wide_self[0],
        small[2],
        wide_self[1],
        wide_self[2],
        small[3],
        wide_self[3],
        small[4],
        small[5],
        small[6],
        wide_cross[0],
        small[7],
        wide_cross[1],
        wide_cross[2],
        small[8],
        wide_cross[3],
        small[9],
        small[10],
        small[11],
        grad_ffn_in,
        small[12],
        grad_outer,
        small[13],
    )
    return (outputs[None], grad_tokens[None], grad_patches[None]) + totals


def solution(mesh):
    page_count, seq_count = mesh.devices.shape
    mesh = Mesh(
        mesh.devices.reshape(page_count // 8, 2, 2, 2, seq_count),
        ("zhi", "zlo", "x", "core", "seq"),
    )
    page = ("zhi", "zlo", "x", "core")
    pages = P(page, "seq", None)
    rows, vector = P("seq", None), P("seq")
    layer = (
        (vector, vector)
        + (rows, vector, rows, rows, vector, rows, vector)
        + (vector, vector)
        + (rows, vector, rows, rows, vector, rows, vector)
        + (vector, vector)
        + (rows, vector, rows, vector)
    )
    return jax.shard_map(
        on_device,
        mesh=mesh,
        in_specs=(pages, pages, P(page), P(page, None), pages) + layer,
        out_specs=(pages, pages, pages) + layer,
        check_vma=False,
    )
```

```python
import functools
import math

import jax
import jax.numpy as jnp
from jax import lax
from jax.experimental import pallas as pl
from jax.experimental.pallas import tpu as pltpu
from jax.sharding import Mesh
from jax.sharding import PartitionSpec as P

HEADS = 16
HEAD = 64


norm_epsilon = 1e-05
masked_score = -1000000000.0


def layer_norm(values, norm_gain, norm_shift):
    center = values - jnp.mean(values, axis=-1, keepdims=True)
    spread = jnp.mean(center * center, axis=-1, keepdims=True)
    return center * lax.rsqrt(spread + norm_epsilon) * norm_gain + norm_shift


pair_width = 2 * HEAD
vmem_bytes = 60 * 1024 * 1024
light = pl.CostEstimate(flops=1, bytes_accessed=1, transcendentals=0)


def dot_nt(left_side, right_side):
    return lax.dot_general(
        left_side, right_side, (((1,), (1,)), ((), ())), preferred_element_type=jnp.float32
    )


def dot_nn(left_side, right_side):
    return jnp.dot(left_side, right_side, preferred_element_type=jnp.float32)


def dot_tn(left_side, right_side):
    return lax.dot_general(
        left_side, right_side, (((0,), (0,)), ((), ())), preferred_element_type=jnp.float32
    )


def one_head(values, head):
    lane = lax.broadcasted_iota(jnp.int32, values.shape, 1)
    return jnp.where((lane >= head * HEAD) & (lane < (head + 1) * HEAD), values, 0)


class Plan:
    def __init__(self, kinds, key_rows, query_rows, chunk, causal):
        self.kinds = kinds
        self.key_rows = key_rows
        self.all_rows = key_rows * len(kinds)
        self.query_rows = query_rows
        self.chunk = min(chunk, query_rows)
        self.causal = causal

    def blocks(self, start, segments):
        found = []
        for segment in segments:
            rows = self.key_rows
            if self.causal and self.kinds[segment] == "limit":
                rows = min(rows, start + self.chunk)
            found.append((self.kinds[segment], pl.ds(segment * self.key_rows, rows)))
        return found


def query_limit(info_ref, start, chunk):
    lane = lax.broadcasted_iota(jnp.int32, (1, chunk), 1) + start
    place = info_ref[0] + lane
    return jnp.minimum(place, info_ref[1] - 1) - info_ref[2]


def masked_block(kind, scores, limit, bias_ref):
    if kind == "limit":
        key = lax.broadcasted_iota(jnp.int32, scores.shape, 0)
        return jnp.where(key <= limit, scores, masked_score)
    if kind == "bias":
        return scores + bias_ref[...]
    return scores


def run_segments(plan, info_ref, body):
    every = list(range(len(plan.kinds)))
    needed = [segment for segment in every if plan.kinds[segment] != "earlier"]
    if len(needed) == len(every):
        body(every)
        return
    pl.when(info_ref[3] == 1)(lambda: body(every))
    pl.when(info_ref[3] != 1)(lambda: body(needed))


def attend_kernel(plan, info_ref, query_ref, key_ref, value_ref, bias_ref, mixed_ref, log_ref):
    def body(segments):
        for start in range(0, plan.query_rows, plan.chunk):
            limit = query_limit(info_ref, start, plan.chunk)
            lane = lax.broadcasted_iota(jnp.int32, (1, plan.chunk), 1) + start
            valid = (info_ref[0] + lane < info_ref[1]).astype(jnp.float32)
            query = query_ref[pl.ds(start, plan.chunk), :]
            parts = []
            for head in range(2):
                head_query = one_head(query, head)
                blocks = plan.blocks(start, segments)
                scores = [
                    masked_block(kind, dot_nt(key_ref[rows, :], head_query), limit, bias_ref)
                    for kind, rows in blocks
                ]
                peak = jnp.max(scores[0], axis=0, keepdims=True)
                for block in scores[1:]:
                    peak = jnp.maximum(peak, jnp.max(block, axis=0, keepdims=True))
                total = jnp.zeros_like(peak)
                mixed = jnp.zeros((pair_width, plan.chunk), jnp.float32)
                for (kind, rows), block in zip(blocks, scores):
                    weights = jnp.exp(block - peak)
                    total = total + jnp.sum(weights, axis=0, keepdims=True)
                    mixed = mixed + dot_tn(value_ref[rows, :], weights.astype(jnp.bfloat16))
                parts.append(mixed[head * HEAD : (head + 1) * HEAD] * (valid / total))
                log_ref[0, pl.ds(head, 1), pl.ds(start, plan.chunk)] = peak + jnp.log(total)
            joined = jnp.concatenate(parts, axis=0)
            mixed_ref[pl.ds(start, plan.chunk), :] = joined.T.astype(jnp.bfloat16)

    run_segments(plan, info_ref, body)


def attend_back_kernel(
    plan,
    info_ref,
    query_ref,
    mixed_ref,
    grad_ref,
    log_ref,
    key_ref,
    value_ref,
    bias_ref,
    grad_query_ref,
    grad_key_ref,
    grad_value_ref,
    key_sum,
    value_sum,
):
    def body(segments):
        key_sum[...] = jnp.zeros_like(key_sum)
        value_sum[...] = jnp.zeros_like(value_sum)
        for start in range(0, plan.query_rows, plan.chunk):
            limit = query_limit(info_ref, start, plan.chunk)
            rows_here = pl.ds(start, plan.chunk)
            row = lax.broadcasted_iota(jnp.int32, (plan.chunk, 1), 0) + start
            valid = info_ref[0] + row < info_ref[1]
            query = query_ref[rows_here, :]
            grad = jnp.where(valid, grad_ref[rows_here, :], 0).astype(jnp.bfloat16)
            product = grad.astype(jnp.float32) * mixed_ref[rows_here, :].astype(jnp.float32)
            product = product.T
            parts = []
            for head in range(2):
                own = slice(head * HEAD, (head + 1) * HEAD)
                head_query, head_grad = one_head(query, head), one_head(grad, head)
                weighted = jnp.sum(product[own], axis=0, keepdims=True)
                log_total = log_ref[0, pl.ds(head, 1), rows_here]
                grad_query = jnp.zeros((pair_width, plan.chunk), jnp.float32)
                for kind, rows in plan.blocks(start, segments):
                    keys = key_ref[rows, :]
                    scores = masked_block(kind, dot_nt(keys, head_query), limit, bias_ref)
                    shares = jnp.exp(scores - log_total)
                    grad_shares = dot_nt(value_ref[rows, :], head_grad)
                    grad_scores = (shares * (grad_shares - weighted)).astype(jnp.bfloat16)
                    value_sum[rows, :] += dot_nn(shares.astype(jnp.bfloat16), head_grad)
                    key_sum[rows, :] += dot_nn(grad_scores, head_query)
                    grad_query = grad_query + dot_tn(keys, grad_scores)
                parts.append(grad_query[own])
            joined = jnp.concatenate(parts, axis=0) * (1.0 / math.sqrt(HEAD))
            grad_query_ref[rows_here, :] = joined.T.astype(jnp.bfloat16)
        grad_key_ref[...] = key_sum[...].astype(jnp.bfloat16)
        grad_value_ref[...] = value_sum[...].astype(jnp.bfloat16)

    run_segments(plan, info_ref, body)


def column_block(rows, first):
    return pl.BlockSpec((rows, pair_width), lambda step, info: (0, first + step))


def log_block(rows, first):
    return pl.BlockSpec((1, 2, rows), lambda step, info: (first + step, 0, 0))


def key_specs(plan, first):
    return [
        column_block(plan.all_rows, first),
        column_block(plan.all_rows, HEADS // 2 + first),
        pl.BlockSpec((plan.all_rows, 1), lambda step, info: (0, 0)),
    ]


any_block = pl.BlockSpec(memory_space=pl.ANY)


def skip_refs(kernel, place, count):
    def run(*refs):
        kernel(*refs[:place], *refs[place + count :])

    return run


def attend(plan, info, queries, key_values, bias, part, parts, into=()):
    pairs = HEADS // 2
    count, first = pairs // parts, part * (pairs // parts)
    rows, keys = plan.query_rows, plan.all_rows
    return pl.pallas_call(
        skip_refs(functools.partial(attend_kernel, plan), 5, len(into)),
        grid_spec=pltpu.PrefetchScalarGridSpec(
            num_scalar_prefetch=1,
            grid=(count,),
            in_specs=[column_block(rows, first)] + key_specs(plan, first) + [any_block] * len(into),
            out_specs=[column_block(rows, first), log_block(rows, first)],
        ),
        out_shape=[
            jax.ShapeDtypeStruct((rows, HEADS * HEAD), jnp.bfloat16),
            jax.ShapeDtypeStruct((pairs, 2, rows), jnp.float32),
        ],
        input_output_aliases={5 + index: index for index in range(len(into))},
        compiler_params=pltpu.CompilerParams(vmem_limit_bytes=vmem_bytes),
        cost_estimate=light,
    )(info, queries, key_values, key_values, bias, *into)


def attend_back(
    plan, info, queries, mixed, grad_mixed, log_total, key_values, bias, part, parts, into=()
):
    pairs = HEADS // 2
    count, first = pairs // parts, part * (pairs // parts)
    rows, keys = plan.query_rows, plan.all_rows
    return pl.pallas_call(
        skip_refs(functools.partial(attend_back_kernel, plan), 8, len(into)),
        grid_spec=pltpu.PrefetchScalarGridSpec(
            num_scalar_prefetch=1,
            grid=(count,),
            in_specs=[column_block(rows, first)] * 3
            + [log_block(rows, first)]
            + key_specs(plan, first)
            + [any_block] * len(into),
            out_specs=[
                column_block(rows, first),
                column_block(keys, first),
                column_block(keys, first),
            ],
            scratch_shapes=[pltpu.VMEM((keys, pair_width), jnp.float32)] * 2,
        ),
        out_shape=[
            jax.ShapeDtypeStruct((rows, HEADS * HEAD), jnp.bfloat16),
            jax.ShapeDtypeStruct((keys, HEADS * HEAD), jnp.bfloat16),
            jax.ShapeDtypeStruct((keys, HEADS * HEAD), jnp.bfloat16),
        ],
        input_output_aliases={8 + index: index for index in range(len(into))},
        compiler_params=pltpu.CompilerParams(vmem_limit_bytes=vmem_bytes),
        cost_estimate=light,
    )(info, queries, mixed, grad_mixed, log_total, key_values, key_values, bias, *into)


def join_kernel(count, place_ref, *refs):
    out_ref = refs[count]
    for index, source in enumerate(refs[:count]):
        rows = source.shape[0]
        first = pl.multiple_of(place_ref[index] * rows, rows)
        out_ref[pl.ds(first, rows), :] = source[...]


def join(places, parts):
    count, (rows, width) = len(parts), parts[0].shape
    steps = 1 if count * rows * width <= 1024 * 1024 else 4
    wide = width // steps
    return pl.pallas_call(
        functools.partial(join_kernel, count),
        grid_spec=pltpu.PrefetchScalarGridSpec(
            num_scalar_prefetch=1,
            grid=(steps,),
            in_specs=[pl.BlockSpec((rows, wide), lambda i, place: (0, i))] * count,
            out_specs=pl.BlockSpec((count * rows, wide), lambda i, place: (0, i)),
        ),
        out_shape=jax.ShapeDtypeStruct((count * rows, width), parts[0].dtype),
        compiler_params=pltpu.CompilerParams(vmem_limit_bytes=vmem_bytes),
        cost_estimate=light,
    )(jnp.stack(places).astype(jnp.int32), *parts)


def merge(index, own, other):
    return join([index, 1 - index], [own, other])


def assemble_kernel(count, place_ref, *refs):
    shards, parts, out_ref = refs[:count], refs[count:-1], refs[-1]
    for index, part in enumerate(parts):
        rows = part.shape[0]
        first = pl.multiple_of(place_ref[1 + index] * rows, rows)
        out_ref[pl.ds(first, rows), :] = part[...]
    for index, shard in enumerate(shards):

        def store(shard=shard):
            rows = shard.shape[0]
            first = pl.multiple_of(place_ref[0] * rows, rows)
            out_ref[pl.ds(first, rows), :] = shard[...]

        pl.when(pl.program_id(0) == index)(store)


def assemble(seq, places, shards, parts):
    count, (rows, wide) = len(shards), shards[0].shape
    part_rows = parts[0].shape[0]
    places = [seq] + [(1 - seq) * len(parts) + place for place in places]
    return pl.pallas_call(
        functools.partial(assemble_kernel, count),
        grid_spec=pltpu.PrefetchScalarGridSpec(
            num_scalar_prefetch=1,
            grid=(count,),
            in_specs=[pl.BlockSpec((rows, wide), lambda i, place: (0, 0))] * count
            + [pl.BlockSpec((part_rows, wide), lambda i, place: (0, i))] * len(parts),
            out_specs=pl.BlockSpec((2 * rows, wide), lambda i, place: (0, i)),
        ),
        out_shape=jax.ShapeDtypeStruct((2 * rows, count * wide), shards[0].dtype),
        compiler_params=pltpu.CompilerParams(vmem_limit_bytes=vmem_bytes),
        cost_estimate=light,
    )(jnp.stack(places).astype(jnp.int32), *shards, *parts)


def row_sums_kernel(norms, plain, *refs):
    steps = refs[: 2 * norms + plain]
    out_ref = refs[-1]

    @pl.when(pl.program_id(0) == 0)
    def start():
        out_ref[...] = jnp.zeros_like(out_ref)

    for index in range(norms):
        values, grad = steps[2 * index][...].astype(jnp.float32), steps[2 * index + 1][...]
        center = values - jnp.mean(values, axis=-1, keepdims=True)
        spread = jnp.mean(center * center, axis=-1, keepdims=True)
        unit = center * lax.rsqrt(spread + norm_epsilon)
        out_ref[pl.ds(2 * index, 1), :] += jnp.sum(grad * unit, axis=0, keepdims=True)
        out_ref[pl.ds(2 * index + 1, 1), :] += jnp.sum(grad, axis=0, keepdims=True)
    for index in range(plain):
        values = steps[2 * norms + index][...].astype(jnp.float32)
        at = pl.ds(2 * norms + index, 1)
        out_ref[at, :] += jnp.sum(values, axis=0, keepdims=True)


def row_sums(norm_pairs, plain):
    arrays = [values for pair in norm_pairs for values in pair] + list(plain)
    width = arrays[0].shape[1]
    rows = -(-(2 * len(norm_pairs) + len(plain)) // 8) * 8
    return pl.pallas_call(
        functools.partial(row_sums_kernel, len(norm_pairs), len(plain)),
        grid=(4,),
        in_specs=[
            pl.BlockSpec((values.shape[0] // 4, width), lambda step: (step, 0)) for values in arrays
        ],
        out_specs=pl.BlockSpec((rows, width), lambda step: (0, 0)),
        out_shape=jax.ShapeDtypeStruct((rows, width), jnp.float32),
        compiler_params=pltpu.CompilerParams(vmem_limit_bytes=vmem_bytes),
        cost_estimate=light,
    )(*arrays)


def ffn_kernel(half_steps, place_ref, *refs):
    normed, inner = refs[0:4], refs[4:8]
    outer_own, outer_other, bias_ref, bias_outer_ref, hidden_ref, cotangent_ref = refs[8:14]
    out_ref, grad_ref, column_ref, kept_outer, sent_outer, kept_inner, sent_inner = refs[14:21]
    total_ref, turned_ref = refs[21], refs[22]
    grad_sums = refs[23:27]
    step = pl.program_id(0)
    quarter = normed[0].shape[1]

    @pl.when(step == 0)
    def start():
        for index in range(4):
            turned_ref[index] = normed[index][...].T
            grad_sums[index][...] = jnp.zeros_like(grad_sums[index])
        total_ref[...] = hidden_ref[...] + bias_outer_ref[...]

    def run(outer_ref):
        inner_sum = bias_ref[...] + dot_nn(normed[0][...], inner[0][...])
        for index in range(1, 4):
            inner_sum = inner_sum + dot_nn(normed[index][...], inner[index][...])
        part = 0.5 + 0.5 * lax.erf(inner_sum * math.sqrt(0.5))
        active = (inner_sum * part).astype(jnp.bfloat16)
        slope = part + inner_sum * (
            jnp.exp(-0.5 * inner_sum * inner_sum) * (1.0 / math.sqrt(2.0 * math.pi))
        )
        cotangent = cotangent_ref[...]
        total_ref[...] += dot_nn(active, outer_ref[...])
        grad_inner = (dot_nt(cotangent, outer_ref[...]) * slope).astype(jnp.bfloat16)
        column_ref[...] = jnp.sum(grad_inner.astype(jnp.float32), axis=0, keepdims=True)
        for index in range(4):
            grad_sums[index][...] += dot_nt(grad_inner, inner[index][...])
        grad_outer = dot_tn(active, cotangent).astype(jnp.bfloat16)
        for which, out in ((0, kept_outer), (1, sent_outer)):

            def store(out=out):
                out[0] = grad_outer

            pl.when(step % 2 == which)(store)
        for index, (out, seq_at) in enumerate(
            ((kept_inner, 0), (sent_inner, 0), (kept_inner, 1), (sent_inner, 1))
        ):
            out[pl.ds(place_ref[seq_at], 1)] = dot_nn(turned_ref[index], grad_inner).astype(
                jnp.bfloat16
            )[None]

    pl.when(step < half_steps)(lambda: run(outer_own))
    pl.when(step >= half_steps)(lambda: run(outer_other))

    @pl.when(step == 2 * half_steps - 1)
    def finish():
        out_ref[...] = total_ref[...].astype(jnp.bfloat16)
        for index in range(4):
            first = pl.multiple_of(place_ref[4 + index] * quarter, quarter)
            grad_ref[:, pl.ds(first, quarter)] = grad_sums[index][...]


def ffn_both_ways(
    seq, core, normed, hidden, cotangent, inner_own, inner_other, outer_own, outer_other, bias, last
):
    rows, width = normed.shape
    units = inner_own.shape[1]
    chunk, quarter = units // 4, width // 4
    steps = units // chunk
    half_steps = steps // 2
    run = half_steps // 2
    order = []
    for step in range(steps):
        which, at = (seq, step) if step < half_steps else (1 - seq, step - half_steps)
        side = core if at % 2 == 0 else 1 - core
        order.append((which, side * run + at // 2))
    local = [at for _, at in order]
    whole = [which * half_steps + at for which, at in order]
    out_at = [which * run + step % half_steps // 2 for step, (which, _) in enumerate(order)]
    quarters = [seq * 2 + core, seq * 2 + 1 - core, (1 - seq) * 2 + core, (1 - seq) * 2 + 1 - core]
    place = jnp.stack(
        [seq, 1 - seq, core, 1 - core] + quarters + whole + local + out_at
    ).astype(jnp.int32)
    at_whole, at_local, at_out = 8, 8 + steps, 8 + 2 * steps
    fixed = lambda shape: pl.BlockSpec(shape, lambda step, place: (0,) * len(shape))
    normed_specs = [
        pl.BlockSpec((rows, quarter), lambda step, place, i=i: (0, place[4 + i])) for i in range(4)
    ]
    inner_specs = [
        pl.BlockSpec(
            (quarter, chunk), lambda step, place, i=i: (place[2 + i % 2], place[at_whole + step])
        )
        for i in range(4)
    ]
    own_at = lambda step, place: place[at_local + jnp.minimum(step, half_steps - 1)]
    other_at = lambda step, place: place[at_local + jnp.maximum(step, half_steps)]
    outer_shape = jax.ShapeDtypeStruct((2 * run, chunk, width), jnp.bfloat16)
    inner_shape = jax.ShapeDtypeStruct((2, quarter, units), jnp.bfloat16)
    outer_spec = pl.BlockSpec((1, chunk, width), lambda step, place: (place[at_out + step], 0, 0))
    inner_spec = pl.BlockSpec(
        (2, quarter, chunk), lambda step, place: (0, 0, place[at_whole + step])
    )
    row_spec = pl.BlockSpec((1, chunk), lambda step, place: (0, place[at_whole + step]))
    out, grad, column, kept_outer, sent_outer, kept_inner, sent_inner = pl.pallas_call(
        functools.partial(ffn_kernel, half_steps),
        grid_spec=pltpu.PrefetchScalarGridSpec(
            num_scalar_prefetch=1,
            grid=(steps,),
            in_specs=normed_specs
            + inner_specs
            + [
                pl.BlockSpec((chunk, width), lambda step, place: (own_at(step, place), 0)),
                pl.BlockSpec((chunk, width), lambda step, place: (other_at(step, place), 0)),
                row_spec,
                fixed((1, width)),
                fixed((rows, width)),
                fixed((rows, width)),
            ],
            out_specs=[
                fixed((rows, width)),
                fixed((rows, width)),
                row_spec,
                outer_spec,
                outer_spec,
                inner_spec,
                inner_spec,
            ],
            scratch_shapes=[
                pltpu.VMEM((rows, width), jnp.float32),
                pltpu.VMEM((4, quarter, rows), jnp.bfloat16),
            ]
            + [pltpu.VMEM((rows, quarter), jnp.float32)] * 4,
        ),
        out_shape=[
            jax.ShapeDtypeStruct((rows, width), jnp.bfloat16),
            jax.ShapeDtypeStruct((rows, width), jnp.float32),
            jax.ShapeDtypeStruct((1, units), jnp.float32),
            outer_shape,
            outer_shape,
            inner_shape,
            inner_shape,
        ],
        compiler_params=pltpu.CompilerParams(vmem_limit_bytes=vmem_bytes),
        cost_estimate=light,
    )(
        place,
        *[normed] * 4,
        inner_own,
        inner_own,
        inner_other,
        inner_other,
        outer_own,
        outer_other,
        bias[None],
        last[None],
        hidden,
        cotangent,
    )
    split = lambda kept, sent: (kept.reshape(2, -1, kept.shape[2]), sent.reshape(2, -1, kept.shape[2]))
    return out, grad, column[0], split(kept_outer, sent_outer), (kept_inner, sent_inner)


def outer_group_kernel(products, count, place_ref, *refs):
    lefts, rights = refs[:count], refs[count : count + len(products)]
    kept_ref, sent_ref, turned_ref = refs[count + len(products) :]
    part = kept_ref.shape[1]
    step = pl.program_id(0)
    sides = [side for side, _ in products]
    start = 0
    for index, (side, blocks) in enumerate(products):
        left, right = lefts[side], rights[index]
        tokens = pl.ds(0, left.shape[0])
        if sides.index(side) == index:

            def turn(left=left, tokens=tokens):
                turned_ref[:, tokens] = left[...].T

            pl.when(step == start)(turn)

        def run(right=right, tokens=tokens):
            for seq in range(2):
                for which, out_ref in ((0, kept_ref), (1, sent_ref)):
                    first = pl.multiple_of((seq * 2 + place_ref[which]) * part, part)
                    rows = turned_ref[pl.ds(first, part), tokens]
                    out_ref[seq] = dot_nn(rows, right[...]).astype(jnp.bfloat16)

        pl.when((step >= start) & (step < start + blocks))(run)
        start += blocks


def outer_group(core, lefts, products):
    chunk = 512
    width = lefts[0].shape[1]
    part = width // 4
    tokens = max(left.shape[0] for left in lefts)
    specs, start = [], 0
    for _, right in products:
        blocks = right.shape[1] // chunk
        specs.append(
            pl.BlockSpec(
                (right.shape[0], chunk),
                lambda step, place, start=start, blocks=blocks: (
                    0,
                    jnp.clip(step - start, 0, blocks - 1),
                ),
            )
        )
        start += blocks
    out_spec = pl.BlockSpec((2, part, chunk), lambda step, place: (0, 0, step))
    shape = jax.ShapeDtypeStruct((2, part, start * chunk), jnp.bfloat16)
    kinds = [(side, right.shape[1] // chunk) for side, right in products]
    return pl.pallas_call(
        functools.partial(outer_group_kernel, kinds, len(lefts)),
        grid_spec=pltpu.PrefetchScalarGridSpec(
            num_scalar_prefetch=1,
            grid=(start,),
            in_specs=[pl.BlockSpec(left.shape, lambda step, place: (0, 0)) for left in lefts]
            + specs,
            out_specs=[out_spec, out_spec],
            scratch_shapes=[pltpu.VMEM((width, tokens), jnp.bfloat16)],
        ),
        out_shape=[shape, shape],
        compiler_params=pltpu.CompilerParams(vmem_limit_bytes=vmem_bytes),
        cost_estimate=light,
    )(
        jnp.stack([core, 1 - core]).astype(jnp.int32),
        *lefts,
        *[right for _, right in products],
    )


def halve_kernel(split, place_ref, kept_a, came_a, kept_b, came_b, kept_ref, *sent_refs):
    add = lambda kept, came: (kept[0].astype(jnp.float32) + came[0].astype(jnp.float32)).astype(
        jnp.bfloat16
    )
    kept_ref[0] = add(kept_a, came_a)
    if not split:
        sent_refs[0][0] = add(kept_b, came_b)
        return

    for index, sent_ref in enumerate(sent_refs):

        def store(sent_ref=sent_ref):
            sent_ref[0] = add(kept_b, came_b)

        pl.when(pl.program_id(0) == index)(store)


def halve(keep_at, send_at, kept, came, split=False):
    blocks, rows, width = kept.shape
    count = len(keep_at)
    place = jnp.stack(list(keep_at) + list(send_at)).astype(jnp.int32)
    tiles = 2 if rows * width >= 256 * 1024 else 1
    wide = width // tiles
    spec = lambda first: pl.BlockSpec(
        (1, rows, wide), lambda j, i, place: (place[first + j], 0, i)
    )
    out_spec = pl.BlockSpec((1, rows, wide), lambda j, i, place: (j, 0, i))
    one_spec = lambda at: pl.BlockSpec(
        (1, rows, wide),
        lambda j, i, place: (0, 0, jnp.where(j == at, i, jnp.where(j > at, tiles - 1, 0))),
    )
    shape = jax.ShapeDtypeStruct((count, rows, width), jnp.bfloat16)
    one = jax.ShapeDtypeStruct((1, rows, width), jnp.bfloat16)
    out = pl.pallas_call(
        functools.partial(halve_kernel, split),
        grid_spec=pltpu.PrefetchScalarGridSpec(
            num_scalar_prefetch=1,
            grid=(count, tiles),
            in_specs=[spec(0), spec(0), spec(count), spec(count)],
            out_specs=[out_spec]
            + ([one_spec(at) for at in range(count)] if split else [out_spec]),
        ),
        out_shape=[shape] + ([one] * count if split else [shape]),
        compiler_params=pltpu.CompilerParams(vmem_limit_bytes=vmem_bytes),
        cost_estimate=light,
    )(place, kept, came, kept, came)
    return out[0], out[1:]


def halve_late_kernel(place_ref, *refs):
    step = pl.program_id(0)
    for which in range(2):
        own_ref, early_ref, late_ref = refs[3 * which : 3 * which + 3]
        out_ref = refs[6 + which]
        for block, came_ref in enumerate((early_ref, late_ref)):

            def store(out_ref=out_ref, own_ref=own_ref, came_ref=came_ref):
                total = own_ref[0].astype(jnp.float32) + came_ref[0].astype(jnp.float32)
                out_ref[0] = total.astype(jnp.bfloat16)

            pl.when(place_ref[2 * which + step] // 2 == block)(store)


def halve_late(keep_at, send_at, kept, early, late):
    rows, width = kept.shape[1:]
    at = list(keep_at) + list(send_at)
    place = jnp.stack(at + [block % 2 for block in at]).astype(jnp.int32)
    spec = lambda first: pl.BlockSpec((1, rows, width), lambda j, place: (place[first + j], 0, 0))
    out_spec = pl.BlockSpec((1, rows, width), lambda j, place: (j, 0, 0))
    shape = jax.ShapeDtypeStruct((2, rows, width), jnp.bfloat16)
    return pl.pallas_call(
        halve_late_kernel,
        grid_spec=pltpu.PrefetchScalarGridSpec(
            num_scalar_prefetch=1,
            grid=(2,),
            in_specs=[spec(0), spec(4), spec(4), spec(2), spec(6), spec(6)],
            out_specs=[out_spec, out_spec],
        ),
        out_shape=[shape, shape],
        compiler_params=pltpu.CompilerParams(vmem_limit_bytes=vmem_bytes),
        cost_estimate=light,
    )(place, kept, early, late, kept, early, late)


def combine_kernel(place_ref, *refs):
    kept_ref, sent_refs = refs[8], refs[9:]

    def put(sources, out_ref):
        total = lambda kept, came: (
            kept[0].astype(jnp.float32) + came[0].astype(jnp.float32)
        ).astype(jnp.bfloat16)
        outer, inner = total(*sources[:2]), total(*sources[2:])
        tall, low = outer.shape[0] // 4, inner.shape[0] // 4
        wide = outer.shape[1]
        both = tall + inner.shape[1] // wide * low
        for piece in range(4):
            out_ref[0, pl.ds(piece * both, tall), :] = outer[piece * tall : (piece + 1) * tall]
            for block in range(inner.shape[1] // wide):
                out_ref[0, pl.ds(piece * both + tall + block * low, low), :] = inner[
                    piece * low : (piece + 1) * low, block * wide : (block + 1) * wide
                ]

    put(refs[:4], kept_ref)
    for index, sent_ref in enumerate(sent_refs):
        pl.when(pl.program_id(0) == index)(functools.partial(put, refs[4:8], sent_ref))


def combine(keep_at, send_at, outer, inner):
    place = jnp.stack(list(keep_at) + list(send_at)).astype(jnp.int32)
    spec = lambda values, first: pl.BlockSpec(
        (1,) + values.shape[1:], lambda j, place: (place[first + j], 0, 0)
    )
    arrays = list(outer) + list(inner)
    width = outer[0].shape[2]
    rows = outer[0].shape[1] + inner[0].shape[1] * inner[0].shape[2] // width
    one = jax.ShapeDtypeStruct((1, rows, width), jnp.bfloat16)
    one_spec = pl.BlockSpec((1, rows, width), lambda j, place: (0, 0, 0))
    return pl.pallas_call(
        combine_kernel,
        grid_spec=pltpu.PrefetchScalarGridSpec(
            num_scalar_prefetch=1,
            grid=(2,),
            in_specs=[spec(values, first) for first in (0, 2) for values in arrays],
            out_specs=[
                pl.BlockSpec((1, rows, width), lambda j, place: (j, 0, 0)),
                one_spec,
                one_spec,
            ],
        ),
        out_shape=[jax.ShapeDtypeStruct((2, rows, width), jnp.bfloat16), one, one],
        compiler_params=pltpu.CompilerParams(vmem_limit_bytes=vmem_bytes),
        cost_estimate=light,
    )(place, *arrays, *arrays)


def unpack_kernel(tall, inner_blocks, place_ref, own_ref, other_ref, *out_refs):
    def put(source):
        if not inner_blocks:
            for index, out_ref in enumerate(out_refs):
                wide = out_ref.shape[1]
                out_ref[...] = source[:, index * wide : (index + 1) * wide].astype(jnp.float32)
            return
        outer_ref, inner_ref = out_refs
        low, wide = inner_ref.shape[0], source.shape[1]
        outer_ref[...] = source[pl.ds(0, tall), :].astype(jnp.float32)
        for block in range(inner_blocks):
            rows = source[pl.ds(tall + block * low, low), :]
            inner_ref[:, block * wide : (block + 1) * wide] = rows.astype(jnp.float32)

    pl.when(pl.program_id(0) == 0)(lambda: put(own_ref))
    pl.when(pl.program_id(0) == 1)(lambda: put(other_ref))


def unpack(core, own, other, count=0, tall=0, inner_blocks=0):
    rows, width = own.shape
    if inner_blocks:
        steps, block = 8, rows // 8
        low = (block - tall) // inner_blocks
        shapes = [(16 * tall, width), (16 * low, inner_blocks * width)]
        blocks = [(tall, width), (low, inner_blocks * width)]
    else:
        steps, block = 2, rows // 2
        shapes = [(2 * rows, width // count)] * count
        blocks = [(block, width // count)] * count
    return pl.pallas_call(
        functools.partial(unpack_kernel, tall, inner_blocks),
        grid_spec=pltpu.PrefetchScalarGridSpec(
            num_scalar_prefetch=1,
            grid=(2, steps),
            in_specs=[
                pl.BlockSpec(
                    (block, width),
                    lambda side, i, place: (jnp.where(side == 0, i, steps - 1), 0),
                ),
                pl.BlockSpec((block, width), lambda side, i, place: (jnp.where(side == 1, i, 0), 0)),
            ],
            out_specs=[
                pl.BlockSpec(shape, lambda side, i, place: (place[side] * steps + i, 0))
                for shape in blocks
            ],
        ),
        out_shape=[jax.ShapeDtypeStruct(shape, jnp.float32) for shape in shapes],
        compiler_params=pltpu.CompilerParams(vmem_limit_bytes=vmem_bytes),
        cost_estimate=light,
    )(jnp.stack([core, 1 - core]).astype(jnp.int32), own, other)


def norm_unit(values):
    center = values - jnp.mean(values, axis=-1, keepdims=True)
    inverse = lax.rsqrt(jnp.mean(center * center, axis=-1, keepdims=True) + norm_epsilon)
    return center * inverse, inverse


def layer_norm_back(values, norm_gain, grad):
    unit, inverse = norm_unit(values)
    scaled = grad * norm_gain
    back = scaled - jnp.mean(scaled, axis=-1, keepdims=True)
    back = back - unit * jnp.mean(scaled * unit, axis=-1, keepdims=True)
    return back * inverse


def dot_back(gradient, weight):
    return dot_nt(gradient, weight)


def column_sum(values):
    return jnp.sum(values.astype(jnp.float32), axis=0)


def swap(values, axis_name):
    return lax.ppermute(values, axis_name, [(0, 1), (1, 0)])


flips = {"x": 4, "y": 1, "z": 8}
square = ("zlo", "x", "core", "seq")


def exchange(values, axes):
    flip = [flips[axis] for axis in axes]
    return lax.ppermute(values, square, [(i, i ^ flip[i // 2 % 2]) for i in range(16)])


def square_bits(turned):
    core, x, zlo = lax.axis_index("core"), lax.axis_index("x"), lax.axis_index("zlo")
    first = 1 - core if turned else core
    return core, jnp.where(first == 1, x, zlo), jnp.where(first == 1, zlo, x)


def after(values, *others):
    return lax.optimization_barrier((values,) + others)[0]


def first_piece(shards):
    piece_rows = shards[0].shape[0] // 8
    core, high, low = square_bits(False)
    place = (core * 2 + high) * 2 + low
    piece = [
        lax.dynamic_slice_in_dim(shard, place * piece_rows, piece_rows, axis=0) for shard in shards
    ]
    return swap(piece[0] if len(piece) == 1 else jnp.concatenate(piece, axis=1), "seq")


class Pieces:
    def __init__(self, piece):
        core, high, low = square_bits(False)
        self.own = piece
        place = lambda side, one, two: (side * 2 + one) * 2 + two
        self.places = [
            place(core, high, low),
            place(core, high, 1 - low),
            place(core, 1 - high, low),
            place(core, 1 - high, 1 - low),
            place(1 - core, low, high),
            place(1 - core, low, 1 - high),
            place(1 - core, 1 - low, high),
            place(1 - core, 1 - low, 1 - high),
        ]

    def first(self, *others):
        self.own = after(self.own, *others)
        self.low = exchange(self.own, "xz")
        self.high = exchange(self.own, "zx")
        self.core = swap(self.own, "core")
        return self.low, self.high, self.core

    def second(self, *others):
        low, high = after(self.low, *others), after(self.high, *others)
        self.both = exchange(low, "zx")
        self.core_low, self.core_high = swap(low, "core"), swap(high, "core")
        return self.both, self.core_low, self.core_high

    def third(self, *others):
        self.core_both = swap(after(self.both, *others), "core")
        return [self.core_both]

    def parts(self, *others):
        return [
            after(self.own, *others),
            self.low,
            self.high,
            self.both,
            self.core,
            self.core_low,
            self.core_high,
            self.core_both,
        ]


class Total:
    def __init__(self, split, steps, turned, halves, inner=None):
        kept, sent = split
        self.inner = None
        if inner is not None:
            self.inner = (inner[0], swap(self.blocks(inner[1], 4), "core"))
            self.tall, self.inner_blocks = kept.shape[1] // 8, inner[0].shape[2] // kept.shape[2]
        self.core, self.first, self.second = square_bits(turned)
        self.seq, self.zhi = lax.axis_index("seq"), lax.axis_index("zhi")
        self.steps, self.halves = steps, halves
        self.along = ("x", "z") if turned else ("z", "x")
        self.came = swap(self.blocks(sent, 4), "core")
        self.kept = self.blocks(kept, 4)
        self.stage = 0

    def blocks(self, values, count):
        return values.reshape(count, -1, values.shape[-1])

    def by_core(self, choose):
        both = [choose([axes[core] for axes in self.steps]) for core in range(2)]
        return [jnp.where(self.core == 0, *pair) for pair in zip(*both)]

    def bits(self):
        seq, first, second = self.seq, self.first, self.second

        def one(axes):
            if axes[0] == "y":
                return [seq * 2, seq * 2 + 1, 2 - seq * 2, 3 - seq * 2]
            return [first, 2 + first, 1 - first, 3 - first]

        def two(axes):
            if axes[0] != "y" and axes[1] != "y":
                return [second, 2 + second, 1 - second, 3 - second]
            bit = first if axes[0] == "y" else seq
            return [bit * 2, bit * 2 + 1, 2 - bit * 2, 3 - bit * 2]

        def three(axes):
            bit = seq if axes[2] == "y" else second
            return [bit, 1 - bit]

        def four(axes):
            return [self.zhi, 1 - self.zhi]

        at = self.by_core((one, two, three, four)[self.stage])
        return at[: len(at) // 2], at[len(at) // 2 :]

    def step(self, *others):
        self.kept = after(self.kept, *others)
        keep, send = self.bits()
        self.kept = self.blocks(self.kept, 2 * len(keep))
        if self.stage == 0 and self.inner is not None:
            kept, came = (self.blocks(values, 4) for values in self.inner)
            self.kept, *sent = combine(keep, send, (self.kept, self.came), (kept, came))
            self.came, self.rest = exchange(sent[0], self.steps[0]), sent[1]
            self.stage += 1
            return sent[0]
        if self.stage == 1 and self.halves:
            early, late = (self.blocks(came, 2) for came in self.came)
            self.kept, sent = halve_late(keep, send, self.kept, early, late)
        else:
            split = self.stage == 0 and self.halves
            came = self.blocks(self.came, 2 * len(keep))
            self.kept, sent = halve(keep, send, self.kept, came, split)
            if split:
                self.came, self.rest = exchange(sent[0], self.steps[0]), sent[1]
                self.stage += 1
                return sent[0]
            sent = sent[0]
        if self.stage < 3:
            self.came = exchange(sent, self.steps[self.stage])
        else:
            self.came = swap(sent, "zhi")
        self.stage += 1
        return sent

    def step_rest(self, *others):
        sent = after(self.rest, self.came, *others)
        self.came = (self.came, exchange(sent, self.steps[0]))
        return sent

    def gather(self, *others):
        if self.stage > 4:
            self.part = after(self.part, *others)
        if self.stage == 4:
            piece = self.kept[0].astype(jnp.float32) + self.came[0].astype(jnp.float32)
            self.part = piece.astype(jnp.bfloat16)
            self.came = swap(self.part, "zhi")
        elif self.stage == 5:
            self.part = merge(self.zhi, self.part, self.came)
            self.came = exchange(self.part, self.along[::-1])
        elif self.stage == 6:
            self.part = merge(self.second, self.part, self.came)
            self.came = exchange(self.part, self.along)
        else:
            self.part = merge(self.first, self.part, self.came)
            self.came = swap(self.part, "core")
        self.stage += 1
        return self.part

    def advance(self, *others):
        if self.stage < 4:
            return [self.step(*others)]
        return [self.gather(*others)] if self.stage < 8 else []

    def result(self, count, *others):
        part = after(self.part, *others)
        if self.inner is None:
            return unpack(self.core, part, self.came, count)
        return unpack(self.core, part, self.came, 2, self.tall, self.inner_blocks)


def sum_plain(terms):
    terms = lax.psum_scatter(terms.astype(jnp.bfloat16), "seq", scatter_dimension=0, tiled=True)
    return lax.psum(terms, page_axes)


page_axes = ("zhi", "zlo", "x", "core")


class VectorTotal:
    def __init__(self, values):
        self.values = values
        self.axes = [axis for axis in page_axes + ("seq",) if lax.axis_size(axis) == 2]
        rest = tuple(axis for axis in page_axes + ("seq",) if lax.axis_size(axis) != 2)
        if rest:
            self.values = lax.psum(self.values, rest)
        self.came = swap(self.values, self.axes.pop(0))

    def advance(self, *others):
        if self.came is None:
            return []
        self.values, self.came = after(self.values, *others) + self.came, None
        if self.axes:
            self.came = swap(self.values, self.axes.pop(0))
        return [self.values]

    def result(self):
        while self.came is not None:
            self.advance()
        return self.values


def on_device(
    tokens,
    patches,
    lengths,
    blank_mask,
    cotangent,
    first_gain,
    first_shift,
    self_query,
    self_query_bias,
    self_key,
    self_value,
    self_value_bias,
    self_output,
    self_output_bias,
    second_gain,
    second_shift,
    cross_query,
    cross_query_bias,
    cross_key,
    cross_value,
    cross_value_bias,
    cross_output,
    cross_output_bias,
    third_gain,
    third_shift,
    ffn_inner,
    ffn_inner_bias,
    ffn_outer,
    ffn_outer_bias,
):
    seq_count = lax.axis_size("seq")
    seq_index = lax.axis_index("seq")
    vectors = (
        first_gain,
        first_shift,
        self_query_bias,
        self_value_bias,
        self_output_bias,
        second_gain,
        second_shift,
        cross_query_bias,
        cross_value_bias,
        cross_output_bias,
        third_gain,
        third_shift,
        ffn_inner_bias,
        ffn_outer_bias,
    )
    two = seq_count == 2 and lax.axis_size("zhi") == 2
    joined = jnp.concatenate(vectors).reshape(-1, 128)
    if two:
        joined_other = swap(joined, "seq")
        gathered = jnp.where(
            seq_index == 0,
            jnp.stack([joined, joined_other]),
            jnp.stack([joined_other, joined]),
        )
    else:
        gathered = lax.all_gather(joined, "seq", axis=0, tiled=False)
    gathered = gathered.reshape(seq_count, -1)
    whole_vectors, start = [], 0
    for vector in vectors:
        part = gathered[:, start : start + vector.shape[0]].reshape(-1)
        whole_vectors.append(part.astype(jnp.float32))
        start += vector.shape[0]
    (
        gain_one,
        shift_one,
        bias_self_query,
        bias_self_value,
        bias_self_output,
        gain_two,
        shift_two,
        bias_cross_query,
        bias_cross_value,
        bias_cross_output,
        gain_three,
        shift_three,
        bias_inner,
        bias_outer,
    ) = whole_vectors
    tokens, patches, cotangent = tokens[0], patches[0], cotangent[0]
    tok_rows, width = tokens.shape
    patch_rows = patches.shape[0]
    query_scale = 1.0 / math.sqrt(HEAD)

    core = lax.axis_index("core")
    self_shards = [self_query, self_key, self_value, self_output]
    cross_shards = [cross_key, cross_value, cross_query, cross_output]
    if two:
        pieces = Pieces(first_piece(self_shards))
        pieces.first(joined_other)
        tokens_other = lax.ppermute(after(tokens, pieces.own), "seq", [(0, 1)])
        pieces.second()
        cross_pieces = Pieces(first_piece([after(cross_key, pieces.low)] + cross_shards[1:]))
        pieces.third()
        whole_self = assemble(
            seq_index, pieces.places, self_shards, pieces.parts(tokens_other)
        )
        tokens_all = jnp.concatenate([tokens, after(tokens_other, whole_self)])
    else:
        gather = lambda shard: lax.all_gather(shard, "seq", axis=0, tiled=True)
        whole_self = gather(jnp.concatenate(self_shards, axis=1))
        whole_cross = gather(jnp.concatenate(cross_shards, axis=1))
        whole_ffn_inner, whole_ffn_outer = gather(ffn_inner), gather(ffn_outer)
        tokens_all, patches_all = gather(tokens), gather(patches)

    first_place = seq_index * tok_rows
    key_start = first_place if two else 0
    info = jnp.stack([first_place, lengths[0], key_start, seq_index]).astype(jnp.int32)
    self_plan = Plan(
        ("limit", "earlier") if two else ("limit",),
        tok_rows if two else tok_rows * seq_count,
        tok_rows,
        256,
        two,
    )
    cross_plan = Plan(("bias",), patch_rows * seq_count, tok_rows, 256, False)
    blank_bias = jnp.where(blank_mask[0] == 0, 0.0, masked_score).astype(jnp.float32)
    if two:
        halves = blank_bias.reshape(2, patch_rows)
        blank_bias = jnp.where(seq_index == 0, halves, halves[::-1]).reshape(-1)
    blank_bias = blank_bias[:, None]
    no_bias = jnp.zeros((self_plan.all_rows, 1), jnp.float32)

    zeros = jnp.zeros_like(bias_self_value)
    token_values = tokens.astype(jnp.float32)
    normed_all = layer_norm(tokens_all.astype(jnp.float32), gain_one, shift_one).astype(
        jnp.bfloat16
    )
    if two:
        normed_one = normed_all[:tok_rows]
    else:
        normed_one = layer_norm(token_values, gain_one, shift_one).astype(jnp.bfloat16)
    queries_self = (
        (dot_nn(normed_one, whole_self[:, :width]) + bias_self_query) * query_scale
    ).astype(jnp.bfloat16)
    self_bias = jnp.concatenate([zeros, bias_self_value])
    self_pairs = (dot_nn(normed_all, whole_self[:, width : 3 * width]) + self_bias).astype(
        jnp.bfloat16
    )
    attend_self = functools.partial(attend, self_plan, info)
    if two:
        sent = cross_pieces.first(queries_self)
        patches_other = swap(after(patches, cross_pieces.own), "seq")
        mixed_self, log_self = attend_self(
            after(queries_self, *sent), self_pairs, no_bias, 0, 1
        )
        mixed_self = after(mixed_self, patches_other, *cross_pieces.second())
        inner_pieces = Pieces(first_piece([after(ffn_inner, patches_other)]))
    else:
        mixed_self, log_self = attend_self(queries_self, self_pairs, no_bias, 0, 1)
    hidden_one = token_values + dot_nn(mixed_self, whole_self[:, 3 * width :]) + bias_self_output
    normed_two = layer_norm(hidden_one, gain_two, shift_two).astype(jnp.bfloat16)
    if two:
        cross_pieces.third()
        whole_cross = assemble(
            seq_index, cross_pieces.places, cross_shards, cross_pieces.parts(normed_two)
        )
        patches_all = jnp.concatenate([patches, patches_other])
        patches_all = after(patches_all, whole_cross, inner_pieces.own)
        outer_pieces = Pieces(first_piece([after(ffn_outer, inner_pieces.own)]))
    patch_bias = jnp.concatenate([zeros, bias_cross_value])
    patch_pairs = (dot_nn(patches_all, whole_cross[:, : 2 * width]) + patch_bias).astype(
        jnp.bfloat16
    )
    queries_cross = (
        (dot_nn(normed_two, whole_cross[:, 2 * width : 3 * width]) + bias_cross_query) * query_scale
    ).astype(jnp.bfloat16)
    attend_cross = functools.partial(attend, cross_plan, info)
    if two:
        keys = (patch_pairs, blank_bias)
        sent = inner_pieces.first(queries_cross) + (outer_pieces.own,)
        done = attend_cross(after(queries_cross, *sent), *keys, 0, 2)
        sent = inner_pieces.second() + outer_pieces.first()
        sent = [after(values, done[0]) for values in sent]
        inner_pieces.both, inner_pieces.core_low, inner_pieces.core_high = sent[:3]
        outer_pieces.low, outer_pieces.high, outer_pieces.core = sent[3:]
        inner_pieces.third()
        outer_pieces.second()
        done = attend_cross(after(queries_cross, *sent), *keys, 1, 2, done)
        late = [after(values, done[0]) for values in (outer_pieces.both, inner_pieces.core_both)]
        outer_pieces.both, inner_pieces.core_both = late
        inner_other = join(inner_pieces.places, inner_pieces.parts(done[0]))
        mixed_cross, log_cross = done
        outer_pieces.third()
        mixed_cross = after(mixed_cross, inner_other)
    else:
        mixed_cross, log_cross = attend_cross(queries_cross, patch_pairs, blank_bias, 0, 1)
    hidden_two = hidden_one + dot_nn(mixed_cross, whole_cross[:, 3 * width :]) + bias_cross_output
    normed_three = layer_norm(hidden_two, gain_three, shift_three).astype(jnp.bfloat16)
    if two:
        outer_other = join(outer_pieces.places, outer_pieces.parts(normed_three))
        outputs, grad_normed_three, column_inner, split_outer, split_inner = ffn_both_ways(
            seq_index,
            core,
            normed_three,
            hidden_two,
            cotangent,
            ffn_inner,
            inner_other,
            ffn_outer,
            outer_other,
            bias_inner,
            bias_outer,
        )
        total_ffn = Total(split_outer, ("xy", "yz", "zx"), True, True, split_inner)
    else:
        inner_sum = dot_nn(normed_three, whole_ffn_inner) + bias_inner
        active = jax.nn.gelu(inner_sum, approximate=False).astype(jnp.bfloat16)
        outputs = (hidden_two + dot_nn(active, whole_ffn_outer) + bias_outer).astype(jnp.bfloat16)
        grad_active = dot_back(cotangent, whole_ffn_outer)
        gelu_pull = jax.vjp(lambda u: jax.nn.gelu(u, approximate=False), inner_sum)[1]
        grad_inner = gelu_pull(grad_active)[0].astype(jnp.bfloat16)
        column_inner = column_sum(grad_inner)
        grad_normed_three = dot_back(grad_inner, whole_ffn_inner)
    back_two = layer_norm_back(hidden_two, gain_three, grad_normed_three)
    grad_hidden_two = cotangent.astype(jnp.float32) + back_two
    branch_cross = grad_hidden_two.astype(jnp.bfloat16)
    grad_mixed_cross = dot_back(branch_cross, whole_cross[:, 3 * width :]).astype(jnp.bfloat16)
    back_cross = functools.partial(
        attend_back, cross_plan, info, queries_cross, mixed_cross
    )
    cross_rest = (log_cross, patch_pairs, blank_bias)
    if two:
        sent = total_ffn.step(grad_mixed_cross)
        cross_back = back_cross(after(grad_mixed_cross, sent), *cross_rest, 0, 1)
    else:
        cross_back = back_cross(grad_mixed_cross, *cross_rest, 0, 1)
    scaled_cross, grad_patch_keys, grad_patch_values = cross_back
    cross_products = [
        (normed_two, scaled_cross),
        (patches_all, grad_patch_keys),
        (patches_all, grad_patch_values),
        (mixed_cross, branch_cross),
    ]
    if two:
        scaled_cross = after(scaled_cross, total_ffn.step_rest(scaled_cross))
    grad_normed_two = dot_back(scaled_cross, whole_cross[:, 2 * width : 3 * width])
    back_one = layer_norm_back(hidden_one, gain_two, grad_normed_two)
    grad_hidden_one = grad_hidden_two + back_one
    branch_self = grad_hidden_one.astype(jnp.bfloat16)
    grad_mixed_self = dot_back(branch_self, whole_self[:, 3 * width :]).astype(jnp.bfloat16)
    back_self = functools.partial(attend_back, self_plan, info, queries_self, mixed_self)
    self_rest = (log_self, self_pairs, no_bias)
    if two:
        products = [
            (0, scaled_cross),
            (1, grad_patch_keys),
            (1, grad_patch_values),
            (2, branch_cross),
            (3, branch_self),
        ]
        lefts = [after(normed_two, grad_mixed_self), patches_all, mixed_cross, mixed_self]
        kept, sent = outer_group(core, lefts, products)
        late = total_ffn.step(kept)
        total_mid = Total((kept, after(sent, late)), ("zx", "yz", "xy"), False, True)
        sent = total_mid.step(late)
        self_back = back_self(after(grad_mixed_self, sent), *self_rest, 0, 1)
    else:
        self_back = back_self(grad_mixed_self, *self_rest, 0, 1)
    scaled_self, grad_keys, grad_values = self_back
    self_products = [
        (normed_one, scaled_self),
        (normed_all, grad_keys),
        (normed_all, grad_values),
        (mixed_self, branch_self),
    ]
    if two:
        late = (total_ffn.step(scaled_self), total_mid.step_rest(scaled_self))
        products = [(0, scaled_self), (1, grad_keys), (1, grad_values)]
        lefts = [after(normed_one, *late), normed_all]
        kept, sent = outer_group(core, lefts, products)
        late = (total_ffn.step(kept), total_mid.step(kept))
        total_last = Total((kept, after(sent, *late)), ("yz", "xy", "zx"), True, False)
        grad_keys, scaled_self = (after(values, *late) for values in (grad_keys, scaled_self))
    normed_terms = dot_back(grad_keys, whole_self[:, width : 2 * width]) + dot_back(
        grad_values, whole_self[:, 2 * width : 3 * width]
    )
    if two:
        sent = total_last.advance(normed_terms)
        for total in (total_mid, total_ffn):
            sent = sent + total.advance(*sent)
        grad_patch_keys = after(grad_patch_keys, *sent)
    patch_terms = dot_back(grad_patch_keys, whole_cross[:, :width]) + dot_back(
        grad_patch_values, whole_cross[:, width : 2 * width]
    )
    if two:
        normed_sent = normed_terms[tok_rows:].astype(jnp.bfloat16)
        normed_came = lax.ppermute(normed_sent, "seq", [(1, 0)])
        grad_normed = normed_terms[:tok_rows] + normed_came.astype(jnp.float32)
        patch_sent = patch_terms[patch_rows:].astype(jnp.bfloat16)
        grad_patches = patch_terms[:patch_rows] + swap(patch_sent, "seq").astype(jnp.float32)
    else:
        grad_patches, grad_normed = (
            lax.psum_scatter(
                terms.astype(jnp.bfloat16), "seq", scatter_dimension=0, tiled=True
            ).astype(jnp.float32)
            for terms in (patch_terms, normed_terms)
        )
    grad_normed = grad_normed + dot_back(scaled_self, whole_self[:, :width])
    grad_tokens = grad_hidden_one + layer_norm_back(token_values, gain_one, grad_normed)
    norm_pairs = (
        (token_values, grad_normed),
        (hidden_one, grad_normed_two),
        (hidden_two, grad_normed_three),
    )
    plain = (
        scaled_self,
        grad_values,
        branch_self,
        scaled_cross,
        grad_patch_values,
        branch_cross,
        cotangent,
    )
    if two:
        late = total_last.advance(patch_terms)
        for total in (total_mid, total_ffn):
            late = late + total.advance(*late)
        norm_pairs = ((after(token_values, *late), grad_normed),) + norm_pairs[1:]
    sums = row_sums(norm_pairs, plain)
    vector_sums = jnp.concatenate([sums, column_inner.reshape(-1, width)])
    if two:
        totals = (total_mid, total_ffn, total_last)
        late = [vector_sums]
        while any(total.stage < 8 for total in totals):
            ahead = total_last.advance(*late)
            late = ahead
            for total in totals[:-1]:
                late = late + total.advance(*late)
        vector_total = VectorTotal(after(vector_sums, *late))
        grad_outer, grad_ffn_in = total_ffn.result(2, *late)
        late = vector_total.advance(grad_outer)
        *wide_cross, wide_output = total_mid.result(5, *late)
        late = vector_total.advance(wide_output)
        wide_self = [*total_last.result(3, *late), wide_output]
    else:
        grad_outer = sum_plain(dot_tn(active, cotangent)).astype(jnp.float32)
        grad_ffn_in = sum_plain(dot_tn(normed_three, grad_inner)).astype(jnp.float32)
        wide_cross = [
            sum_plain(dot_tn(*product)).astype(jnp.float32) for product in cross_products
        ]
        wide_self = [sum_plain(dot_tn(*product)).astype(jnp.float32) for product in self_products]
        vector_total = VectorTotal(vector_sums)
    sums = vector_total.result()
    small_width = width // seq_count
    own_sums = lax.dynamic_slice_in_dim(sums[:-4], seq_index * small_width, small_width, axis=1)
    inner_rows = sums[-(column_inner.shape[0] // width) :].reshape(-1)
    inner_width = column_inner.shape[0] // seq_count
    own_inner = lax.dynamic_slice_in_dim(inner_rows, seq_index * inner_width, inner_width, axis=0)
    order = (0, 1, 6, 7, 8, 2, 3, 9, 10, 11, 4, 5, None, 12)
    small = [own_inner if at is None else own_sums[at] for at in order]
    totals = (
        small[0],
        small[1],
        wide_self[0],
        small[2],
        wide_self[1],
        wide_self[2],
        small[3],
        wide_self[3],
        small[4],
        small[5],
        small[6],
        wide_cross[0],
        small[7],
        wide_cross[1],
        wide_cross[2],
        small[8],
        wide_cross[3],
        small[9],
        small[10],
        small[11],
        grad_ffn_in,
        small[12],
        grad_outer,
        small[13],
    )
    return (outputs[None], grad_tokens[None], grad_patches[None]) + totals


def solution(mesh):
    page_count, seq_count = mesh.devices.shape
    mesh = Mesh(
        mesh.devices.reshape(page_count // 8, 2, 2, 2, seq_count),
        ("zhi", "zlo", "x", "core", "seq"),
    )
    page = ("zhi", "zlo", "x", "core")
    pages = P(page, "seq", None)
    rows, vector = P("seq", None), P("seq")
    layer = (
        (vector, vector)
        + (rows, vector, rows, rows, vector, rows, vector)
        + (vector, vector)
        + (rows, vector, rows, rows, vector, rows, vector)
        + (vector, vector)
        + (rows, vector, rows, vector)
    )
    return jax.shard_map(
        on_device,
        mesh=mesh,
        in_specs=(pages, pages, P(page), P(page, None), pages) + layer,
        out_specs=(pages, pages, pages) + layer,
        check_vma=False,
    )
```
